32 devices in a mesh: space: 8 (over y, x, core), filt: 4 (over z).
Axes of the slice: x: 2, y: 2, z: 4, core: 2. Of those that a mesh axis runs over, the one named last changes fastest.
Arguments:
- image: bfloat16 [96, 32, 1024], P(None, 'space', 'filt'), may hold values from -6 to 6
- cotangent: bfloat16 [96, 32, 1024], P(None, 'space', 'filt'), may hold values from -6 to 6
- kernel: float32 [96, 7, 7], replicated, may hold values from -0.875 to 0.875
- dw_bias: float32 [96], replicated, may hold values from -0.5 to 0.5
- layer_norm_gain: float32 [96], replicated, may hold values from 0.5 to 1.5
- layer_norm_bias: float32 [96], replicated, may hold values from -3 to 3
- w_expand: bfloat16 [384, 96], replicated, may hold values from -0.625 to 0.625
- b_expand: bfloat16 [384], replicated, may hold values from -3 to 3
- w_reduce: bfloat16 [384, 96], replicated, may hold values from -0.3125 to 0.3125
- b_reduce: float32 [96], replicated, may hold values from -3 to 3
- layer_scale: float32 [96], replicated, may hold values from 0.2 to 1
Outputs:
- output: bfloat16 [96, 32, 1024], P(None, 'space', 'filt')
- image_grad: bfloat16 [96, 32, 1024], P(None, 'space', 'filt')
- kernel_grad: float32 [96, 7, 7], replicated
- dw_bias_grad: float32 [96], replicated
- gain_grad: float32 [96], replicated
- ln_bias_grad: float32 [96], replicated
- expand_grad: float32 [384, 96], P('filt')
- expand_bias_grad: float32 [384], P('filt')
- reduce_grad: float32 [384, 96], P('filt')
- reduce_bias_grad: float32 [96], replicated
- scale_grad: float32 [96], replicated
The draws below stay inside these ranges and needn't reach their ends.
All inputs are finite; a program needn't handle non-finite values.
Results may differ from the reference program's by a relative error of at most 0.011.
Values may be sent and summed in bfloat16 or wider, within the bound.
No kernel may reach another device: no remote copies, remote signals or barrier semaphores. Data moves between devices by JAX's collectives and lax.ppermute only.
A program may use at most 64 MiB of HBM per device.

```python
import math
import jax
import jax.numpy as jnp
from jax import lax

C = 96
HID = 384
KSIZE = 7
HEIGHT = 32
WIDTH = 1024
TOKENS = 32768


def block_scale(own_key, extent, split, smallest, top_value):
    def one(axis_at, parts):
        heights = jax.random.uniform(jax.random.fold_in(jax.random.fold_in(own_key, 6), axis_at), (parts,), jnp.float32, smallest / len(split), top_value / len(split))
        return jnp.repeat(jnp.exp(heights), extent[axis_at] // parts).reshape((-1,) + (1,) * (len(extent) - axis_at - 1))

    factor_of = one(*split[0])
    for cut in split[1:]:
        factor_of = factor_of * one(*cut)
    return factor_of


def centred(own_key, extent, deviation, most, pieces=(), kind=jnp.bfloat16):
    result = jax.random.normal(own_key, extent, jnp.float32) * deviation
    if len(pieces) > 0:
        result = block_scale(own_key, extent, pieces, -0.22, 0.18) * result
    return jnp.clip(result, min=-most, max=most).astype(kind)


def setup_inputs(seed: int = 0) -> dict:
    splits = jax.random.split(jax.random.key(seed), 12)
    image = centred(splits[0], (C, HEIGHT, WIDTH), 1.0, 6.0, ((1, 8), (2, 4)))
    cotangent = centred(splits[1], (C, HEIGHT, WIDTH), 1.0, 6.0, ((1, 8), (2, 4)))
    kernel = centred(splits[2], (C, KSIZE, KSIZE), (KSIZE * KSIZE) ** -0.5, 0.875, (), jnp.float32)
    dw_bias = jnp.clip(jax.random.uniform(splits[3], (C,), jnp.float32, -0.5, 0.5), -0.5, 0.5)
    layer_norm_gain = jnp.clip(jax.random.uniform(splits[4], (C,), jnp.float32, 0.5, 1.5), 0.5, 1.5)
    layer_norm_bias = centred(splits[5], (C,), 0.5, 3.0, (), jnp.float32)
    w_expand = centred(splits[6], (HID, C), C ** -0.5, 0.625)
    b_expand = centred(splits[7], (HID,), 0.5, 3.0)
    w_reduce = centred(splits[8], (HID, C), HID ** -0.5, 0.3125)
    b_reduce = centred(splits[9], (C,), 0.5, 3.0, (), jnp.float32)
    layer_scale = jnp.clip(jnp.exp(jax.random.uniform(splits[10], (C,), jnp.float32, math.log(0.2), math.log(1.0))), 0.2, 1.0)
    return {"image": image, "cotangent": cotangent, "kernel": kernel, "dw_bias": dw_bias, "layer_norm_gain": layer_norm_gain, "layer_norm_bias": layer_norm_bias, "w_expand": w_expand, "b_expand": b_expand, "w_reduce": w_reduce, "b_reduce": b_reduce, "layer_scale": layer_scale}


def depthwise(padded, kernel, row_count, col_count):
    total = jnp.zeros((padded.shape[0], row_count, col_count), jnp.float32)
    for shift_row in range(7):
        for shift_col in range(7):
            piece = padded[:, shift_row:shift_row + row_count, shift_col:shift_col + col_count].astype(jnp.float32)
            total = total + kernel[:, shift_row, shift_col][:, None, None] * piece
    return total

def conv_back(padded, kernel, row_count, col_count):
    total = jnp.zeros((padded.shape[0], row_count, col_count), jnp.float32)
    for shift_row in range(7):
        for shift_col in range(7):
            piece = padded[:, 6 - shift_row:6 - shift_row + row_count, 6 - shift_col:6 - shift_col + col_count].astype(jnp.float32)
            total = total + kernel[:, shift_row, shift_col][:, None, None] * piece
    return total

def kernel_terms(padded, convolution_gradient, row_count, col_count):
    lines = []
    for shift_row in range(7):
        entries = []
        for shift_col in range(7):
            piece = padded[:, shift_row:shift_row + row_count, shift_col:shift_col + col_count].astype(jnp.float32)
            entries.append(lax.optimization_barrier(jnp.sum(piece * convolution_gradient, axis=(1, 2))))
        lines.append(jnp.stack(entries, axis=1))
    return jnp.stack(lines, axis=1)

def gelu_exact(value):
    return value * (1.0 + jax.scipy.special.erf(value / math.sqrt(2.0))) * 0.5

def gelu_slope(value):
    return (1.0 + jax.scipy.special.erf(value / math.sqrt(2.0))) * 0.5 + value * jnp.exp(-0.5 * value * value) / math.sqrt(2.0 * math.pi)

def local_pass(padded, incoming, kernel, dw_bias, layer_norm_gain, layer_norm_bias, w_expand, b_expand, w_reduce, b_reduce, layer_scale):
    channels = incoming.shape[0]
    row_count = incoming.shape[1]
    col_count = incoming.shape[2]
    tok_count = row_count * col_count
    conv = depthwise(padded, kernel, row_count, col_count) + dw_bias[:, None, None]
    flat = conv.reshape(channels, tok_count)
    average = lax.optimization_barrier(jnp.mean(flat, axis=0, keepdims=True))
    mean_removed = flat - average
    inverse_deviation = lax.rsqrt(lax.optimization_barrier(jnp.mean(mean_removed * mean_removed, axis=0, keepdims=True)) + 1e-06)
    standardized_input = mean_removed * inverse_deviation
    normalized_input = (standardized_input * layer_norm_gain[:, None] + layer_norm_bias[:, None]).astype(jnp.bfloat16)
    hidden = jnp.dot(w_expand, normalized_input, preferred_element_type=jnp.float32) + b_expand.astype(jnp.float32)[:, None]
    active = gelu_exact(hidden).astype(jnp.bfloat16)
    branch = lax.dot_general(w_reduce, active, (((0,), (0,)), ((), ())), preferred_element_type=jnp.float32) + b_reduce[:, None]
    resid = padded[:, 3:3 + row_count, 3:3 + col_count].reshape(channels, tok_count).astype(jnp.float32)
    output = (resid + layer_scale[:, None] * branch).astype(jnp.bfloat16).reshape(channels, row_count, col_count)
    cot_flat = incoming.reshape(channels, tok_count).astype(jnp.float32)
    scaled = layer_scale[:, None] * cot_flat
    g_scale = lax.optimization_barrier(jnp.sum(cot_flat * branch, axis=1))
    g_rbias = lax.optimization_barrier(jnp.sum(scaled, axis=1))
    d_branch = scaled.astype(jnp.bfloat16)
    g_reduce = lax.dot_general(active, d_branch, (((1,), (1,)), ((), ())), preferred_element_type=jnp.float32)
    d_active = jnp.dot(w_reduce, d_branch, preferred_element_type=jnp.float32)
    d_hidden = (d_active * gelu_slope(hidden)).astype(jnp.bfloat16)
    g_ebias = lax.optimization_barrier(jnp.sum(d_hidden.astype(jnp.float32), axis=1))
    g_expand = lax.dot_general(d_hidden, normalized_input, (((1,), (1,)), ((), ())), preferred_element_type=jnp.float32)
    normalized_gradient = lax.dot_general(w_expand, d_hidden, (((0,), (0,)), ((), ())), preferred_element_type=jnp.float32)
    norm_gain_gradient = lax.optimization_barrier(jnp.sum(normalized_gradient * standardized_input, axis=1))
    g_lbias = lax.optimization_barrier(jnp.sum(normalized_gradient, axis=1))
    standardized_gradient = normalized_gradient * layer_norm_gain[:, None]
    convolution_gradient = inverse_deviation * (standardized_gradient - lax.optimization_barrier(jnp.mean(standardized_gradient, axis=0, keepdims=True)) - standardized_input * lax.optimization_barrier(jnp.mean(standardized_gradient * standardized_input, axis=0, keepdims=True)))
    convolution_gradient = convolution_gradient.astype(jnp.bfloat16).reshape(channels, row_count, col_count)
    g_dbias = lax.optimization_barrier(jnp.sum(convolution_gradient.astype(jnp.float32), axis=(1, 2)))
    return (output, convolution_gradient, (g_scale, g_rbias, g_reduce, g_ebias, g_expand, norm_gain_gradient, g_lbias, g_dbias))

def reference(image, cotangent, kernel, dw_bias, layer_norm_gain, layer_norm_bias, w_expand, b_expand, w_reduce, b_reduce, layer_scale):
    block = math.gcd(HEIGHT, 32)
    count = HEIGHT // block
    padded_image = jnp.pad(image, ((0, 0), (3, 3), (3, 3)))
    zeros_c = jnp.zeros((C,), jnp.float32)
    zeros_h = jnp.zeros((HID,), jnp.float32)
    zeros_w = jnp.zeros((HID, C), jnp.float32)
    init = (zeros_c, zeros_c, zeros_w, zeros_h, zeros_w, zeros_c, zeros_c, zeros_c)

    def first(carry, index):
        start = (index * block).astype(jnp.int32)
        xblock = lax.dynamic_slice_in_dim(padded_image, start, block + 6, 1)
        cblock = lax.dynamic_slice_in_dim(cotangent, start, block, 1)
        output, convolution_gradient, terms = local_pass(xblock, cblock, kernel, dw_bias, layer_norm_gain, layer_norm_bias, w_expand, b_expand, w_reduce, b_reduce, layer_scale)
        carry = jax.tree.map(lambda left, right: left + right, carry, terms)
        return (carry, (output, convolution_gradient))
    indices = jnp.arange(count, dtype=jnp.int32)
    sums, stacked = lax.scan(first, init, indices)
    output = jnp.transpose(stacked[0], (1, 0, 2, 3)).reshape(C, HEIGHT, WIDTH)
    convolution_gradient = jnp.transpose(stacked[1], (1, 0, 2, 3)).reshape(C, HEIGHT, WIDTH)
    padded_grad = jnp.pad(convolution_gradient, ((0, 0), (3, 3), (3, 3)))

    def second(carry, index):
        start = (index * block).astype(jnp.int32)
        xblock = lax.dynamic_slice_in_dim(padded_image, start, block + 6, 1)
        gblock = lax.dynamic_slice_in_dim(padded_grad, start, block + 6, 1)
        dblock = lax.dynamic_slice_in_dim(convolution_gradient, start, block, 1).astype(jnp.float32)
        cblock = lax.dynamic_slice_in_dim(cotangent, start, block, 1).astype(jnp.float32)
        grad_block = (cblock + conv_back(gblock, kernel, block, WIDTH)).astype(jnp.bfloat16)
        carry = carry + kernel_terms(xblock, dblock, block, WIDTH)
        return (carry, grad_block)
    kernel_sum, grad_blocks = lax.scan(second, jnp.zeros((C, 7, 7), jnp.float32), indices)
    image_grad = jnp.transpose(grad_blocks, (1, 0, 2, 3)).reshape(C, HEIGHT, WIDTH)
    factor = 1.0 / math.sqrt(TOKENS)
    g_scale, g_rbias, g_reduce, g_ebias, g_expand, norm_gain_gradient, g_lbias, g_dbias = sums
    return (output, image_grad, kernel_sum * factor, g_dbias * factor, norm_gain_gradient * factor, g_lbias * factor, g_expand * factor, g_ebias * factor, g_reduce * factor, g_rbias * factor, g_scale * factor)
```

```python
import functools
import math

import jax
import jax.numpy as jnp
from jax import lax
from jax.experimental import pallas as pl
from jax.experimental.pallas import tpu as pltpu
from jax.sharding import PartitionSpec as P

F32 = jnp.float32
BF16 = jnp.bfloat16
SIDE = 7
HALO = 3
LANES = 128
EDGE = 16
PIECES = 8
NT = (((1,), (1,)), ((), ()))
TN = (((0,), (0,)), ((), ()))


def iota(shape, dim):
    return lax.broadcasted_iota(jnp.int32, shape, dim)


def dot(a, b, dims=(((1,), (0,)), ((), ()))):
    return lax.dot_general(a, b, dims, preferred_element_type=F32)


def column(row):
    n = row.shape[1]
    eye = iota((n, n), 0) == iota((n, n), 1)
    return jnp.sum(jnp.where(eye, row, 0.0), axis=1, keepdims=True)


def pack_edges(rows):
    width = rows[0].shape[1]
    q, j = iota((2 * EDGE, width), 0), iota((2 * EDGE, width), 1)
    total = None
    for i, row in enumerate(rows):
        last = (q == HALO * i + j - (width - HALO)) & (j >= width - HALO)
        first = (q == EDGE + HALO * i + j) & (j < HALO)
        pick = jnp.where(last | first, 1.0, 0.0).astype(BF16)
        part = dot(pick, row, NT)
        total = part if total is None else total + part
    return total


def halo_tile(edges, i):
    q, l = iota((2 * EDGE, LANES), 0), iota((2 * EDGE, LANES), 1)
    left = (q == HALO * i + l - (LANES - HALO)) & (l >= LANES - HALO)
    right = (q == EDGE + HALO * i + l) & (l < HALO)
    pick = jnp.where(left | right, 1.0, 0.0).astype(BF16)
    return dot(edges, pick, TN).astype(BF16)


def taps_matrix(taps_ref, line_ref, w_ref, flip):
    channels = taps_ref.shape[2]
    for b in range(SIDE):
        line_ref[0:SIDE, b * channels : (b + 1) * channels] = taps_ref[:, SIDE - 1 - b if flip else b, :]
    lane = iota((1, SIDE * channels), 1)
    for b in range(1, SIDE):
        lane = jnp.where(iota((1, SIDE * channels), 1) >= b * channels, iota((1, SIDE * channels), 1) - b * channels, lane)
    mask = lane == iota((channels, SIDE * channels), 0)
    for m in range(SIDE):
        a = m if flip else SIDE - 1 - m
        w_ref[m * channels : (m + 1) * channels, :] = jnp.where(mask, line_ref[a : a + 1, :], 0.0).astype(BF16)
    return mask


def shifted(x, amount):
    return x if amount % x.shape[1] == 0 else pltpu.roll(x, amount % x.shape[1], 1)


def spread(xs_ref, r, x):
    channels = x.shape[0]
    width = xs_ref.shape[1]
    for b in range(SIDE):
        xs_ref[(r * SIDE + b) * channels : (r * SIDE + b + 1) * channels, :] = shifted(x, HALO - b)[:, :width]


def depthwise(w_ref, xs_ref, acc_ref, row_count, channels):
    deep = SIDE * channels
    acc_ref[...] = jnp.zeros_like(acc_ref)
    for r in range(row_count + 2 * HALO):
        i0, i1 = max(0, r - (SIDE - 1)), min(row_count - 1, r)
        m0 = SIDE - 1 - r + i0
        part = dot(w_ref[m0 * channels : (m0 + i1 - i0 + 1) * channels, :], xs_ref[r * deep : (r + 1) * deep, :])
        acc_ref[i0 * channels : (i1 + 1) * channels, :] += part


def pack_kernel(image_ref, edges_ref):
    rows = image_ref.shape[0]
    edges = pack_edges([image_ref[i] for i in range(rows)]).astype(BF16)
    edges_ref[0] = edges[:EDGE]
    edges_ref[1] = edges[EDGE:]


def widen_kernel(image_ref, left_ref, right_ref, wide_ref, top_ref, bottom_ref):
    rows, _, width = image_ref.shape
    edges = jnp.concatenate([left_ref[...], right_ref[...]], axis=0)
    for i in range(rows):
        row = jnp.concatenate([image_ref[i], halo_tile(edges, i)], axis=1)
        wide_ref[i] = row
        if i < HALO:
            top_ref[i] = row
        if i >= rows - HALO:
            bottom_ref[i - rows + HALO] = row


def gelu_parts(v):
    z = jnp.abs(v)
    t = 1.0 / (1.0 + (0.3275911 / math.sqrt(2.0)) * z)
    e = jnp.exp(-0.5 * (v * v))
    half = 0.5
    poly = t * (
        half * 0.254829592
        + t * (half * -0.284496736 + t * (half * 1.421413741 + t * (half * -1.453152027 + t * (half * 1.061405429))))
    )
    tail = poly * e
    return jnp.where(v >= 0.0, 1.0 - tail, tail), (v * (1.0 / math.sqrt(2.0 * math.pi))) * e


def main_kernel(
    spread_parts,
    axes,
    up_ref,
    mid_ref,
    down_ref,
    cot_ref,
    taps_ref,
    dwb_ref,
    gain_ref,
    lnb_ref,
    we_ref,
    be_ref,
    wr_ref,
    br_ref,
    scale_ref,
    out_ref,
    dconv_ref,
    top_ref,
    bottom_ref,
    *rest,
):
    if spread_parts:
        (block_ref, *scratch) = rest
    else:
        (grads_ref, small_out_ref, edges_ref, *scratch) = rest
    x_ref, xs_ref, w_ref, line_ref, acc_ref, xhat_ref, nm_ref, db_ref, act_ref, dh_ref, we2_ref, wide_ref, dcs_ref, small_ref = scratch
    rows, channels, width = cot_ref.shape
    hidden_n = we_ref.shape[1]
    deep = SIDE * channels
    dwb, gain, lnb, br, scale = (column(ref[...]) for ref in (dwb_ref, gain_ref, lnb_ref, br_ref, scale_ref))
    we_t = we_ref[...]
    wr_t = wr_ref[...]
    we2_ref[0:channels, :] = we_t
    extra = nm_ref.shape[0] - channels
    we2_ref[channels:, :] = jnp.where(iota((extra, hidden_n), 0) == 0, be_ref[...].astype(F32), 0.0).astype(BF16)
    we2 = we2_ref[...].T
    wr = wr_t.T
    mask = taps_matrix(taps_ref, line_ref, w_ref, False)
    for r in range(rows + 2 * HALO):
        if r < HALO:
            x = up_ref[r]
        elif r < HALO + rows:
            x = mid_ref[r - HALO]
        else:
            x = down_ref[r - HALO - rows]
        x_ref[r * channels : (r + 1) * channels, :] = x
        spread(xs_ref, r, x)
    depthwise(w_ref, xs_ref, acc_ref, rows, channels)
    nm_ref[channels:, :] = jnp.where(iota((extra, rows * width), 0) == 0, 1.0, 0.0).astype(BF16)
    zero = jnp.zeros((channels, LANES), F32)
    sums = {k: zero for k in ("dwb", "gain", "lnb", "rb", "scale")}

    def add(name, value):
        for k in range(0, width, LANES):
            sums[name] = sums[name] + value[:, k : k + LANES]

    chunk = 128
    dconv_rows = []
    for i in range(rows):
        cols = slice(i * width, (i + 1) * width)
        conv = acc_ref[i * channels : (i + 1) * channels, :] + dwb
        conv = conv - jnp.mean(conv, axis=0, keepdims=True)
        inv = lax.rsqrt(jnp.mean(conv * conv, axis=0, keepdims=True) + 1e-6)
        xhat = conv * inv
        xhat_ref[...] = xhat
        nm_ref[0:channels, cols] = (xhat * gain + lnb).astype(BF16)
        cot = cot_ref[i].astype(F32)
        add("rb", cot)
        db_ref[:, cols] = (cot * scale).astype(BF16)
        for h0 in range(0, hidden_n, chunk):
            hs = slice(h0, h0 + chunk)
            hidden = dot(we2[hs, :], nm_ref[:, cols])
            back = dot(wr[hs, :], db_ref[:, cols])
            phi, bump = gelu_parts(hidden)
            act_ref[hs, cols] = (hidden * phi).astype(BF16)
            dh_ref[hs, cols] = (back * (phi + bump)).astype(BF16)
        branch = dot(wr_t, act_ref[:, cols]) + br
        out_ref[i] = (mid_ref[i][:, :width].astype(F32) + scale * branch).astype(BF16)
        add("scale", cot * branch)
        d_normed = dot(we_t, dh_ref[:, cols])
        xhat = xhat_ref[...]
        add("lnb", d_normed)
        add("gain", d_normed * xhat)
        d_xhat = d_normed * gain
        m1 = jnp.mean(d_xhat, axis=0, keepdims=True)
        m2 = jnp.mean(d_xhat * xhat, axis=0, keepdims=True)
        dconv = (inv * (d_xhat - m1 - xhat * m2)).astype(BF16)
        add("dwb", dconv.astype(F32))
        dconv_ref[i] = dconv
        if i < HALO:
            top_ref[i] = dconv
        if i >= rows - HALO:
            bottom_ref[i - rows + HALO] = dconv
        dconv_rows.append(dconv)
        padded = jnp.concatenate([dconv, jnp.zeros((channels, LANES), BF16)], axis=1)
        for b in range(SIDE):
            dcs_ref[b * channels : (b + 1) * channels, i * (width + LANES) : (i + 1) * (width + LANES)] = shifted(padded, b - HALO)
    edges = pack_edges(dconv_rows).astype(BF16)
    g_reduce = dot(act_ref[...], db_ref[...], NT)
    g_expand = dot(dh_ref[...], nm_ref[...], NT)
    for i in range(rows):
        wide_ref[:, i * (width + LANES) : (i + 1) * (width + LANES)] = x_ref[i * channels : i * channels + deep, :]
    taps = dot(wide_ref[...], dcs_ref[...], NT)
    small_ref[...] = jnp.zeros_like(small_ref)
    for a in range(SIDE):
        line_ref[a : a + 1, :] = jnp.sum(
            jnp.where(mask, taps[a * channels : (a + 1) * channels, :], 0.0), axis=0, keepdims=True
        )
    for b in range(SIDE):
        small_ref[b * 8 : b * 8 + SIDE, 0:channels] = line_ref[0:SIDE, b * channels : (b + 1) * channels]
    for b, name in enumerate(("dwb", "gain", "lnb", "rb", "scale")):
        total = jnp.sum(sums[name].T, axis=0, keepdims=True)
        small_ref[b * 8 + SIDE : b * 8 + 8, 0:channels] = total * scale_ref[...] if name == "rb" else total
    if not spread_parts:
        grads_ref[...] = jnp.zeros_like(grads_ref)
        grads_ref[0, :, 0:channels] = g_reduce
        grads_ref[1, :, 0 : nm_ref.shape[0]] = g_expand
        small_out_ref[...] = small_ref[...]
        edges_ref[...] = jnp.zeros_like(edges_ref)
        edges_ref[:, 0:channels] = edges
        return
    space, filt = spread_parts
    me = lax.axis_index(axes[1])
    panel = hidden_n // filt
    step = 2 * panel // PIECES
    pad = lambda v: jnp.concatenate([v, jnp.zeros((v.shape[0], LANES - v.shape[1]), v.dtype)], axis=1)
    g_reduce, g_expand = pad(g_reduce), pad(g_expand)
    edges = pad(edges)
    for f in range(filt):
        edge = jnp.where(f > me, edges[:EDGE], edges[EDGE:])
        for s in range(space):
            source = g_reduce if s < PIECES // 2 else g_expand
            at = f * panel + (s % (PIECES // 2)) * step
            head = jnp.concatenate([source[at : at + step], small_ref[s * 8 : s * 8 + 8, :]], axis=0)
            block_ref[s * filt + f, 0 : step + 8, :] = head.astype(BF16)
            block_ref[s * filt + f, step + 8 :, :] = edge


def sum_kernel(axes, sizes, block_ref, total_ref, edges_ref):
    count, _, _ = block_ref.shape
    head = block_ref.shape[1] - EDGE
    total = block_ref[0, :head, :].astype(F32)
    for d in range(1, count):
        total = total + block_ref[d, :head, :].astype(F32)
    for s in range(total_ref.shape[0]):
        total_ref[s] = total
    space, filt = sizes
    s, f = lax.axis_index(axes[0]), lax.axis_index(axes[1])
    for k in range(3):
        for side in range(2):
            ss, ff = s + k - 1, f + 2 * side - 1
            inside = (ss >= 0) & (ss < space) & (ff >= 0) & (ff < filt)
            at = jnp.clip(ss, 0, space - 1) * filt + jnp.clip(ff, 0, filt - 1)
            value = block_ref[at, head:, :]
            edges_ref[k, side * EDGE : (side + 1) * EDGE, :] = jnp.where(inside, value, jnp.zeros_like(value))


def back_kernel(up_ref, mid_ref, down_ref, edges_ref, cot_ref, taps_ref, out_ref, xs_ref, w_ref, line_ref, acc_ref):
    rows, channels, width = cot_ref.shape
    taps_matrix(taps_ref, line_ref, w_ref, True)
    edges = [edges_ref[k][:, 0:channels] for k in range(3)]
    for r in range(rows + 2 * HALO):
        if r < HALO:
            x, h = up_ref[r], halo_tile(edges[0], rows - HALO + r)
        elif r < HALO + rows:
            x, h = mid_ref[r - HALO], halo_tile(edges[1], r - HALO)
        else:
            x, h = down_ref[r - HALO - rows], halo_tile(edges[2], r - HALO - rows)
        spread(xs_ref, r, jnp.concatenate([x, h], axis=1))
    depthwise(w_ref, xs_ref, acc_ref, rows, channels)
    for i in range(rows):
        out_ref[i] = (cot_ref[i].astype(F32) + acc_ref[i * channels : (i + 1) * channels, :]).astype(BF16)


def finish_kernel(factor, total_ref, kg_ref, dwb_ref, gain_ref, lnb_ref, ge_ref, eb_ref, gr_ref, rb_ref, sc_ref):
    channels = kg_ref.shape[2]
    step = total_ref.shape[1] - 8
    for b in range(SIDE):
        kg_ref[:, b, :] = total_ref[b, step : step + SIDE, 0:channels] * factor
    for b, ref in enumerate((dwb_ref, gain_ref, lnb_ref, rb_ref, sc_ref)):
        ref[...] = total_ref[b, step + SIDE :, 0:channels] * factor
    half = PIECES // 2
    for s in range(half):
        gr_ref[s * step : (s + 1) * step, :] = total_ref[s, 0:step, 0:channels] * factor
        part = total_ref[half + s, 0:step, :] * factor
        ge_ref[s * step : (s + 1) * step, :] = part[:, 0:channels]
        eye = iota((step, half * step), 0) + s * step == iota((step, half * step), 1)
        line = jnp.sum(jnp.where(eye, part[:, channels : channels + 1], 0.0), axis=0, keepdims=True)
        eb_ref[...] = line if s == 0 else eb_ref[...] + line


def call(kernel, outs, *args, scratch=(), flops=0):
    moved = sum(math.prod(a.shape) * a.dtype.itemsize for a in args) + sum(
        math.prod(s) * jnp.dtype(d).itemsize for s, d in outs
    )
    return pl.pallas_call(
        kernel,
        out_shape=[jax.ShapeDtypeStruct(s, d) for s, d in outs],
        scratch_shapes=[pltpu.VMEM(s, d) for s, d in scratch],
        compiler_params=pltpu.CompilerParams(vmem_limit_bytes=40 * 2**20),
        cost_estimate=pl.CostEstimate(flops=flops, bytes_accessed=moved, transcendentals=0),
    )(*args)


def moved(x, axis, step):
    size = lax.axis_size(axis)
    return lax.ppermute(x, axis, [(i, i + step) for i in range(size) if 0 <= i + step < size])


def shards(
    axes,
    image,
    cotangent,
    kernel,
    dw_bias,
    layer_norm_gain,
    layer_norm_bias,
    w_expand,
    b_expand,
    w_reduce,
    b_reduce,
    layer_scale,
):
    over_rows, over_cols = axes
    space, filt = lax.axis_size(over_rows), lax.axis_size(over_cols)
    channels, rows, width = image.shape
    hidden_n = w_expand.shape[0]
    panel = hidden_n // filt
    step = 2 * panel // PIECES
    deep = SIDE * channels
    tall = rows + 2 * HALO
    wide = width + LANES
    tokens = rows * width
    direct = space == PIECES
    image_t = jnp.transpose(image, (1, 0, 2))
    cot_t = jnp.transpose(cotangent, (1, 0, 2))
    taps = jnp.transpose(kernel, (1, 2, 0))
    (edges,) = call(pack_kernel, [((2, EDGE, channels), BF16)], image_t)
    left = moved(edges[0], over_cols, 1)
    right = moved(edges[1], over_cols, -1)
    mid, top, bottom = call(
        widen_kernel,
        [((rows, channels, wide), BF16), ((HALO, channels, wide), BF16), ((HALO, channels, wide), BF16)],
        image_t,
        left,
        right,
    )
    up = moved(bottom, over_rows, 1)
    down = moved(top, over_rows, -1)
    row = lambda v: v.reshape(1, -1)
    outs = [
        ((rows, channels, width), BF16),
        ((rows, channels, width), BF16),
        ((HALO, channels, width), BF16),
        ((HALO, channels, width), BF16),
    ]
    if direct:
        outs += [((space * filt, step + 8 + EDGE, LANES), BF16)]
    else:
        outs += [((2, hidden_n, LANES), F32), ((PIECES * 8, LANES), F32), ((2 * EDGE, LANES), BF16)]
    lift = channels + 16
    out_t, dconv, top, bottom, *rest = call(
        functools.partial(main_kernel, (space, filt) if direct else None, axes),
        outs,
        up,
        mid,
        down,
        cot_t,
        taps,
        row(dw_bias),
        row(layer_norm_gain),
        row(layer_norm_bias),
        w_expand.T,
        row(b_expand),
        w_reduce.T,
        row(b_reduce),
        row(layer_scale),
        scratch=[
            ((tall * channels, wide), BF16),
            ((tall * deep, width), BF16),
            ((deep, deep), BF16),
            ((8, deep), F32),
            ((rows * channels, width), F32),
            ((channels, width), F32),
            ((lift, tokens), BF16),
            ((channels, tokens), BF16),
            ((hidden_n, tokens), BF16),
            ((hidden_n, tokens), BF16),
            ((lift, hidden_n), BF16),
            ((deep, rows * wide), BF16),
            ((deep, rows * wide), BF16),
            ((PIECES * 8, LANES), F32),
        ],
    )
    up = moved(bottom, over_rows, 1)
    down = moved(top, over_rows, -1)
    if direct:
        (block,) = rest
        block = lax.all_to_all(block, axes, 0, 0, tiled=True)
        total, edges = call(
            functools.partial(sum_kernel, axes, (space, filt)),
            [((PIECES, step + 8, LANES), F32), ((3, 2 * EDGE, LANES), BF16)],
            block,
        )
        total = lax.all_to_all(total, over_rows, 0, 0, tiled=True)
    else:
        grads, small, edges = rest
        edges = jnp.concatenate([moved(edges[:EDGE], over_cols, 1), moved(edges[EDGE:], over_cols, -1)], axis=0)
        edges = jnp.stack([moved(edges, over_rows, 1), edges, moved(edges, over_rows, -1)])
        grads, small = lax.psum((grads, small), axes)
        grads = lax.dynamic_slice_in_dim(grads, lax.axis_index(over_cols) * panel, panel, 1)
        total = jnp.concatenate([grads.reshape(PIECES, step, LANES), small.reshape(PIECES, 8, LANES)], axis=1)
    (back_t,) = call(
        back_kernel,
        [((rows, channels, width), BF16)],
        up,
        dconv,
        down,
        edges,
        cot_t,
        taps,
        scratch=[
            ((tall * deep, width), BF16),
            ((deep, deep), BF16),
            ((8, deep), F32),
            ((rows * channels, width), F32),
        ],
    )
    factor = 1.0 / math.sqrt(tokens * space * filt)
    line = ((1, channels), F32)
    kg, dwb, gain, lnb, ge, eb, gr, rb, sc = call(
        functools.partial(finish_kernel, factor),
        [
            ((SIDE, SIDE, channels), F32),
            line,
            line,
            line,
            ((panel, channels), F32),
            ((1, panel), F32),
            ((panel, channels), F32),
            line,
            line,
        ],
        total,
    )
    flat = lambda v: v.reshape(-1)
    return (
        jnp.transpose(out_t, (1, 0, 2)),
        jnp.transpose(back_t, (1, 0, 2)),
        jnp.transpose(kg, (2, 0, 1)),
        flat(dwb),
        flat(gain),
        flat(lnb),
        ge,
        flat(eb),
        gr,
        flat(rb),
        flat(sc),
    )


def solution(mesh):
    axes = ("space", "filt")
    pixels = P(None, *axes)
    return jax.shard_map(
        functools.partial(shards, axes),
        mesh=mesh,
        in_specs=(pixels, pixels) + (P(),) * 9,
        out_specs=(pixels, pixels, P(), P(), P(), P(), P("filt", None), P("filt"), P("filt", None), P(), P()),
        check_vma=False,
    )
```

```python
import functools
import math

import jax
import jax.numpy as jnp
from jax import lax
from jax.experimental import pallas as pl
from jax.experimental.pallas import tpu as pltpu
from jax.sharding import Mesh, PartitionSpec as P

F32 = jnp.float32
BF16 = jnp.bfloat16
SIDE = 7
HALO = 3
LANES = 128
GROUP = 32
DEEP = SIDE * GROUP
NT = (((1,), (1,)), ((), ()))
VECTORS = ("dwb", "gain", "lnb", "rb", "scale")


def iota(shape, dim):
    return lax.broadcasted_iota(jnp.int32, shape, dim)


def dot(a, b, dims=(((1,), (0,)), ((), ()))):
    return lax.dot_general(a, b, dims, preferred_element_type=F32)


def column(row):
    n = row.shape[1]
    eye = iota((n, n), 0) == iota((n, n), 1)
    return jnp.sum(jnp.where(eye, row, 0.0), axis=1, keepdims=True)


def widened(value):
    fill = jnp.zeros((value.shape[0], LANES - value.shape[1]), value.dtype)
    return jnp.concatenate([value, fill], axis=1)


def edge_height(rows):
    return -(-HALO * rows // 16) * 16


def pack_edges(rows):
    width, high = rows[0].shape[1], edge_height(len(rows))
    q, j = iota((2 * high, width), 0), iota((2 * high, width), 1)
    total = None
    for i, row in enumerate(rows):
        last = (q == HALO * i + j - (width - HALO)) & (j >= width - HALO)
        first = (q == high + HALO * i + j) & (j < HALO)
        pick = jnp.where(last | first, 1.0, 0.0).astype(BF16)
        part = dot(pick, row, NT)
        total = part if total is None else total + part
    return total.astype(BF16)


def halo_tile(edges_t, i):
    high = edges_t.shape[1] // 2
    q, l = iota((2 * high, LANES), 0), iota((2 * high, LANES), 1)
    left = (q == HALO * i + l - (LANES - HALO)) & (l >= LANES - HALO)
    right = (q == high + HALO * i + l) & (l < HALO)
    pick = jnp.where(left | right, 1.0, 0.0).astype(BF16)
    return dot(edges_t, pick).astype(BF16)


def group_diagonal():
    lane = iota((1, DEEP), 1)
    inner = lane
    for b in range(1, SIDE):
        inner = jnp.where(lane >= b * GROUP, lane - b * GROUP, inner)
    return inner == iota((GROUP, DEEP), 0)


def tap_matrices(taps_ref, line_ref, w_ref, flip):
    diagonal = group_diagonal()
    for g in range(w_ref.shape[0]):
        for b in range(SIDE):
            piece = taps_ref[:, SIDE - 1 - b if flip else b, g * GROUP : (g + 1) * GROUP]
            line_ref[0:SIDE, b * GROUP : (b + 1) * GROUP] = piece
        for m in range(SIDE):
            a = m if flip else SIDE - 1 - m
            w_ref[g, m * GROUP : (m + 1) * GROUP, :] = jnp.where(diagonal, line_ref[a : a + 1, :], 0.0).astype(BF16)


def shifted(x, amount):
    return x if amount % x.shape[1] == 0 else pltpu.roll(x, amount % x.shape[1], 1)


def spread(xs_ref, r, x):
    channels = x.shape[0]
    width = xs_ref.shape[1]
    for b in range(SIDE):
        moved = shifted(x, HALO - b)[:, :width]
        for g in range(channels // GROUP):
            at = r * SIDE * channels + g * DEEP + b * GROUP
            xs_ref[at : at + GROUP, :] = moved[g * GROUP : (g + 1) * GROUP]


def depthwise(w_ref, xs_ref, acc_ref, rows):
    groups = w_ref.shape[0]
    channels = groups * GROUP
    for g in range(groups):
        sums = [None] * rows
        for r in range(rows + 2 * HALO):
            i0, i1 = max(0, r - (SIDE - 1)), min(rows - 1, r)
            m0 = SIDE - 1 - r + i0
            at = r * SIDE * channels + g * DEEP
            part = dot(w_ref[g, m0 * GROUP : (m0 + i1 - i0 + 1) * GROUP, :], xs_ref[at : at + DEEP, :])
            for i in range(i0, i1 + 1):
                piece = part[(i - i0) * GROUP : (i - i0 + 1) * GROUP]
                sums[i] = piece if sums[i] is None else sums[i] + piece
        for i in range(rows):
            at = i * channels + g * GROUP
            acc_ref[at : at + GROUP, :] = sums[i]


def enter_kernel(core_axis, image_ref, mid_ref, pair_ref, far_ref):
    rows = mid_ref.shape[0]
    core = lax.axis_index(core_axis)
    for i in range(rows):
        mid_ref[i] = image_ref[:, i, :]
    for k in range(HALO):
        pair_ref[k] = mid_ref[k + (rows - HALO) * (1 - core)]
        far_ref[k] = mid_ref[k + (rows - HALO) * core]


def prepare_kernel(
    cot_ref, taps_ref, dwb_ref, gain_ref, lnb_ref, we_ref, be_ref, wr_ref, br_ref, scale_ref,
    cot_t_ref, forward_ref, backward_ref, we2_ref, wr2_ref, columns_ref, lift_ref, line_ref,
):
    for i in range(cot_t_ref.shape[0]):
        cot_t_ref[i] = cot_ref[:, i, :]
    tap_matrices(taps_ref, line_ref, forward_ref, False)
    tap_matrices(taps_ref, line_ref, backward_ref, True)
    channels, hidden_n = we_ref.shape
    extra = lift_ref.shape[0] - channels
    lift_ref[0:channels, :] = we_ref[...]
    lift_ref[channels:, :] = jnp.where(iota((extra, hidden_n), 0) == 0, be_ref[...].astype(F32), 0.0).astype(BF16)
    we2_ref[...] = lift_ref[...].T
    wr2_ref[...] = wr_ref[...].T
    lane = iota(columns_ref.shape, 1)
    total = jnp.zeros(columns_ref.shape, F32)
    for k, ref in enumerate((dwb_ref, gain_ref, lnb_ref, br_ref, scale_ref)):
        total = jnp.where(lane == k, column(ref[...]), total)
    columns_ref[...] = total


def gather_kernel(axes, mid_ref, pair_ref, far_ref, tall_ref, first_ref, second_ref):
    rows = mid_ref.shape[0]
    upper = lax.axis_index(axes[1]) == 0
    for k in range(HALO):
        pair, far = pair_ref[k], far_ref[k]
        tall_ref[k] = jnp.where(upper, far, pair)
        tall_ref[HALO + rows + k] = jnp.where(upper, pair, far)
    for i in range(rows):
        tall_ref[HALO + i] = mid_ref[i]
    edges = pack_edges([tall_ref[r] for r in range(rows + 2 * HALO)])
    high = edges.shape[0] // 2
    even = lax.rem(lax.axis_index(axes[2]), 2) == 0
    first_ref[...] = jnp.where(even, edges[:high], edges[high:])
    second_ref[...] = jnp.where(even, edges[high:], edges[:high])


def gelu_parts(v):
    z = jnp.abs(v)
    t = 1.0 / (1.0 + (0.3275911 / math.sqrt(2.0)) * z)
    e = jnp.exp(-0.5 * (v * v))
    half = 0.5
    poly = t * (
        half * 0.254829592
        + t * (half * -0.284496736 + t * (half * 1.421413741 + t * (half * -1.453152027 + t * (half * 1.061405429))))
    )
    tail = poly * e
    return jnp.where(v >= 0.0, 1.0 - tail, tail), (v * (1.0 / math.sqrt(2.0 * math.pi))) * e


def main_kernel(
    direct, axes,
    tall_ref, first_ref, second_ref, cot_ref, w_ref, we_ref, wr_ref, we2_ref, wr2_ref, columns_ref, scale_ref,
    out_ref, dconv_ref, far_ref, share_ref, edges_ref, *rest,
):
    if direct:
        (keep_ref, *scratch) = rest
    else:
        (grads_ref, small_out_ref, *scratch) = rest
    xs_ref, acc_ref, xhat_ref, nm_ref, db_ref, act_ref, dh_ref, wide_ref, dcs_ref, line_ref, small_ref = scratch
    rows, channels, width = cot_ref.shape
    groups = channels // GROUP
    hidden_n = we_ref.shape[1]
    extent = width + LANES
    core = lax.axis_index(axes[1])
    even = lax.rem(lax.axis_index(axes[2]), 2) == 0
    dwb, gain, lnb, br, scale = (columns_ref[:, k : k + 1] for k in range(5))
    first, second = first_ref[...], second_ref[...]
    edges_t = jnp.concatenate([jnp.where(even, second, first), jnp.where(even, first, second)], axis=0).T
    for r in range(rows + 2 * HALO):
        x = jnp.concatenate([tall_ref[r], halo_tile(edges_t, r)], axis=1)
        spread(xs_ref, r, x)
        for i in range(rows):
            if 0 <= r - i < SIDE:
                for g in range(groups):
                    at = g * DEEP + (r - i) * GROUP
                    wide_ref[at : at + GROUP, i * extent : (i + 1) * extent] = x[g * GROUP : (g + 1) * GROUP]
    depthwise(w_ref, xs_ref, acc_ref, rows)
    extra = nm_ref.shape[0] - channels
    nm_ref[channels:, :] = jnp.where(iota((extra, rows * width), 0) == 0, 1.0, 0.0).astype(BF16)
    zero = jnp.zeros((channels, LANES), F32)
    sums = {k: zero for k in VECTORS}

    def add(name, value):
        for k in range(0, width, LANES):
            sums[name] = sums[name] + value[:, k : k + LANES]

    chunk = 128
    dconv_rows = []
    for i in range(rows):
        cols = slice(i * width, (i + 1) * width)
        conv = acc_ref[i * channels : (i + 1) * channels, :] + dwb
        conv = conv - jnp.mean(conv, axis=0, keepdims=True)
        inv = lax.rsqrt(jnp.mean(conv * conv, axis=0, keepdims=True) + 1e-6)
        xhat = conv * inv
        xhat_ref[...] = xhat
        nm_ref[0:channels, cols] = (xhat * gain + lnb).astype(BF16)
        cot = cot_ref[i].astype(F32)
        add("rb", cot)
        db_ref[:, cols] = (cot * scale).astype(BF16)
        for h0 in range(0, hidden_n, chunk):
            hs = slice(h0, h0 + chunk)
            hidden = dot(we2_ref[hs, :], nm_ref[:, cols])
            back = dot(wr2_ref[hs, :], db_ref[:, cols])
            phi, bump = gelu_parts(hidden)
            act_ref[hs, cols] = (hidden * phi).astype(BF16)
            dh_ref[hs, cols] = (back * (phi + bump)).astype(BF16)
        branch = dot(wr_ref[...], act_ref[:, cols]) + br
        out_ref[i] = (tall_ref[HALO + i].astype(F32) + scale * branch).astype(BF16)
        add("scale", cot * branch)
        d_normed = dot(we_ref[...], dh_ref[:, cols])
        xhat = xhat_ref[...]
        add("lnb", d_normed)
        add("gain", d_normed * xhat)
        d_xhat = d_normed * gain
        m1 = jnp.mean(d_xhat, axis=0, keepdims=True)
        m2 = jnp.mean(d_xhat * xhat, axis=0, keepdims=True)
        dconv = (inv * (d_xhat - m1 - xhat * m2)).astype(BF16)
        add("dwb", dconv.astype(F32))
        dconv_ref[i] = dconv
        dconv_rows.append(dconv)
        padded = jnp.concatenate([dconv, jnp.zeros((channels, LANES), BF16)], axis=1)
        for b in range(SIDE):
            moved = shifted(padded, b - HALO)
            for g in range(groups):
                at = g * DEEP + b * GROUP
                dcs_ref[at : at + GROUP, i * extent : (i + 1) * extent] = moved[g * GROUP : (g + 1) * GROUP]
    for k in range(HALO):
        pair = dconv_ref[k + (rows - HALO) * (1 - core)]
        far_ref[k] = dconv_ref[k + (rows - HALO) * core]
        for p in range(width // LANES):
            at = (k * (width // LANES) + p) * channels
            share_ref[at : at + channels, :] = pair[:, p * LANES : (p + 1) * LANES]
    edges_ref[...] = widened(pack_edges(dconv_rows))
    g_reduce = widened(dot(act_ref[...], db_ref[...], NT))
    g_expand = widened(dot(dh_ref[...], nm_ref[...], NT))
    small_ref[...] = jnp.zeros_like(small_ref)
    diagonal = group_diagonal()
    for g in range(groups):
        taps = dot(wide_ref[g * DEEP : (g + 1) * DEEP, :], dcs_ref[g * DEEP : (g + 1) * DEEP, :], NT)
        for a in range(SIDE):
            part = jnp.where(diagonal, taps[a * GROUP : (a + 1) * GROUP, :], 0.0)
            line_ref[a : a + 1, :] = jnp.sum(part, axis=0, keepdims=True)
        for b in range(SIDE):
            small_ref[b * 8 : b * 8 + SIDE, g * GROUP : (g + 1) * GROUP] = line_ref[0:SIDE, b * GROUP : (b + 1) * GROUP]
    for b, name in enumerate(VECTORS):
        total = jnp.sum(sums[name].T, axis=0, keepdims=True)
        small_ref[b * 8 + SIDE : b * 8 + 8, 0:channels] = total * scale_ref[...] if name == "rb" else total
    if not direct:
        grads_ref[0] = g_reduce
        grads_ref[1] = g_expand
        small_out_ref[...] = small_ref[...]
        return
    half = small_ref.shape[0] // 2
    low, high = small_ref[0:half, :], small_ref[half:, :]
    lead = HALO * (width // LANES) * channels
    keep_ref[0:hidden_n, :] = jnp.where(core == 0, g_reduce, g_expand)
    keep_ref[hidden_n:, :] = jnp.where(core == 0, low, high)
    share_ref[lead : lead + hidden_n, :] = jnp.where(core == 0, g_expand, g_reduce).astype(BF16)
    share_ref[lead + hidden_n :, :] = jnp.where(core == 0, high, low).astype(BF16)


def block_kernel(sizes, filt_axis, share_ref, keep_ref, edges_ref, block_ref):
    chips, filt = sizes
    me = lax.axis_index(filt_axis)
    count = keep_ref.shape[0]
    lead = share_ref.shape[0] - count
    total = keep_ref[...] + share_ref[lead:, :].astype(F32)
    edges = edges_ref[...]
    high = edges.shape[0] // 2
    hidden_n = count - 8 * chips
    step = hidden_n // (filt * chips)
    for f in range(filt):
        edge = jnp.where(f > me, edges[:high], edges[high:])
        for q in range(chips):
            at = (f * chips + q) * step
            low = hidden_n + 8 * q
            head = jnp.concatenate([total[at : at + step], total[low : low + 8]], axis=0)
            block_ref[q * filt + f, 0 : step + 8, :] = head.astype(BF16)
            block_ref[q * filt + f, step + 8 :, :] = edge


def sum_kernel(axes, sizes, block_ref, total_ref, edges_ref):
    chips, filt = sizes
    head = total_ref.shape[1]
    total = block_ref[0, :head, :].astype(F32)
    for d in range(1, block_ref.shape[0]):
        total = total + block_ref[d, :head, :].astype(F32)
    total = total.astype(BF16)
    for s in range(total_ref.shape[0]):
        total_ref[s] = total
    q, core, f = (lax.axis_index(a) for a in axes)
    high = edges_ref.shape[0] // 4
    for k, chip in enumerate((q, q + 1 - 2 * core)):
        for side in range(2):
            ff = f + 2 * side - 1
            inside = (chip >= 0) & (chip < chips) & (ff >= 0) & (ff < filt)
            at = jnp.clip(chip, 0, chips - 1) * filt + jnp.clip(ff, 0, filt - 1)
            value = block_ref[at, head:, :]
            low = (2 * k + side) * high
            edges_ref[low : low + high, :] = jnp.where(inside, value, jnp.zeros_like(value))


def back_kernel(core_axis, share_ref, far_ref, mid_ref, own_ref, other_ref, cot_ref, w_ref, out_ref, xs_ref, acc_ref):
    rows, channels, width = cot_ref.shape
    upper = lax.axis_index(core_axis) == 0
    high = own_ref.shape[0] // 2
    near, beyond = other_ref[:high, 0:channels], other_ref[high:, 0:channels]
    edges = (jnp.where(upper, beyond, near).T, own_ref[:high, 0:channels].T, jnp.where(upper, near, beyond).T)
    parts = width // LANES
    for k in range(HALO):
        pair = [share_ref[(k * parts + p) * channels : (k * parts + p + 1) * channels, :] for p in range(parts)]
        pair = jnp.concatenate(pair, axis=1)
        far = far_ref[k]
        up, down = jnp.where(upper, far, pair), jnp.where(upper, pair, far)
        spread(xs_ref, k, jnp.concatenate([up, halo_tile(edges[0], rows - HALO + k)], axis=1))
        spread(xs_ref, HALO + rows + k, jnp.concatenate([down, halo_tile(edges[2], k)], axis=1))
    for i in range(rows):
        spread(xs_ref, HALO + i, jnp.concatenate([mid_ref[i], halo_tile(edges[1], i)], axis=1))
    depthwise(w_ref, xs_ref, acc_ref, rows)
    for i in range(rows):
        out_ref[i] = (cot_ref[i].astype(F32) + acc_ref[i * channels : (i + 1) * channels, :]).astype(BF16)


def finish_kernel(factor, total_ref, kg_ref, dwb_ref, gain_ref, lnb_ref, ge_ref, eb_ref, gr_ref, rb_ref, sc_ref):
    channels = kg_ref.shape[2]
    chips = total_ref.shape[0] // 2
    step = total_ref.shape[1] - 8
    vectors = (dwb_ref, gain_ref, lnb_ref, rb_ref, sc_ref)
    for s in range(2 * chips):
        q, core = s // 2, s % 2
        part = total_ref[s].astype(F32) * factor
        b = core * chips + q
        if b < SIDE:
            kg_ref[:, b, :] = part[step : step + SIDE, 0:channels]
        if b < len(vectors):
            vectors[b][...] = part[step + SIDE :, 0:channels]
        if core == 0:
            gr_ref[q * step : (q + 1) * step, :] = part[0:step, 0:channels]
        else:
            ge_ref[q * step : (q + 1) * step, :] = part[0:step, 0:channels]
            eye = iota((step, chips * step), 0) + q * step == iota((step, chips * step), 1)
            line = jnp.sum(jnp.where(eye, part[0:step, channels : channels + 1], 0.0), axis=0, keepdims=True)
            eb_ref[...] = line if q == 0 else eb_ref[...] + line


def call(kernel, outs, *args, scratch=(), flops=0):
    size = sum(math.prod(a.shape) * a.dtype.itemsize for a in args)
    size += sum(math.prod(s) * jnp.dtype(d).itemsize for s, d in outs)
    return pl.pallas_call(
        kernel,
        out_shape=[jax.ShapeDtypeStruct(s, d) for s, d in outs],
        scratch_shapes=[pltpu.VMEM(s, d) for s, d in scratch],
        compiler_params=pltpu.CompilerParams(vmem_limit_bytes=40 * 2**20),
        cost_estimate=pl.CostEstimate(flops=flops, bytes_accessed=size, transcendentals=0),
    )(*args)


def swap(x, axis, parity):
    size = lax.axis_size(axis)
    pairs = [(i, i + 1) for i in range(parity, size - 1, 2)]
    return lax.ppermute(x, axis, pairs + [(j, i) for i, j in pairs])


def moved(x, axis, step):
    size = lax.axis_size(axis)
    return lax.ppermute(x, axis, [(i, i + step) for i in range(size) if 0 <= i + step < size])


def shards(
    axes, image, cotangent, kernel, dw_bias, layer_norm_gain, layer_norm_bias,
    w_expand, b_expand, w_reduce, b_reduce, layer_scale,
):
    chip, core, filt = axes
    space = (chip, core)
    chip_n, filt_n = lax.axis_size(chip), lax.axis_size(filt)
    channels, rows, width = image.shape
    hidden_n = w_expand.shape[0]
    groups = channels // GROUP
    panel = hidden_n // filt_n
    tall = rows + 2 * HALO
    deep = SIDE * channels
    extent = width + LANES
    tokens = rows * width
    lift = channels + 16
    direct = chip_n == 4
    pieces = 8
    step = 2 * panel // pieces
    strip = ((HALO, channels, width), BF16)
    block = ((rows, channels, width), BF16)
    row = lambda v: v.reshape(1, -1)

    mid, pair, far = call(functools.partial(enter_kernel, core), [block, strip, strip], image)
    far = swap(far, space, 1)
    pair = swap(pair, core, 0)
    we_t, wr_t = w_expand.T, w_reduce.T
    cot_t, forward, backward, we2, wr2, columns = call(
        prepare_kernel,
        [
            block,
            ((groups, DEEP, DEEP), BF16),
            ((groups, DEEP, DEEP), BF16),
            ((hidden_n, lift), BF16),
            ((hidden_n, channels), BF16),
            ((channels, LANES), F32),
        ],
        cotangent, jnp.transpose(kernel, (1, 2, 0)), row(dw_bias), row(layer_norm_gain), row(layer_norm_bias),
        we_t, row(b_expand), wr_t, row(b_reduce), row(layer_scale),
        scratch=[((lift, hidden_n), BF16), ((8, DEEP), F32)],
    )
    edge = ((edge_height(tall), channels), BF16)
    image_t, first, second = call(
        functools.partial(gather_kernel, axes), [((tall, channels, width), BF16), edge, edge], mid, pair, far
    )
    first = swap(first, filt, 0)
    second = swap(second, filt, 1)
    lead = HALO * channels * (width // LANES)
    half = pieces * 8 // 2
    high = edge_height(rows)
    outs = [block, block, strip]
    if direct:
        outs += [((lead + hidden_n + half, LANES), BF16), ((2 * high, LANES), BF16), ((hidden_n + half, LANES), F32)]
    else:
        outs += [((lead, LANES), BF16), ((2 * high, LANES), BF16)]
        outs += [((2, hidden_n, LANES), F32), ((2 * half, LANES), F32)]
    out_t, dconv, far, share, edges, *rest = call(
        functools.partial(main_kernel, direct, axes),
        outs,
        image_t, first, second, cot_t, forward, we_t, wr_t, we2, wr2, columns, row(layer_scale),
        scratch=[
            ((tall * deep, width), BF16),
            ((rows * channels, width), F32),
            ((channels, width), F32),
            ((lift, tokens), BF16),
            ((channels, tokens), BF16),
            ((hidden_n, tokens), BF16),
            ((hidden_n, tokens), BF16),
            ((deep, rows * extent), BF16),
            ((deep, rows * extent), BF16),
            ((8, DEEP), F32),
            ((2 * half, LANES), F32),
        ],
    )
    share = swap(share, core, 0)
    far = swap(far, space, 1)
    if direct:
        (blocks,) = call(
            functools.partial(block_kernel, (chip_n, filt_n), filt),
            [((chip_n * filt_n, step + 8 + high, LANES), BF16)],
            share, *rest, edges,
        )
        blocks = lax.all_to_all(blocks, (chip, filt), 0, 0, tiled=True)
        total, edges = call(
            functools.partial(sum_kernel, axes, (chip_n, filt_n)),
            [((pieces, step + 8, LANES), BF16), ((4 * high, LANES), BF16)],
            blocks,
        )
        other = swap(edges, core, 0)
        total = lax.all_to_all(total, space, 0, 0, tiled=True)
    else:
        grads, small = rest
        edges = jnp.concatenate([moved(edges[:high], filt, 1), moved(edges[high:], filt, -1)], axis=0)
        above, below = moved(edges, space, 1), moved(edges, space, -1)
        upper = lax.axis_index(core) == 0
        other = jnp.concatenate([jnp.where(upper, below, above), jnp.where(upper, above, below)], axis=0)
        edges = jnp.concatenate([edges, edges], axis=0)
        grads, small = lax.psum((grads, small), axes)
        grads = lax.dynamic_slice_in_dim(grads, lax.axis_index(filt) * panel, panel, 1)
        grads = grads.reshape(2, pieces // 2, step, LANES).swapaxes(0, 1).reshape(pieces, step, LANES)
        small = small.reshape(2, pieces // 2, 8, LANES).swapaxes(0, 1).reshape(pieces, 8, LANES)
        total = jnp.concatenate([grads, small], axis=1)
    (back_t,) = call(
        functools.partial(back_kernel, core),
        [block],
        share, far, dconv, edges, other, cot_t, backward,
        scratch=[((tall * deep, width), BF16), ((rows * channels, width), F32)],
    )
    factor = 1.0 / math.sqrt(tokens * chip_n * lax.axis_size(core) * filt_n)
    line = ((1, channels), F32)
    matrix = ((panel, channels), F32)
    kg, dwb, gain, lnb, ge, eb, gr, rb, sc = call(
        functools.partial(finish_kernel, factor),
        [((SIDE, SIDE, channels), F32), line, line, line, matrix, ((1, panel), F32), matrix, line, line],
        total,
    )
    flat = lambda v: v.reshape(-1)
    swapped = lambda v: jnp.transpose(v, (1, 0, 2))
    return (
        swapped(out_t), swapped(back_t), jnp.transpose(kg, (2, 0, 1)),
        flat(dwb), flat(gain), flat(lnb), ge, flat(eb), gr, flat(rb), flat(sc),
    )


def solution(mesh):
    space, filt = mesh.devices.shape
    axes = ("chip", "core", "filt")
    pairs = Mesh(mesh.devices.reshape(space // 2, 2, filt), axes)
    pixels = P(None, ("chip", "core"), "filt")
    whole, shard = P(), P("filt")
    return jax.shard_map(
        functools.partial(shards, axes),
        mesh=pairs,
        in_specs=(pixels, pixels) + (whole,) * 9,
        out_specs=(pixels, pixels, whole, whole, whole, whole, shard, shard, shard, whole, whole),
        check_vma=False,
    )
```

```python
import functools
import math

import jax
import jax.numpy as jnp
from jax import lax
from jax.experimental import pallas as pl
from jax.experimental.pallas import tpu as pltpu
from jax.sharding import Mesh, PartitionSpec as P

F32 = jnp.float32
BF16 = jnp.bfloat16
SIDE = 7
HALO = 3
LANES = 128
GROUP = 32
DEEP = SIDE * GROUP
NT = (((1,), (1,)), ((), ()))
VECTORS = ("dwb", "gain", "lnb", "rb", "scale")


def iota(shape, dim):
    return lax.broadcasted_iota(jnp.int32, shape, dim)


def dot(a, b, dims=(((1,), (0,)), ((), ()))):
    return lax.dot_general(a, b, dims, preferred_element_type=F32)


def column(row):
    n = row.shape[1]
    eye = iota((n, n), 0) == iota((n, n), 1)
    return jnp.sum(jnp.where(eye, row, 0.0), axis=1, keepdims=True)


def widened(value):
    fill = jnp.zeros((value.shape[0], LANES - value.shape[1]), value.dtype)
    return jnp.concatenate([value, fill], axis=1)


def widened(value):
    fill = jnp.zeros((value.shape[0], LANES - value.shape[1]), value.dtype)
    return jnp.concatenate([value, fill], axis=1)


def edge_height(rows):
    return -(-HALO * rows // 16) * 16


def pack_edges(rows):
    width, high = rows[0].shape[1], edge_height(len(rows))
    q, j = iota((2 * high, width), 0), iota((2 * high, width), 1)
    total = None
    for i, row in enumerate(rows):
        last = (q == HALO * i + j - (width - HALO)) & (j >= width - HALO)
        first = (q == high + HALO * i + j) & (j < HALO)
        pick = jnp.where(last | first, 1.0, 0.0).astype(BF16)
        part = dot(pick, row, NT)
        total = part if total is None else total + part
    return total.astype(BF16)


def halo_tile(edges_t, i):
    high = edges_t.shape[1] // 2
    q, l = iota((2 * high, LANES), 0), iota((2 * high, LANES), 1)
    left = (q == HALO * i + l - (LANES - HALO)) & (l >= LANES - HALO)
    right = (q == high + HALO * i + l) & (l < HALO)
    pick = jnp.where(left | right, 1.0, 0.0).astype(BF16)
    return dot(edges_t, pick).astype(BF16)


def group_diagonal():
    lane = iota((1, DEEP), 1)
    inner = lane
    for b in range(1, SIDE):
        inner = jnp.where(lane >= b * GROUP, lane - b * GROUP, inner)
    return inner == iota((GROUP, DEEP), 0)


def tap_matrices(taps_ref, line_ref, w_ref, flip):
    diagonal = group_diagonal()
    for g in range(w_ref.shape[0]):
        for b in range(SIDE):
            piece = taps_ref[:, SIDE - 1 - b if flip else b, g * GROUP : (g + 1) * GROUP]
            line_ref[0:SIDE, b * GROUP : (b + 1) * GROUP] = piece
        for m in range(SIDE):
            a = m if flip else SIDE - 1 - m
            w_ref[g, m * GROUP : (m + 1) * GROUP, :] = jnp.where(diagonal, line_ref[a : a + 1, :], 0.0).astype(BF16)


def shifted(x, amount):
    return x if amount % x.shape[1] == 0 else pltpu.roll(x, amount % x.shape[1], 1)


def spread(xs_ref, r, x):
    channels = x.shape[0]
    width = xs_ref.shape[1]
    for b in range(SIDE):
        moved = shifted(x, HALO - b)[:, :width]
        for g in range(channels // GROUP):
            at = r * SIDE * channels + g * DEEP + b * GROUP
            xs_ref[at : at + GROUP, :] = moved[g * GROUP : (g + 1) * GROUP]


def depthwise(w_ref, xs_ref, acc_ref, rows):
    groups = w_ref.shape[0]
    channels = groups * GROUP
    for g in range(groups):
        sums = [None] * rows
        for r in range(rows + 2 * HALO):
            i0, i1 = max(0, r - (SIDE - 1)), min(rows - 1, r)
            m0 = SIDE - 1 - r + i0
            at = r * SIDE * channels + g * DEEP
            part = dot(w_ref[g, m0 * GROUP : (m0 + i1 - i0 + 1) * GROUP, :], xs_ref[at : at + DEEP, :])
            for i in range(i0, i1 + 1):
                piece = part[(i - i0) * GROUP : (i - i0 + 1) * GROUP]
                sums[i] = piece if sums[i] is None else sums[i] + piece
        for i in range(rows):
            at = i * channels + g * GROUP
            acc_ref[at : at + GROUP, :] = sums[i]


def enter_kernel(core_axis, image_ref, mid_ref, pair_ref, far_ref):
    rows = mid_ref.shape[0]
    core = lax.axis_index(core_axis)
    for i in range(rows):
        mid_ref[i] = image_ref[:, i, :]
    for k in range(HALO):
        pair_ref[k] = mid_ref[k + (rows - HALO) * (1 - core)]
        far_ref[k] = mid_ref[k + (rows - HALO) * core]


def gather_kernel(axes, mid_ref, pair_ref, far_ref, tall_ref, first_ref, second_ref):
    rows = mid_ref.shape[0]
    upper = lax.axis_index(axes[1]) == 0
    for k in range(HALO):
        pair, far = pair_ref[k], far_ref[k]
        tall_ref[k] = jnp.where(upper, far, pair)
        tall_ref[HALO + rows + k] = jnp.where(upper, pair, far)
    for i in range(rows):
        tall_ref[HALO + i] = mid_ref[i]
    edges = pack_edges([tall_ref[r] for r in range(rows + 2 * HALO)])
    high = edges.shape[0] // 2
    even = lax.rem(lax.axis_index(axes[2]), 2) == 0
    first_ref[...] = jnp.where(even, edges[:high], edges[high:])
    second_ref[...] = jnp.where(even, edges[high:], edges[:high])


def put_strip(ref, k, row):
    channels, width = row.shape
    parts = width // LANES
    for p in range(parts):
        ref[(k * parts + p) * channels : (k * parts + p + 1) * channels, :] = row[:, p * LANES : (p + 1) * LANES]


def get_strip(ref, k, channels, width):
    parts = width // LANES
    pieces = [ref[(k * parts + p) * channels : (k * parts + p + 1) * channels, :] for p in range(parts)]
    return jnp.concatenate(pieces, axis=1)


def prepare_kernel(
    cot_ref, taps_ref, dwb_ref, gain_ref, lnb_ref, we_ref, be_ref, wr_ref, br_ref, scale_ref,
    cot_t_ref, forward_ref, backward_ref, we2_ref, wr2_ref, columns_ref, lift_ref, line_ref,
):
    for i in range(cot_t_ref.shape[0]):
        cot_t_ref[i] = cot_ref[:, i, :]
    tap_matrices(taps_ref, line_ref, forward_ref, False)
    tap_matrices(taps_ref, line_ref, backward_ref, True)
    channels, hidden_n = we_ref.shape
    extra = lift_ref.shape[0] - channels
    lift_ref[0:channels, :] = we_ref[...]
    lift_ref[channels:, :] = jnp.where(iota((extra, hidden_n), 0) == 0, be_ref[...].astype(F32), 0.0).astype(BF16)
    we2_ref[...] = lift_ref[...].T
    wr2_ref[...] = wr_ref[...].T
    lane = iota(columns_ref.shape, 1)
    total = jnp.zeros(columns_ref.shape, F32)
    for k, ref in enumerate((dwb_ref, gain_ref, lnb_ref, br_ref, scale_ref)):
        total = jnp.where(lane == k, column(ref[...]), total)
    columns_ref[...] = total


def gelu_parts(v):
    z = jnp.abs(v)
    t = 1.0 / (1.0 + (0.3275911 / math.sqrt(2.0)) * z)
    e = jnp.exp(-0.5 * (v * v))
    half = 0.5
    poly = t * (
        half * 0.254829592
        + t * (half * -0.284496736 + t * (half * 1.421413741 + t * (half * -1.453152027 + t * (half * 1.061405429))))
    )
    tail = poly * e
    return jnp.where(v >= 0.0, 1.0 - tail, tail), (v * (1.0 / math.sqrt(2.0 * math.pi))) * e


def main_kernel(
    direct, axes,
    tall_ref, first_ref, second_ref, cot_ref, w_ref, we_ref, wr_ref, we2_ref, wr2_ref, columns_ref, scale_ref,
    out_ref, dconv_ref, far_ref, edges_ref, share_ref, *rest,
):
    if direct:
        (keep_ref, *scratch) = rest
    else:
        (grads_ref, small_out_ref, *scratch) = rest
    xs_ref, acc_ref, xhat_ref, nm_ref, db_ref, act_ref, dh_ref, wide_ref, dcs_ref, line_ref, small_ref = scratch
    rows, channels, width = cot_ref.shape
    groups = channels // GROUP
    hidden_n = we_ref.shape[1]
    extent = width + LANES
    core = lax.axis_index(axes[1])
    dwb, gain, lnb, br, scale = (columns_ref[:, k : k + 1] for k in range(5))
    lead = HALO * channels * (width // LANES)
    even = lax.rem(lax.axis_index(axes[2]), 2) == 0
    first, second = first_ref[...], second_ref[...]
    edges_t = jnp.concatenate([jnp.where(even, second, first), jnp.where(even, first, second)], axis=0).T
    for r in range(rows + 2 * HALO):
        x = jnp.concatenate([tall_ref[r], halo_tile(edges_t, r)], axis=1)
        spread(xs_ref, r, x)
        for i in range(rows):
            if 0 <= r - i < SIDE:
                for g in range(groups):
                    at = g * DEEP + (r - i) * GROUP
                    wide_ref[at : at + GROUP, i * extent : (i + 1) * extent] = x[g * GROUP : (g + 1) * GROUP]
    depthwise(w_ref, xs_ref, acc_ref, rows)
    extra = nm_ref.shape[0] - channels
    nm_ref[channels:, :] = jnp.where(iota((extra, rows * width), 0) == 0, 1.0, 0.0).astype(BF16)
    zero = jnp.zeros((channels, LANES), F32)
    sums = {k: zero for k in VECTORS}

    def add(name, value):
        for k in range(0, width, LANES):
            sums[name] = sums[name] + value[:, k : k + LANES]

    chunk = 128
    dconv_rows = []
    for i in range(rows):
        cols = slice(i * width, (i + 1) * width)
        conv = acc_ref[i * channels : (i + 1) * channels, :] + dwb
        conv = conv - jnp.mean(conv, axis=0, keepdims=True)
        inv = lax.rsqrt(jnp.mean(conv * conv, axis=0, keepdims=True) + 1e-6)
        xhat = conv * inv
        xhat_ref[...] = xhat
        nm_ref[0:channels, cols] = (xhat * gain + lnb).astype(BF16)
        cot = cot_ref[i].astype(F32)
        add("rb", cot)
        db_ref[:, cols] = (cot * scale).astype(BF16)
        for h0 in range(0, hidden_n, chunk):
            hs = slice(h0, h0 + chunk)
            hidden = dot(we2_ref[hs, :], nm_ref[:, cols])
            back = dot(wr2_ref[hs, :], db_ref[:, cols])
            phi, bump = gelu_parts(hidden)
            act_ref[hs, cols] = (hidden * phi).astype(BF16)
            dh_ref[hs, cols] = (back * (phi + bump)).astype(BF16)
        branch = dot(wr_ref[...], act_ref[:, cols]) + br
        out_ref[i] = (tall_ref[HALO + i].astype(F32) + scale * branch).astype(BF16)
        add("scale", cot * branch)
        d_normed = dot(we_ref[...], dh_ref[:, cols])
        xhat = xhat_ref[...]
        add("lnb", d_normed)
        add("gain", d_normed * xhat)
        d_xhat = d_normed * gain
        m1 = jnp.mean(d_xhat, axis=0, keepdims=True)
        m2 = jnp.mean(d_xhat * xhat, axis=0, keepdims=True)
        dconv = (inv * (d_xhat - m1 - xhat * m2)).astype(BF16)
        add("dwb", dconv.astype(F32))
        dconv_ref[i] = dconv
        dconv_rows.append(dconv)
        padded = jnp.concatenate([dconv, jnp.zeros((channels, LANES), BF16)], axis=1)
        for b in range(SIDE):
            moved = shifted(padded, b - HALO)
            for g in range(groups):
                at = g * DEEP + b * GROUP
                dcs_ref[at : at + GROUP, i * extent : (i + 1) * extent] = moved[g * GROUP : (g + 1) * GROUP]
    for k in range(HALO):
        put_strip(share_ref, k, dconv_ref[k + (rows - HALO) * (1 - core)])
        far_ref[k] = dconv_ref[k + (rows - HALO) * core]
    edges_ref[...] = widened(pack_edges(dconv_rows))
    g_reduce = widened(dot(act_ref[...], db_ref[...], NT))
    g_expand = widened(dot(dh_ref[...], nm_ref[...], NT))
    small_ref[...] = jnp.zeros_like(small_ref)
    diagonal = group_diagonal()
    for g in range(groups):
        taps = dot(wide_ref[g * DEEP : (g + 1) * DEEP, :], dcs_ref[g * DEEP : (g + 1) * DEEP, :], NT)
        for a in range(SIDE):
            part = jnp.where(diagonal, taps[a * GROUP : (a + 1) * GROUP, :], 0.0)
            line_ref[a : a + 1, :] = jnp.sum(part, axis=0, keepdims=True)
        for b in range(SIDE):
            small_ref[b * 8 : b * 8 + SIDE, g * GROUP : (g + 1) * GROUP] = line_ref[0:SIDE, b * GROUP : (b + 1) * GROUP]
    for b, name in enumerate(VECTORS):
        total = jnp.sum(sums[name].T, axis=0, keepdims=True)
        small_ref[b * 8 + SIDE : b * 8 + 8, 0:channels] = total * scale_ref[...] if name == "rb" else total
    if not direct:
        grads_ref[0] = g_reduce
        grads_ref[1] = g_expand
        small_out_ref[...] = small_ref[...]
        return
    half = small_ref.shape[0] // 2
    low, high = small_ref[0:half, :], small_ref[half:, :]
    keep_ref[0:hidden_n, :] = jnp.where(core == 0, g_reduce, g_expand)
    keep_ref[hidden_n:, :] = jnp.where(core == 0, low, high)
    share_ref[lead : lead + hidden_n, :] = jnp.where(core == 0, g_expand, g_reduce).astype(BF16)
    share_ref[lead + hidden_n :, :] = jnp.where(core == 0, high, low).astype(BF16)


def block_kernel(axis, small, share_ref, keep_ref, edges_ref, block_ref):
    filt = lax.axis_size(axis)
    me = lax.axis_index(axis)
    count = keep_ref.shape[0]
    lead = share_ref.shape[0] - count
    high = edges_ref.shape[0] // 2
    panel = (count - small) // filt
    total = (keep_ref[...] + share_ref[lead:, :].astype(F32)).astype(BF16)
    edges = edges_ref[...]
    for f in range(filt):
        block_ref[f, 0:panel, :] = total[f * panel : (f + 1) * panel]
        block_ref[f, panel : panel + small, :] = total[count - small :]
        block_ref[f, panel + small :, :] = jnp.where(f > me, edges[:high], edges[high:])


def columns_kernel(axis, block_ref, spread_ref):
    filt = block_ref.shape[0]
    count = spread_ref.shape[1]
    high = count - block_ref.shape[1]
    head = block_ref.shape[1] - high
    f = lax.axis_index(axis)
    total = block_ref[0, :head, :].astype(F32)
    for d in range(1, filt):
        total = total + block_ref[d, :head, :].astype(F32)
    pieces = [total.astype(BF16)]
    for ff in (f - 1, f + 1):
        value = block_ref[jnp.clip(ff, 0, filt - 1), head:, :]
        pieces.append(jnp.where((ff >= 0) & (ff < filt), value, jnp.zeros_like(value)))
    value = jnp.concatenate(pieces, axis=0)
    for q in range(spread_ref.shape[0]):
        spread_ref[q] = value


def chips_kernel(axes, block_ref, total_ref):
    chips, count, _ = block_ref.shape
    low = 2 * count - total_ref.shape[0]
    q, core = lax.axis_index(axes[0]), lax.axis_index(axes[1])
    total = block_ref[0, :low, :].astype(F32)
    for d in range(1, chips):
        total = total + block_ref[d, :low, :].astype(F32)
    total_ref[:low, :] = total
    total_ref[low:count, :] = block_ref[q, low:, :].astype(F32)
    other = q + 1 - 2 * core
    value = block_ref[jnp.clip(other, 0, chips - 1), low:, :].astype(F32)
    total_ref[count:, :] = jnp.where((other >= 0) & (other < chips), value, jnp.zeros_like(value))


def back_kernel(core_axis, mid_ref, share_ref, far_ref, cot_ref, w_ref, acc_ref, xs_ref):
    rows, channels, width = cot_ref.shape
    upper = lax.axis_index(core_axis) == 0
    nothing = jnp.zeros((channels, LANES), BF16)
    put = lambda r, x: spread(xs_ref, r, jnp.concatenate([x, nothing], axis=1))
    for k in range(HALO):
        pair, far = get_strip(share_ref, k, channels, width), far_ref[k]
        put(k, jnp.where(upper, far, pair))
        put(HALO + rows + k, jnp.where(upper, pair, far))
    for i in range(rows):
        put(HALO + i, mid_ref[i])
    depthwise(w_ref, xs_ref, acc_ref, rows)
    for i in range(rows):
        acc_ref[i * channels : (i + 1) * channels, :] += cot_ref[i].astype(F32)


def finish_kernel(
    factor, core_axis, mine_ref, other_ref, acc_ref, w_ref,
    back_ref, kg_ref, dwb_ref, gain_ref, lnb_ref, ge_ref, eb_ref, gr_ref, rb_ref, sc_ref, xs_ref, side_ref,
):
    channels = kg_ref.shape[2]
    panel = gr_ref.shape[0]
    low = panel + 32
    core = lax.axis_index(core_axis)
    rows, width = back_ref.shape[1:]
    wide = 2 * edge_height(rows)
    own, near, beyond = (
        ref[at : at + wide, :].astype(BF16)[:, :channels].T
        for ref, at in ((mine_ref, low), (other_ref, low), (other_ref, low + wide))
    )
    above, below = jnp.where(core == 0, beyond, near), jnp.where(core == 0, near, beyond)
    sources = [(above, rows - HALO + k) for k in range(HALO)] + [(own, i) for i in range(rows)]
    sources += [(below, k) for k in range(HALO)]
    lane = iota((channels, LANES), 1)
    for r, (edges_t, i) in enumerate(sources):
        tile = halo_tile(edges_t, i)
        left = jnp.where(lane >= LANES - HALO, tile, jnp.zeros_like(tile))
        right = jnp.where(lane < HALO, tile, jnp.zeros_like(tile))
        for b in range(SIDE):
            if b < HALO:
                moved = jnp.where(lane < HALO, shifted(left, HALO - b), jnp.zeros_like(tile))
            elif b > HALO:
                moved = jnp.where(lane >= LANES - HALO, shifted(right, HALO - b), jnp.zeros_like(tile))
            else:
                moved = jnp.zeros_like(tile)
            for g in range(channels // GROUP):
                at = r * SIDE * channels + g * DEEP + b * GROUP
                xs_ref[at : at + GROUP, :] = moved[g * GROUP : (g + 1) * GROUP]
    depthwise(w_ref, xs_ref, side_ref, rows)
    for i in range(rows):
        at = slice(i * channels, (i + 1) * channels)
        side = side_ref[at, :]
        value = acc_ref[at, :]
        first = value[:, :LANES] + jnp.where(lane < HALO, side, 0.0)
        last = value[:, width - LANES :] + jnp.where(lane >= LANES - HALO, side, 0.0)
        middle = [value[:, k : k + LANES] for k in range(LANES, width - LANES, LANES)]
        value = jnp.concatenate([first, *middle, last], axis=1)
        back_ref[:, i, :] = value.astype(BF16)
    mine, other = mine_ref[0:low, :] * factor, other_ref[0:low, :] * factor
    low, high = jnp.where(core == 0, mine, other), jnp.where(core == 0, other, mine)
    small = jnp.concatenate([low[panel:], high[panel:]], axis=0)
    for b in range(SIDE):
        kg_ref[:, b, :] = small[b * 8 : b * 8 + SIDE, 0:channels]
    for b, ref in enumerate((dwb_ref, gain_ref, lnb_ref, rb_ref, sc_ref)):
        ref[...] = small[b * 8 + SIDE : b * 8 + 8, 0:channels]
    gr_ref[...] = low[0:panel, 0:channels]
    ge_ref[...] = high[0:panel, 0:channels]
    eye = iota((panel, panel), 0) == iota((panel, panel), 1)
    eb_ref[...] = jnp.sum(jnp.where(eye, high[0:panel, channels : channels + 1], 0.0), axis=0, keepdims=True)


def call(kernel, outs, *args, scratch=(), after=()):
    size = sum(math.prod(a.shape) * a.dtype.itemsize for a in args)
    size += sum(math.prod(s) * jnp.dtype(d).itemsize for s, d in outs)
    count = len(args)

    def body(*refs):
        kernel(*refs[:count], *refs[count + len(after) :])

    in_vmem = pl.BlockSpec(memory_space=pltpu.VMEM)
    anywhere = pl.BlockSpec(memory_space=pl.ANY)
    return pl.pallas_call(
        body,
        out_shape=[jax.ShapeDtypeStruct(s, d) for s, d in outs],
        in_specs=[in_vmem] * count + [anywhere] * len(after),
        out_specs=[in_vmem] * len(outs),
        scratch_shapes=[pltpu.VMEM(s, d) for s, d in scratch],
        compiler_params=pltpu.CompilerParams(vmem_limit_bytes=40 * 2**20),
        cost_estimate=pl.CostEstimate(flops=0, bytes_accessed=size, transcendentals=0),
    )(*args, *after)


def swap(x, axis, parity):
    size = lax.axis_size(axis)
    pairs = [(i, i + 1) for i in range(parity, size - 1, 2)]
    return lax.ppermute(x, axis, pairs + [(j, i) for i, j in pairs])


def edges_by_permutes(axes, edges):
    chip, core, filt = axes
    count = lax.axis_size(filt)
    right = [(i, i + 1) for i in range(count - 1)]
    left = [(j, i) for i, j in right]
    high = edges.shape[0] // 2
    own = jnp.concatenate([lax.ppermute(edges[:high], filt, right), lax.ppermute(edges[high:], filt, left)], axis=0)
    return jnp.concatenate([own, swap(own, (chip, core), 1)], axis=0)


def shards(
    axes, image, cotangent, kernel, dw_bias, layer_norm_gain, layer_norm_bias,
    w_expand, b_expand, w_reduce, b_reduce, layer_scale,
):
    chip, core, filt = axes
    chip_n, core_n, filt_n = (lax.axis_size(a) for a in axes)
    channels, rows, width = image.shape
    hidden_n = w_expand.shape[0]
    groups = channels // GROUP
    panel = hidden_n // filt_n
    tall = rows + 2 * HALO
    deep = SIDE * channels
    extent = width + LANES
    tokens = rows * width
    lift = channels + 16
    direct = chip_n == 4
    strip = ((HALO, channels, width), BF16)
    block = ((rows, channels, width), BF16)
    high = edge_height(rows)
    edge = ((2 * high, LANES), BF16)
    row = lambda v: v.reshape(1, -1)

    space = (chip, core)
    lead = HALO * channels * (width // LANES)
    mid, pair, far = call(functools.partial(enter_kernel, core), [block, strip, strip], image)
    far = swap(far, space, 1)
    pair = swap(pair, core, 0)
    we_t, wr_t = w_expand.T, w_reduce.T
    cot_t, forward, backward, we2, wr2, columns = call(
        prepare_kernel,
        [
            block,
            ((groups, DEEP, DEEP), BF16),
            ((groups, DEEP, DEEP), BF16),
            ((hidden_n, lift), BF16),
            ((hidden_n, channels), BF16),
            ((channels, LANES), F32),
        ],
        cotangent, jnp.transpose(kernel, (1, 2, 0)), row(dw_bias), row(layer_norm_gain), row(layer_norm_bias),
        we_t, row(b_expand), wr_t, row(b_reduce), row(layer_scale),
        scratch=[((lift, hidden_n), BF16), ((8, DEEP), F32)],
    )
    ends = ((edge_height(tall), channels), BF16)
    image_t, first, second = call(
        functools.partial(gather_kernel, axes), [((tall, channels, width), BF16), ends, ends], mid, pair, far,
        after=[columns],
    )
    first, second = swap(first, filt, 0), swap(second, filt, 1)
    half = 32
    outs = [block, block, strip, edge]
    if direct:
        outs += [((lead + hidden_n + half, LANES), BF16), ((hidden_n + half, LANES), F32)]
    else:
        outs += [((lead, LANES), BF16), ((2, hidden_n, LANES), F32), ((2 * half, LANES), F32)]
    out_t, dconv, far_out, edges, share, *rest = call(
        functools.partial(main_kernel, direct, axes),
        outs,
        image_t, first, second, cot_t, forward, we_t, wr_t, we2, wr2, columns, row(layer_scale),
        scratch=[
            ((tall * deep, width), BF16),
            ((rows * channels, width), F32),
            ((channels, width), F32),
            ((lift, tokens), BF16),
            ((channels, tokens), BF16),
            ((hidden_n, tokens), BF16),
            ((hidden_n, tokens), BF16),
            ((deep, rows * extent), BF16),
            ((deep, rows * extent), BF16),
            ((8, DEEP), F32),
            ((2 * half, LANES), F32),
        ],
    )
    output = jnp.transpose(out_t, (1, 0, 2))
    share = swap(share, core, 0)
    far = swap(far_out, space, 1)
    low = panel + half
    (back,) = call(
        functools.partial(back_kernel, core),
        [((rows * channels, width), F32)],
        dconv, share, far, cot_t, backward,
        scratch=[((tall * deep, width), BF16)],
    )
    if direct:
        (blocks,) = call(
            functools.partial(block_kernel, filt, half), [((filt_n, low + high, LANES), BF16)], share, *rest, edges
        )
        blocks = lax.all_to_all(blocks, filt, 0, 0, tiled=True)
        (blocks,) = call(
            functools.partial(columns_kernel, filt), [((chip_n, low + 2 * high, LANES), BF16)], blocks, after=[output]
        )
        blocks = lax.all_to_all(blocks, chip, 0, 0, tiled=True)
        (mine,) = call(functools.partial(chips_kernel, axes), [((low + 4 * high, LANES), F32)], blocks, after=[back])
        other = swap(mine, core, 0)
    else:
        edges = edges_by_permutes(axes, edges).astype(F32)
        grads, small = lax.psum(tuple(rest), axes)
        grads = lax.dynamic_slice_in_dim(grads, lax.axis_index(filt) * panel, panel, 1)
        upper = lax.axis_index(core) == 0
        halves = [jnp.concatenate([grads[k], small[k * half : (k + 1) * half]], axis=0) for k in range(2)]
        mine = jnp.concatenate([jnp.where(upper, halves[0], halves[1]), edges], axis=0)
        other = jnp.concatenate([jnp.where(upper, halves[1], halves[0]), swap(edges, core, 0)], axis=0)
    factor = 1.0 / math.sqrt(tokens * chip_n * core_n * filt_n)
    line = ((1, channels), F32)
    matrix = ((panel, channels), F32)
    image_grad, kg, dwb, gain, lnb, ge, eb, gr, rb, sc = call(
        functools.partial(finish_kernel, factor, core),
        [
            ((channels, rows, width), BF16),
            ((SIDE, SIDE, channels), F32),
            line, line, line, matrix, ((1, panel), F32), matrix, line, line,
        ],
        mine, other, back, backward,
        scratch=[((tall * deep, LANES), BF16), ((rows * channels, LANES), F32)],
    )
    flat = lambda v: v.reshape(-1)
    return (
        output, image_grad, jnp.transpose(kg, (2, 0, 1)),
        flat(dwb), flat(gain), flat(lnb), ge, flat(eb), gr, flat(rb), flat(sc),
    )


def solution(mesh):
    space, filt = mesh.devices.shape
    axes = ("chip", "core", "filt")
    pairs = Mesh(mesh.devices.reshape(space // 2, 2, filt), axes)
    pixels = P(None, ("chip", "core"), "filt")
    whole, shard = P(), P("filt")
    return jax.shard_map(
        functools.partial(shards, axes),
        mesh=pairs,
        in_specs=(pixels, pixels) + (whole,) * 9,
        out_specs=(pixels, pixels, whole, whole, whole, whole, shard, shard, shard, whole, whole),
        check_vma=False,
    )
```

```python
import functools
import math

import jax
import jax.numpy as jnp
from jax import lax
from jax.experimental import pallas as pl
from jax.experimental.pallas import tpu as pltpu
from jax.sharding import Mesh, PartitionSpec as P

F32 = jnp.float32
BF16 = jnp.bfloat16
SIDE = 7
HALO = 3
LANES = 128
GROUP = 32
DEEP = SIDE * GROUP
NT = (((1,), (1,)), ((), ()))
VECTORS = ("dwb", "gain", "lnb", "rb", "scale")


def iota(shape, dim):
    return lax.broadcasted_iota(jnp.int32, shape, dim)


def dot(a, b, dims=(((1,), (0,)), ((), ()))):
    return lax.dot_general(a, b, dims, preferred_element_type=F32)


def column(row):
    n = row.shape[1]
    eye = iota((n, n), 0) == iota((n, n), 1)
    return jnp.sum(jnp.where(eye, row, 0.0), axis=1, keepdims=True)


def widened(value):
    fill = jnp.zeros((value.shape[0], LANES - value.shape[1]), value.dtype)
    return jnp.concatenate([value, fill], axis=1)


def edge_height(rows):
    return -(-HALO * rows // 16) * 16


def pack_edges(rows):
    count = len(rows)
    width, high = rows[0].shape[1], edge_height(count)
    q, j = iota((2 * high, width), 0), iota((2 * high, width), 1)
    total = None
    for i, row in enumerate(rows):
        last = (q == count * (j - (width - HALO)) + i) & (j >= width - HALO)
        first = (q == high + count * j + i) & (j < HALO)
        pick = jnp.where(last | first, 1.0, 0.0).astype(BF16)
        part = dot(pick, row, NT)
        total = part if total is None else total + part
    return total.astype(BF16)


def halo_tile(edges_t, i, count):
    high = edges_t.shape[1] // 2
    q, l = iota((2 * high, LANES), 0), iota((2 * high, LANES), 1)
    left = (q == count * (l - (LANES - HALO)) + i) & (l >= LANES - HALO)
    right = (q == high + count * l + i) & (l < HALO)
    pick = jnp.where(left | right, 1.0, 0.0).astype(BF16)
    return dot(edges_t, pick).astype(BF16)


def group_diagonal():
    lane = iota((1, DEEP), 1)
    inner = lane
    for b in range(1, SIDE):
        inner = jnp.where(lane >= b * GROUP, lane - b * GROUP, inner)
    return inner == iota((GROUP, DEEP), 0)


def tap_matrices(taps_ref, line_ref, w_ref, flip):
    diagonal = group_diagonal()
    for g in range(w_ref.shape[0]):
        for b in range(SIDE):
            piece = taps_ref[:, SIDE - 1 - b if flip else b, g * GROUP : (g + 1) * GROUP]
            line_ref[0:SIDE, b * GROUP : (b + 1) * GROUP] = piece
        for m in range(SIDE):
            a = m if flip else SIDE - 1 - m
            w_ref[g, m * GROUP : (m + 1) * GROUP, :] = jnp.where(diagonal, line_ref[a : a + 1, :], 0.0).astype(BF16)


def shifted(x, amount):
    return x if amount % x.shape[1] == 0 else pltpu.roll(x, amount % x.shape[1], 1)


def spread(xs_ref, r, x):
    channels = x.shape[0]
    width = xs_ref.shape[1]
    for b in range(SIDE):
        moved = shifted(x, HALO - b)[:, :width]
        for g in range(channels // GROUP):
            at = r * SIDE * channels + g * DEEP + b * GROUP
            xs_ref[at : at + GROUP, :] = moved[g * GROUP : (g + 1) * GROUP]


def depthwise(w_ref, xs_ref, acc_ref, rows):
    groups = w_ref.shape[0]
    channels = groups * GROUP
    for g in range(groups):
        sums = [None] * rows
        for r in range(rows + 2 * HALO):
            i0, i1 = max(0, r - (SIDE - 1)), min(rows - 1, r)
            m0 = SIDE - 1 - r + i0
            at = r * SIDE * channels + g * DEEP
            part = dot(w_ref[g, m0 * GROUP : (m0 + i1 - i0 + 1) * GROUP, :], xs_ref[at : at + DEEP, :])
            for i in range(i0, i1 + 1):
                piece = part[(i - i0) * GROUP : (i - i0 + 1) * GROUP]
                sums[i] = piece if sums[i] is None else sums[i] + piece
        for i in range(rows):
            at = i * channels + g * GROUP
            acc_ref[at : at + GROUP, :] = sums[i]


def enter_kernel(core_axis, mid_ref, pair_ref, far_ref):
    rows = mid_ref.shape[0]
    core = lax.axis_index(core_axis)
    for k in range(HALO):
        pair_ref[k] = mid_ref[k + (rows - HALO) * (1 - core)]
        far_ref[k] = mid_ref[k + (rows - HALO) * core]


def gather_kernel(axes, mid_ref, pair_ref, far_ref, tall_ref, first_ref, second_ref):
    rows = mid_ref.shape[0]
    upper = lax.axis_index(axes[1]) == 0
    for k in range(HALO):
        pair, far = pair_ref[k], far_ref[k]
        tall_ref[k] = jnp.where(upper, far, pair)
        tall_ref[HALO + rows + k] = jnp.where(upper, pair, far)
    for i in range(rows):
        tall_ref[HALO + i] = mid_ref[i]
    edges = pack_edges([tall_ref[r] for r in range(rows + 2 * HALO)])
    high = edges.shape[0] // 2
    even = lax.rem(lax.axis_index(axes[2]), 2) == 0
    first_ref[...] = jnp.where(even, edges[:high], edges[high:])
    second_ref[...] = jnp.where(even, edges[high:], edges[:high])


def put_strip(ref, k, row):
    channels, width = row.shape
    parts = width // LANES
    for p in range(parts):
        ref[(k * parts + p) * channels : (k * parts + p + 1) * channels, :] = row[:, p * LANES : (p + 1) * LANES]


def get_strip(ref, k, channels, width):
    parts = width // LANES
    pieces = [ref[(k * parts + p) * channels : (k * parts + p + 1) * channels, :] for p in range(parts)]
    return jnp.concatenate(pieces, axis=1)


def prepare_kernel(
    cot_ref, taps_ref, dwb_ref, gain_ref, lnb_ref, we_ref, be_ref, wr_ref, br_ref, scale_ref,
    cot_t_ref, forward_ref, backward_ref, we2_ref, wr2_ref, columns_ref, lift_ref, line_ref,
):
    for i in range(cot_t_ref.shape[0]):
        cot_t_ref[i] = cot_ref[:, i, :]
    tap_matrices(taps_ref, line_ref, forward_ref, False)
    tap_matrices(taps_ref, line_ref, backward_ref, True)
    channels, hidden_n = we_ref.shape
    extra = lift_ref.shape[0] - channels
    lift_ref[0:channels, :] = we_ref[...]
    lift_ref[channels:, :] = jnp.where(iota((extra, hidden_n), 0) == 0, be_ref[...].astype(F32), 0.0).astype(BF16)
    we2_ref[...] = lift_ref[...].T
    wr2_ref[...] = wr_ref[...].T
    lane = iota(columns_ref.shape, 1)
    total = jnp.zeros(columns_ref.shape, F32)
    for k, ref in enumerate((dwb_ref, gain_ref, lnb_ref, br_ref, scale_ref)):
        total = jnp.where(lane == k, column(ref[...]), total)
    columns_ref[...] = total


def gelu_parts(v):
    z = jnp.abs(v)
    t = 1.0 / (1.0 + (0.3275911 / math.sqrt(2.0)) * z)
    e = jnp.exp(-0.5 * (v * v))
    half = 0.5
    poly = t * (
        half * 0.254829592
        + t * (half * -0.284496736 + t * (half * 1.421413741 + t * (half * -1.453152027 + t * (half * 1.061405429))))
    )
    tail = poly * e
    return jnp.where(v >= 0.0, 1.0 - tail, tail), (v * (1.0 / math.sqrt(2.0 * math.pi))) * e


def main_kernel(
    axes,
    tall_ref, first_ref, second_ref, cot_ref, w_ref, we_ref, wr_ref, we2_ref, wr2_ref, columns_ref, scale_ref,
    out_ref, dconv_ref, far_ref, x_ref, vectors_ref, share_ref, keep_ref,
    xs_ref, acc_ref, xhat_ref, nm_ref, db_ref, act_ref, dh_ref,
):
    rows, channels, width = cot_ref.shape
    hidden_n = we_ref.shape[1]
    core = lax.axis_index(axes[1])
    dwb, gain, lnb, br, scale = (columns_ref[:, k : k + 1] for k in range(5))
    lead = HALO * channels * (width // LANES)
    even = lax.rem(lax.axis_index(axes[2]), 2) == 0
    first, second = first_ref[...], second_ref[...]
    edges_t = jnp.concatenate([jnp.where(even, second, first), jnp.where(even, first, second)], axis=0).T
    for r in range(rows + 2 * HALO):
        x = jnp.concatenate([tall_ref[r], halo_tile(edges_t, r, rows + 2 * HALO)], axis=1)
        spread(xs_ref, r, x)
        x_ref[r] = x
    depthwise(w_ref, xs_ref, acc_ref, rows)
    extra = nm_ref.shape[0] - channels
    nm_ref[channels:, :] = jnp.where(iota((extra, rows * width), 0) == 0, 1.0, 0.0).astype(BF16)
    zero = jnp.zeros((channels, LANES), F32)
    sums = {k: zero for k in VECTORS}

    def add(name, value):
        for k in range(0, width, LANES):
            sums[name] = sums[name] + value[:, k : k + LANES]

    chunk = 128
    for i in range(rows):
        cols = slice(i * width, (i + 1) * width)
        conv = acc_ref[i * channels : (i + 1) * channels, :] + dwb
        conv = conv - jnp.mean(conv, axis=0, keepdims=True)
        inv = lax.rsqrt(jnp.mean(conv * conv, axis=0, keepdims=True) + 1e-6)
        xhat = conv * inv
        xhat_ref[...] = xhat
        nm_ref[0:channels, cols] = (xhat * gain + lnb).astype(BF16)
        cot = cot_ref[i].astype(F32)
        add("rb", cot)
        db_ref[:, cols] = (cot * scale).astype(BF16)
        for h0 in range(0, hidden_n, chunk):
            hs = slice(h0, h0 + chunk)
            hidden = dot(we2_ref[hs, :], nm_ref[:, cols])
            back = dot(wr2_ref[hs, :], db_ref[:, cols])
            phi, bump = gelu_parts(hidden)
            act_ref[hs, cols] = (hidden * phi).astype(BF16)
            dh_ref[hs, cols] = (back * (phi + bump)).astype(BF16)
        branch = dot(wr_ref[...], act_ref[:, cols]) + br
        out_ref[i] = (tall_ref[HALO + i].astype(F32) + scale * branch).astype(BF16)
        add("scale", cot * branch)
        d_normed = dot(we_ref[...], dh_ref[:, cols])
        xhat = xhat_ref[...]
        add("lnb", d_normed)
        add("gain", d_normed * xhat)
        d_xhat = d_normed * gain
        m1 = jnp.mean(d_xhat, axis=0, keepdims=True)
        m2 = jnp.mean(d_xhat * xhat, axis=0, keepdims=True)
        dconv = (inv * (d_xhat - m1 - xhat * m2)).astype(BF16)
        add("dwb", dconv.astype(F32))
        dconv_ref[i] = dconv
    for k in range(HALO):
        put_strip(share_ref, k, dconv_ref[k + (rows - HALO) * (1 - core)])
        far_ref[k] = dconv_ref[k + (rows - HALO) * core]
    g_reduce = widened(dot(act_ref[...], db_ref[...], NT))
    g_expand = widened(dot(dh_ref[...], nm_ref[...], NT))
    keep_ref[...] = jnp.where(core == 0, g_reduce, g_expand)
    share_ref[lead:, :] = jnp.where(core == 0, g_expand, g_reduce).astype(BF16)
    vectors_ref[...] = jnp.zeros_like(vectors_ref)
    for b, name in enumerate(VECTORS):
        total = jnp.sum(sums[name].T, axis=0, keepdims=True)
        vectors_ref[b : b + 1, 0:channels] = total * scale_ref[...] if name == "rb" else total


def depthwise_gradient_kernel(x_ref, dconv_ref, vectors_ref, edges_ref, small_ref, wide_ref, dcs_ref, line_ref):
    rows, channels, width = dconv_ref.shape
    groups = channels // GROUP
    extent = width + LANES
    edges_ref[...] = widened(pack_edges([dconv_ref[i] for i in range(rows)]))
    for i in range(rows):
        padded = jnp.concatenate([dconv_ref[i], jnp.zeros((channels, LANES), BF16)], axis=1)
        columns = slice(i * extent, (i + 1) * extent)
        for b in range(SIDE):
            moved = shifted(padded, b - HALO)
            for g in range(groups):
                at = g * DEEP + b * GROUP
                dcs_ref[at : at + GROUP, columns] = moved[g * GROUP : (g + 1) * GROUP]
        for a in range(SIDE):
            for g in range(groups):
                at = g * DEEP + a * GROUP
                wide_ref[at : at + GROUP, columns] = x_ref[i + a, g * GROUP : (g + 1) * GROUP, :]
    small_ref[...] = jnp.zeros_like(small_ref)
    diagonal = group_diagonal()
    for g in range(groups):
        taps = dot(wide_ref[g * DEEP : (g + 1) * DEEP, :], dcs_ref[g * DEEP : (g + 1) * DEEP, :], NT)
        for a in range(SIDE):
            part = jnp.where(diagonal, taps[a * GROUP : (a + 1) * GROUP, :], 0.0)
            line_ref[a : a + 1, :] = jnp.sum(part, axis=0, keepdims=True)
        for b in range(SIDE):
            small_ref[b * 8 : b * 8 + SIDE, g * GROUP : (g + 1) * GROUP] = line_ref[0:SIDE, b * GROUP : (b + 1) * GROUP]
    for b in range(len(VECTORS)):
        small_ref[b * 8 + SIDE : b * 8 + 8, :] = vectors_ref[b : b + 1, :]


def first_kernel(axis, panel, share_ref, keep_ref, small_ref, edges_ref, send_ref, rest_ref, total_ref):
    f = lax.axis_index(axis)
    count = total_ref.shape[0]
    total_ref[...] = keep_ref[...] + share_ref[share_ref.shape[0] - count :, :].astype(F32)
    part = lambda k: total_ref[pl.ds(pl.multiple_of(k * panel, 8), panel), :]
    tail = small_ref[...].astype(BF16)
    small = tail.shape[0]
    even = lax.rem(f, 2) == 0
    mate = f + 1 - 2 * lax.rem(f, 2)
    send_ref[0:panel, :] = part(mate).astype(BF16)
    send_ref[panel : 2 * panel, :] = part(3 - mate).astype(BF16)
    send_ref[2 * panel : 2 * panel + small, :] = tail
    high = edges_ref.shape[0] // 2
    send_ref[2 * panel + small :, :] = jnp.where(even, edges_ref[:high, :], edges_ref[high:, :])
    rest_ref[0:panel, :] = part(f)
    rest_ref[panel : 2 * panel, :] = part(3 - f)
    rest_ref[2 * panel :, :] = tail.astype(F32)


def second_kernel(axis, panel, got_ref, rest_ref, edges_ref, send_ref, kept_ref):
    even = lax.rem(lax.axis_index(axis), 2) == 0
    count = rest_ref.shape[0]
    total = rest_ref[...] + got_ref[0:count, :].astype(F32)
    tail = total[2 * panel :].astype(BF16)
    small = tail.shape[0]
    high = edges_ref.shape[0] // 2
    send_ref[0:panel, :] = total[panel : 2 * panel].astype(BF16)
    send_ref[panel : panel + small, :] = tail
    send_ref[panel + small :, :] = jnp.where(even, edges_ref[high:, :], edges_ref[:high, :])
    kept_ref[0:panel, :] = total[0:panel]
    kept_ref[panel:, :] = tail.astype(F32)


def third_kernel(axis, got_ref, kept_ref, before_ref, send_ref):
    f = lax.axis_index(axis)
    even = lax.rem(f, 2) == 0
    count = kept_ref.shape[0]
    near = before_ref[before_ref.shape[0] - (got_ref.shape[0] - count) :, :]
    far = got_ref[count:, :]
    far = jnp.where((f == 0) | (f == lax.axis_size(axis) - 1), jnp.zeros_like(far), far)
    total = kept_ref[...] + got_ref[0:count, :].astype(F32)
    edges = [jnp.where(even, far, near), jnp.where(even, near, far)]
    send_ref[...] = jnp.concatenate([total.astype(BF16), *edges], axis=0)


def fourth_kernel(count, got_ref, mine_ref, send_ref):
    total = mine_ref[0:count, :].astype(F32) + got_ref[0:count, :].astype(F32)
    send_ref[...] = jnp.concatenate([total.astype(BF16), mine_ref[count:, :], got_ref[count:, :]], axis=0)


def fifth_kernel(axes, count, got_ref, mine_ref, total_ref):
    q, core = lax.axis_index(axes[0]), lax.axis_index(axes[1])
    total_ref[0:count, :] = mine_ref[0:count, :].astype(F32) + got_ref[0:count, :].astype(F32)
    wide = (got_ref.shape[0] - count) // 2
    total_ref[count : count + wide, :] = mine_ref[count : count + wide, :].astype(F32)
    other = q + 1 - 2 * core
    beside = lax.rem(q + core, 2) == 0
    value = jnp.where(beside, got_ref[count : count + wide, :], got_ref[count + wide :, :]).astype(F32)
    total_ref[count + wide :, :] = jnp.where((other >= 0) & (other < lax.axis_size(axes[0])), value, 0.0)


def back_kernel(core_axis, mid_ref, share_ref, far_ref, cot_ref, w_ref, acc_ref, xs_ref):
    rows, channels, width = cot_ref.shape
    upper = lax.axis_index(core_axis) == 0
    nothing = jnp.zeros((channels, LANES), BF16)
    put = lambda r, x: spread(xs_ref, r, jnp.concatenate([x, nothing], axis=1))
    for k in range(HALO):
        pair, far = get_strip(share_ref, k, channels, width), far_ref[k]
        put(k, jnp.where(upper, far, pair))
        put(HALO + rows + k, jnp.where(upper, pair, far))
    for i in range(rows):
        put(HALO + i, mid_ref[i])
    depthwise(w_ref, xs_ref, acc_ref, rows)
    for i in range(rows):
        acc_ref[i * channels : (i + 1) * channels, :] += cot_ref[i].astype(F32)


def finish_kernel(
    factor, core_axis, mine_ref, other_ref, acc_ref, taps_ref,
    back_ref, kg_ref, dwb_ref, gain_ref, lnb_ref, ge_ref, eb_ref, gr_ref, rb_ref, sc_ref, ends_ref, side_ref,
):
    channels = kg_ref.shape[2]
    panel = gr_ref.shape[0]
    core = lax.axis_index(core_axis)
    rows, width = back_ref.shape[1:]
    high = edge_height(rows)
    low = mine_ref.shape[0] - 4 * high
    own, near, beyond = mine_ref[low : low + 2 * high, :], other_ref[low : low + 2 * high, :], other_ref[low + 2 * high :, :]
    above, below = jnp.where(core == 0, beyond, near), jnp.where(core == 0, near, beyond)
    for side in range(2):
        for k in range(HALO):
            at = side * high + k * rows
            ends_ref[side * HALO + k, 0:HALO, :] = above[at + rows - HALO : at + rows]
            ends_ref[side * HALO + k, HALO : HALO + rows, :] = own[at : at + rows]
            ends_ref[side * HALO + k, HALO + rows : 2 * HALO + rows, :] = below[at : at + HALO]
    side_ref[...] = jnp.zeros_like(side_ref)
    for side in range(2):
        for j in range(HALO):
            total = None
            for k in range(HALO):
                b = k + side * (SIDE - 1) - j
                if not 0 <= b < SIDE:
                    continue
                for a in range(SIDE):
                    tap = taps_ref[SIDE - 1 - a, SIDE - 1 - b : SIDE - b, :]
                    part = tap * ends_ref[side * HALO + k, a : a + rows, 0:channels]
                    total = part if total is None else total + part
            at = (side * HALO + j) * rows
            side_ref[at : at + rows, 0:channels] = total
    side = side_ref[...]
    upper = side.astype(BF16)
    lower = (side - upper.astype(F32)).astype(BF16)
    side_t = jnp.concatenate([upper, lower], axis=0).T
    count = side_ref.shape[0]
    q, l = iota((2 * count, LANES), 0), iota((2 * count, LANES), 1)
    q = jnp.where(q >= count, q - count, q)
    for i in range(rows):
        first = (q == l * rows + i) & (l < HALO)
        last = (q == (HALO + l - (LANES - HALO)) * rows + i) & (l >= LANES - HALO)
        extra = [dot(side_t, jnp.where(at, 1.0, 0.0).astype(BF16))[0:channels] for at in (first, last)]
        value = acc_ref[i * channels : (i + 1) * channels, :]
        tiles = [value[:, k : k + LANES] for k in range(0, width, LANES)]
        tiles[0] = tiles[0] + extra[0]
        tiles[-1] = tiles[-1] + extra[1]
        back_ref[:, i, :] = jnp.concatenate(tiles, axis=1).astype(BF16)
    mine, other = mine_ref[0:low, :] * factor, other_ref[0:low, :] * factor
    low, high = jnp.where(core == 0, mine, other), jnp.where(core == 0, other, mine)
    small = mine[panel:] + other[panel:]
    for b in range(SIDE):
        kg_ref[:, b, :] = small[b * 8 : b * 8 + SIDE, 0:channels]
    for b, ref in enumerate((dwb_ref, gain_ref, lnb_ref, rb_ref, sc_ref)):
        ref[...] = small[b * 8 + SIDE : b * 8 + 8, 0:channels]
    gr_ref[...] = low[0:panel, 0:channels]
    ge_ref[...] = high[0:panel, 0:channels]
    eye = iota((panel, panel), 0) == iota((panel, panel), 1)
    eb_ref[...] = jnp.sum(jnp.where(eye, high[0:panel, channels : channels + 1], 0.0), axis=0, keepdims=True)


def call(kernel, outs, *args, scratch=(), after=()):
    size = sum(math.prod(a.shape) * a.dtype.itemsize for a in args)
    size += sum(math.prod(s) * jnp.dtype(d).itemsize for s, d in outs)
    count = len(args)

    def body(*refs):
        kernel(*refs[:count], *refs[count + len(after) :])

    in_vmem = pl.BlockSpec(memory_space=pltpu.VMEM)
    anywhere = pl.BlockSpec(memory_space=pl.ANY)
    return pl.pallas_call(
        body,
        out_shape=[jax.ShapeDtypeStruct(s, d) for s, d in outs],
        in_specs=[in_vmem] * count + [anywhere] * len(after),
        out_specs=[in_vmem] * len(outs),
        scratch_shapes=[pltpu.VMEM(s, d) for s, d in scratch],
        compiler_params=pltpu.CompilerParams(vmem_limit_bytes=40 * 2**20),
        cost_estimate=pl.CostEstimate(flops=0, bytes_accessed=size, transcendentals=0),
    )(*args, *after)


def swap(x, axis, parity):
    size = lax.axis_size(axis)
    pairs = [(i, i + 1) for i in range(parity, size - 1, 2)]
    return lax.ppermute(x, axis, pairs + [(j, i) for i, j in pairs])


def crossed(x, axis, bits):
    return lax.ppermute(x, axis, [(i, i ^ bits) for i in range(lax.axis_size(axis))])


def edges_by_permutes(axes, edges):
    chip, core, filt = axes
    count = lax.axis_size(filt)
    right = [(i, i + 1) for i in range(count - 1)]
    left = [(j, i) for i, j in right]
    high = edges.shape[0] // 2
    own = jnp.concatenate([lax.ppermute(edges[:high], filt, right), lax.ppermute(edges[high:], filt, left)], axis=0)
    return jnp.concatenate([own, swap(own, (chip, core), 1)], axis=0)


def shards(
    axes, image, cotangent, kernel, dw_bias, layer_norm_gain, layer_norm_bias,
    w_expand, b_expand, w_reduce, b_reduce, layer_scale,
):
    chip, core, filt = axes
    chip_n, core_n, filt_n = (lax.axis_size(a) for a in axes)
    channels, rows, width = image.shape
    hidden_n = w_expand.shape[0]
    groups = channels // GROUP
    panel = hidden_n // filt_n
    tall = rows + 2 * HALO
    deep = SIDE * channels
    extent = width + LANES
    tokens = rows * width
    lift = channels + 16
    direct = chip_n == 4 and filt_n == 4
    strip = ((HALO, channels, width), BF16)
    block = ((rows, channels, width), BF16)
    high = edge_height(rows)
    edge = ((2 * high, LANES), BF16)
    row = lambda v: v.reshape(1, -1)

    space = (chip, core)
    lead = HALO * channels * (width // LANES)
    mid = jnp.transpose(image, (1, 0, 2))
    pair, far = call(functools.partial(enter_kernel, core), [strip, strip], mid)
    far = swap(far, space, 1)
    pair = swap(pair, core, 0)
    we_t, wr_t = w_expand.T, w_reduce.T
    taps = jnp.transpose(kernel, (1, 2, 0))
    cot_t, forward, backward, we2, wr2, columns = call(
        prepare_kernel,
        [
            block,
            ((groups, DEEP, DEEP), BF16),
            ((groups, DEEP, DEEP), BF16),
            ((hidden_n, lift), BF16),
            ((hidden_n, channels), BF16),
            ((channels, LANES), F32),
        ],
        cotangent, taps, row(dw_bias), row(layer_norm_gain), row(layer_norm_bias),
        we_t, row(b_expand), wr_t, row(b_reduce), row(layer_scale),
        scratch=[((lift, hidden_n), BF16), ((8, DEEP), F32)],
    )
    ends = ((edge_height(tall), channels), BF16)
    image_t, first, second = call(
        functools.partial(gather_kernel, axes), [((tall, channels, width), BF16), ends, ends], mid, pair, far,
        after=[columns],
    )
    first, second = swap(first, filt, 0), swap(second, filt, 1)
    small_n = 64
    flat = ((hidden_n, LANES), F32)
    out_t, dconv, far_out, x, vectors, share, keep = call(
        functools.partial(main_kernel, axes),
        [
            block, block, strip, ((tall, channels, extent), BF16), ((8, LANES), F32),
            ((HALO * channels * (width // LANES) + hidden_n, LANES), BF16), flat,
        ],
        image_t, first, second, cot_t, forward, we_t, wr_t, we2, wr2, columns, row(layer_scale),
        scratch=[
            ((tall * deep, width), BF16),
            ((rows * channels, width), F32),
            ((channels, width), F32),
            ((lift, tokens), BF16),
            ((channels, tokens), BF16),
            ((hidden_n, tokens), BF16),
            ((hidden_n, tokens), BF16),
        ],
    )
    output = jnp.transpose(out_t, (1, 0, 2))
    edges, small = call(
        depthwise_gradient_kernel,
        [edge, ((small_n, LANES), F32)],
        x, dconv, vectors,
        scratch=[((deep, rows * extent), BF16), ((deep, rows * extent), BF16), ((8, DEEP), F32)],
    )
    share = swap(share, core, 0)
    far = swap(far_out, space, 1)
    low = panel + small_n
    if direct:
        send, kept = call(
            functools.partial(first_kernel, filt, panel),
            [((panel + low + high, LANES), BF16), ((panel + low, LANES), F32)],
            share, keep, small, edges,
            scratch=[flat],
        )
        first = crossed(send, filt, 1)
        send, kept = call(
            functools.partial(second_kernel, filt, panel),
            [((low + high, LANES), BF16), ((low, LANES), F32)],
            first, kept, edges,
        )
        got = crossed(send, filt, 3)
        own = ((low + 2 * high, LANES), BF16)
        (third,) = call(functools.partial(third_kernel, filt), [own], got, kept, first)
        got = crossed(third, chip, 2)
        (send,) = call(
            functools.partial(fourth_kernel, low), [((low + 4 * high, LANES), BF16)], got, third, after=[far]
        )
        got = crossed(send, chip, 1)
        (mine,) = call(
            functools.partial(fifth_kernel, axes, low), [((low + 4 * high, LANES), F32)], got, send, after=[output]
        )
    else:
        edges = edges_by_permutes(axes, edges).astype(F32)
        total, small = lax.psum((keep + share[-hidden_n:].astype(F32), small), (chip, filt))
        total = lax.dynamic_slice_in_dim(total, lax.axis_index(filt) * panel, panel, 0)
        mine = jnp.concatenate([total, small, edges], axis=0)
    other = swap(mine, core, 0)
    (back,) = call(
        functools.partial(back_kernel, core),
        [((rows * channels, width), F32)],
        dconv, share, far, cot_t, backward,
        scratch=[((tall * deep, width), BF16)],
        after=[mine],
    )
    factor = 1.0 / math.sqrt(tokens * chip_n * core_n * filt_n)
    line = ((1, channels), F32)
    matrix = ((panel, channels), F32)
    image_grad, kg, dwb, gain, lnb, ge, eb, gr, rb, sc = call(
        functools.partial(finish_kernel, factor, core),
        [
            ((channels, rows, width), BF16),
            ((SIDE, SIDE, channels), F32),
            line, line, line, matrix, ((1, panel), F32), matrix, line, line,
        ],
        mine, other, back, taps,
        scratch=[((2 * HALO, 16, LANES), F32), ((2 * HALO * rows, LANES), F32)],
    )
    flat = lambda v: v.reshape(-1)
    return (
        output, image_grad, jnp.transpose(kg, (2, 0, 1)),
        flat(dwb), flat(gain), flat(lnb), ge, flat(eb), gr, flat(rb), flat(sc),
    )


def solution(mesh):
    space, filt = mesh.devices.shape
    axes = ("chip", "core", "filt")
    pairs = Mesh(mesh.devices.reshape(space // 2, 2, filt), axes)
    pixels = P(None, ("chip", "core"), "filt")
    whole, shard = P(), P("filt")
    return jax.shard_map(
        functools.partial(shards, axes),
        mesh=pairs,
        in_specs=(pixels, pixels) + (whole,) * 9,
        out_specs=(pixels, pixels, whole, whole, whole, whole, shard, shard, shard, whole, whole),
        check_vma=False,
    )
```

```python
import functools
import math

import jax
import jax.numpy as jnp
from jax import lax
from jax.experimental import pallas as pl
from jax.experimental.pallas import tpu as pltpu
from jax.sharding import Mesh, PartitionSpec as P

F32 = jnp.float32
BF16 = jnp.bfloat16
SIDE = 7
HALO = 3
LANES = 128
GROUP = 32
DEEP = SIDE * GROUP
NT = (((1,), (1,)), ((), ()))
VECTORS = ("dwb", "gain", "lnb", "rb", "scale")


def iota(shape, dim):
    return lax.broadcasted_iota(jnp.int32, shape, dim)


def dot(a, b, dims=(((1,), (0,)), ((), ()))):
    return lax.dot_general(a, b, dims, preferred_element_type=F32)


def column(row):
    n = row.shape[1]
    eye = iota((n, n), 0) == iota((n, n), 1)
    return jnp.sum(jnp.where(eye, row, 0.0), axis=1, keepdims=True)


def widened(value):
    fill = jnp.zeros((value.shape[0], LANES - value.shape[1]), value.dtype)
    return jnp.concatenate([value, fill], axis=1)


def edge_height(rows):
    return -(-HALO * rows // 16) * 16


def pack_edges(rows):
    count = len(rows)
    width, high = rows[0].shape[1], edge_height(count)
    q, j = iota((2 * high, width), 0), iota((2 * high, width), 1)
    total = None
    for i, row in enumerate(rows):
        last = (q == count * (j - (width - HALO)) + i) & (j >= width - HALO)
        first = (q == high + count * j + i) & (j < HALO)
        pick = jnp.where(last | first, 1.0, 0.0).astype(BF16)
        part = dot(pick, row, NT)
        total = part if total is None else total + part
    return total.astype(BF16)


def halo_tile(edges_t, i, count):
    high = edges_t.shape[1] // 2
    q, l = iota((2 * high, LANES), 0), iota((2 * high, LANES), 1)
    left = (q == count * (l - (LANES - HALO)) + i) & (l >= LANES - HALO)
    right = (q == high + count * l + i) & (l < HALO)
    pick = jnp.where(left | right, 1.0, 0.0).astype(BF16)
    return dot(edges_t, pick).astype(BF16)


def group_diagonal():
    lane = iota((1, DEEP), 1)
    inner = lane
    for b in range(1, SIDE):
        inner = jnp.where(lane >= b * GROUP, lane - b * GROUP, inner)
    return inner == iota((GROUP, DEEP), 0)


def tap_matrices(taps_ref, line_ref, w_ref, flip):
    diagonal = group_diagonal()
    for g in range(w_ref.shape[0]):
        for b in range(SIDE):
            piece = taps_ref[:, SIDE - 1 - b if flip else b, g * GROUP : (g + 1) * GROUP]
            line_ref[0:SIDE, b * GROUP : (b + 1) * GROUP] = piece
        for m in range(SIDE):
            a = m if flip else SIDE - 1 - m
            w_ref[g, m * GROUP : (m + 1) * GROUP, :] = jnp.where(diagonal, line_ref[a : a + 1, :], 0.0).astype(BF16)


def shifted(x, amount):
    return x if amount % x.shape[1] == 0 else pltpu.roll(x, amount % x.shape[1], 1)


def spread(xs_ref, r, x):
    channels = x.shape[0]
    width = xs_ref.shape[1]
    for b in range(SIDE):
        moved = shifted(x, HALO - b)[:, :width]
        for g in range(channels // GROUP):
            at = r * SIDE * channels + g * DEEP + b * GROUP
            xs_ref[at : at + GROUP, :] = moved[g * GROUP : (g + 1) * GROUP]


def depthwise(w_ref, xs_ref, acc_ref, rows):
    groups = w_ref.shape[0]
    channels = groups * GROUP
    for g in range(groups):
        sums = [None] * rows
        for r in range(rows + 2 * HALO):
            i0, i1 = max(0, r - (SIDE - 1)), min(rows - 1, r)
            m0 = SIDE - 1 - r + i0
            at = r * SIDE * channels + g * DEEP
            part = dot(w_ref[g, m0 * GROUP : (m0 + i1 - i0 + 1) * GROUP, :], xs_ref[at : at + DEEP, :])
            for i in range(i0, i1 + 1):
                piece = part[(i - i0) * GROUP : (i - i0 + 1) * GROUP]
                sums[i] = piece if sums[i] is None else sums[i] + piece
        for i in range(rows):
            at = i * channels + g * GROUP
            acc_ref[at : at + GROUP, :] = sums[i]


def enter_kernel(core_axis, mid_ref, pair_ref, far_ref):
    rows = mid_ref.shape[0]
    core = lax.axis_index(core_axis)
    for k in range(HALO):
        pair_ref[k] = mid_ref[k + (rows - HALO) * (1 - core)]
        far_ref[k] = mid_ref[k + (rows - HALO) * core]


def gather_kernel(axes, mid_ref, pair_ref, far_ref, tall_ref, first_ref, second_ref):
    rows = mid_ref.shape[0]
    upper = lax.axis_index(axes[1]) == 0
    for k in range(HALO):
        pair, far = pair_ref[k], far_ref[k]
        tall_ref[k] = jnp.where(upper, far, pair)
        tall_ref[HALO + rows + k] = jnp.where(upper, pair, far)
    for i in range(rows):
        tall_ref[HALO + i] = mid_ref[i]
    edges = pack_edges([tall_ref[r] for r in range(rows + 2 * HALO)])
    high = edges.shape[0] // 2
    even = lax.rem(lax.axis_index(axes[2]), 2) == 0
    first_ref[...] = jnp.where(even, edges[:high], edges[high:])
    second_ref[...] = jnp.where(even, edges[high:], edges[:high])


def put_strip(ref, k, row):
    channels, width = row.shape
    parts = width // LANES
    for p in range(parts):
        ref[(k * parts + p) * channels : (k * parts + p + 1) * channels, :] = row[:, p * LANES : (p + 1) * LANES]


def get_strip(ref, k, channels, width):
    parts = width // LANES
    pieces = [ref[(k * parts + p) * channels : (k * parts + p + 1) * channels, :] for p in range(parts)]
    return jnp.concatenate(pieces, axis=1)


def prepare_kernel(
    cot_ref, taps_ref, dwb_ref, gain_ref, lnb_ref, we_ref, be_ref, wr_ref, br_ref, scale_ref,
    cot_t_ref, forward_ref, backward_ref, we2_ref, wr2_ref, columns_ref, lift_ref, line_ref,
):
    for i in range(cot_t_ref.shape[0]):
        cot_t_ref[i] = cot_ref[:, i, :]
    tap_matrices(taps_ref, line_ref, forward_ref, False)
    tap_matrices(taps_ref, line_ref, backward_ref, True)
    channels, hidden_n = we_ref.shape
    extra = lift_ref.shape[0] - channels
    lift_ref[0:channels, :] = we_ref[...]
    lift_ref[channels:, :] = jnp.where(iota((extra, hidden_n), 0) == 0, be_ref[...].astype(F32), 0.0).astype(BF16)
    we2_ref[...] = lift_ref[...].T
    wr2_ref[...] = wr_ref[...].T
    lane = iota(columns_ref.shape, 1)
    total = jnp.zeros(columns_ref.shape, F32)
    for k, ref in enumerate((dwb_ref, gain_ref, lnb_ref, br_ref, scale_ref)):
        total = jnp.where(lane == k, column(ref[...]), total)
    columns_ref[...] = total


def gelu_parts(v):
    z = jnp.abs(v)
    t = 1.0 / (1.0 + (0.3275911 / math.sqrt(2.0)) * z)
    e = jnp.exp2((-0.5 * math.log2(math.e)) * (v * v))
    half = 0.5
    poly = t * (
        half * 0.254829592
        + t * (half * -0.284496736 + t * (half * 1.421413741 + t * (half * -1.453152027 + t * (half * 1.061405429))))
    )
    tail = poly * e
    return jnp.where(v >= 0.0, 1.0 - tail, tail), (v * (1.0 / math.sqrt(2.0 * math.pi))) * e


def main_kernel(
    axes,
    tall_ref, first_ref, second_ref, cot_ref, w_ref, we_ref, wr_ref, we2_ref, wr2_ref, columns_ref, scale_ref,
    out_ref, dconv_ref, far_ref, x_ref, vectors_ref, share_ref, keep_ref,
    xs_ref, acc_ref, xhat_ref, nm_ref, db_ref, act_ref, dh_ref,
):
    rows, channels, width = cot_ref.shape
    hidden_n = we_ref.shape[1]
    core = lax.axis_index(axes[1])
    dwb, gain, lnb, br, scale = (columns_ref[:, k : k + 1] for k in range(5))
    lead = HALO * channels * (width // LANES)
    even = lax.rem(lax.axis_index(axes[2]), 2) == 0
    first, second = first_ref[...], second_ref[...]
    edges_t = jnp.concatenate([jnp.where(even, second, first), jnp.where(even, first, second)], axis=0).T
    for r in range(rows + 2 * HALO):
        x = jnp.concatenate([tall_ref[r], halo_tile(edges_t, r, rows + 2 * HALO)], axis=1)
        spread(xs_ref, r, x)
        x_ref[r] = x
    depthwise(w_ref, xs_ref, acc_ref, rows)
    extra = nm_ref.shape[0] - channels
    nm_ref[channels:, :] = jnp.where(iota((extra, rows * width), 0) == 0, 1.0, 0.0).astype(BF16)
    zero = jnp.zeros((channels, LANES), F32)
    sums = {k: zero for k in VECTORS}

    def add(name, value):
        for k in range(0, width, LANES):
            sums[name] = sums[name] + value[:, k : k + LANES]

    chunk = 128
    for i in range(rows):
        cols = slice(i * width, (i + 1) * width)
        conv = acc_ref[i * channels : (i + 1) * channels, :] + dwb
        conv = conv - jnp.mean(conv, axis=0, keepdims=True)
        inv = lax.rsqrt(jnp.mean(conv * conv, axis=0, keepdims=True) + 1e-6)
        xhat = conv * inv
        xhat_ref[...] = xhat
        nm_ref[0:channels, cols] = (xhat * gain + lnb).astype(BF16)
        cot = cot_ref[i].astype(F32)
        add("rb", cot)
        db_ref[:, cols] = (cot * scale).astype(BF16)
        for h0 in range(0, hidden_n, chunk):
            hs = slice(h0, h0 + chunk)
            hidden = dot(we2_ref[hs, :], nm_ref[:, cols])
            back = dot(wr2_ref[hs, :], db_ref[:, cols])
            phi, bump = gelu_parts(hidden)
            act_ref[hs, cols] = (hidden * phi).astype(BF16)
            dh_ref[hs, cols] = (back * (phi + bump)).astype(BF16)
        branch = dot(wr_ref[...], act_ref[:, cols]) + br
        out_ref[i] = (tall_ref[HALO + i].astype(F32) + scale * branch).astype(BF16)
        add("scale", cot * branch)
        d_normed = dot(we_ref[...], dh_ref[:, cols])
        xhat = xhat_ref[...]
        add("lnb", d_normed)
        add("gain", d_normed * xhat)
        d_xhat = d_normed * gain
        m1 = jnp.mean(d_xhat, axis=0, keepdims=True)
        m2 = jnp.mean(d_xhat * xhat, axis=0, keepdims=True)
        dconv = (inv * (d_xhat - m1 - xhat * m2)).astype(BF16)
        add("dwb", dconv.astype(F32))
        dconv_ref[i] = dconv
    for k in range(HALO):
        put_strip(share_ref, k, dconv_ref[k + (rows - HALO) * (1 - core)])
        far_ref[k] = dconv_ref[k + (rows - HALO) * core]
    g_reduce = widened(dot(act_ref[...], db_ref[...], NT))
    g_expand = widened(dot(dh_ref[...], nm_ref[...], NT))
    keep_ref[...] = jnp.where(core == 0, g_reduce, g_expand)
    share_ref[lead:, :] = jnp.where(core == 0, g_expand, g_reduce).astype(BF16)
    vectors_ref[...] = jnp.zeros_like(vectors_ref)
    for b, name in enumerate(VECTORS):
        total = jnp.sum(sums[name].T, axis=0, keepdims=True)
        vectors_ref[b : b + 1, 0:channels] = total * scale_ref[...] if name == "rb" else total


def depthwise_gradient_kernel(x_ref, dconv_ref, vectors_ref, edges_ref, small_ref, wide_ref, dcs_ref, line_ref):
    rows, channels, width = dconv_ref.shape
    groups = channels // GROUP
    extent = width + LANES
    edges_ref[...] = widened(pack_edges([dconv_ref[i] for i in range(rows)]))
    for i in range(rows):
        padded = jnp.concatenate([dconv_ref[i], jnp.zeros((channels, LANES), BF16)], axis=1)
        columns = slice(i * extent, (i + 1) * extent)
        for b in range(SIDE):
            moved = shifted(padded, b - HALO)
            for g in range(groups):
                at = g * DEEP + b * GROUP
                dcs_ref[at : at + GROUP, columns] = moved[g * GROUP : (g + 1) * GROUP]
        for a in range(SIDE):
            for g in range(groups):
                at = g * DEEP + a * GROUP
                wide_ref[at : at + GROUP, columns] = x_ref[i + a, g * GROUP : (g + 1) * GROUP, :]
    small_ref[...] = jnp.zeros_like(small_ref)
    diagonal = group_diagonal()
    for g in range(groups):
        taps = dot(wide_ref[g * DEEP : (g + 1) * DEEP, :], dcs_ref[g * DEEP : (g + 1) * DEEP, :], NT)
        for a in range(SIDE):
            part = jnp.where(diagonal, taps[a * GROUP : (a + 1) * GROUP, :], 0.0)
            line_ref[a : a + 1, :] = jnp.sum(part, axis=0, keepdims=True)
        for b in range(SIDE):
            small_ref[b * 8 : b * 8 + SIDE, g * GROUP : (g + 1) * GROUP] = line_ref[0:SIDE, b * GROUP : (b + 1) * GROUP]
    for b in range(len(VECTORS)):
        small_ref[b * 8 + SIDE : b * 8 + 8, :] = vectors_ref[b : b + 1, :]


def columns_kernel(axis, panel, share_ref, keep_ref, small_ref, edges_ref, *refs):
    *send_refs, kept_ref, total_ref = refs
    f = lax.axis_index(axis)
    count = total_ref.shape[0]
    total_ref[...] = keep_ref[...] + share_ref[share_ref.shape[0] - count :, :].astype(F32)
    part = lambda k: total_ref[pl.ds(pl.multiple_of(k * panel, 8), panel), :]
    tail = small_ref[...].astype(BF16)
    small = tail.shape[0]
    high = edges_ref.shape[0] // 2
    for mate, send_ref in zip(mates(f), send_refs):
        send_ref[0:panel, :] = part(mate).astype(BF16)
        send_ref[panel : panel + small, :] = tail
        send_ref[panel + small :, :] = jnp.where(mate > f, edges_ref[:high, :], edges_ref[high:, :])
    kept_ref[0:panel, :] = part(f)
    kept_ref[panel:, :] = tail.astype(F32)


def mates(index):
    low = 1 - 2 * lax.rem(index, 2)
    high = jnp.where(index < 2, 2, -2)
    return index + low, index + high, index + low + high


def four_sums(mine, parts):
    first, second, third = (part.astype(F32) for part in parts)
    return (mine + first) + (second + third)


def chips_kernel(axis, kept_ref, first_ref, second_ref, third_ref, send_ref, plain_ref):
    f = lax.axis_index(axis)
    even = lax.rem(f, 2) == 0
    count = kept_ref.shape[0]
    total = four_sums(kept_ref[...], [ref[0:count, :] for ref in (first_ref, second_ref, third_ref)]).astype(BF16)
    near, far = first_ref[count:, :], third_ref[count:, :]
    far = jnp.where((f == 0) | (f == lax.axis_size(axis) - 1), jnp.zeros_like(far), far)
    edges = [jnp.where(even, far, near), jnp.where(even, near, far)]
    plain_ref[...] = total
    send_ref[...] = jnp.concatenate([total, *edges], axis=0)


def total_kernel(axes, mine_ref, first_ref, second_ref, third_ref, total_ref):
    q, core = lax.axis_index(axes[0]), lax.axis_index(axes[1])
    count = second_ref.shape[0]
    wide = mine_ref.shape[0] - count
    mine = mine_ref[0:count, :].astype(F32)
    total_ref[0:count, :] = four_sums(mine, [ref[0:count, :] for ref in (first_ref, second_ref, third_ref)])
    total_ref[count : count + wide, :] = mine_ref[count:, :].astype(F32)
    other = q + 1 - 2 * core
    beside = lax.rem(q + core, 2) == 0
    value = jnp.where(beside, first_ref[count:, :], third_ref[count:, :]).astype(F32)
    total_ref[count + wide :, :] = jnp.where((other >= 0) & (other < lax.axis_size(axes[0])), value, 0.0)


def back_kernel(core_axis, mid_ref, share_ref, far_ref, cot_ref, w_ref, acc_ref, xs_ref):
    rows, channels, width = cot_ref.shape
    upper = lax.axis_index(core_axis) == 0
    nothing = jnp.zeros((channels, LANES), BF16)
    put = lambda r, x: spread(xs_ref, r, jnp.concatenate([x, nothing], axis=1))
    for k in range(HALO):
        pair, far = get_strip(share_ref, k, channels, width), far_ref[k]
        put(k, jnp.where(upper, far, pair))
        put(HALO + rows + k, jnp.where(upper, pair, far))
    for i in range(rows):
        put(HALO + i, mid_ref[i])
    depthwise(w_ref, xs_ref, acc_ref, rows)
    for i in range(rows):
        acc_ref[i * channels : (i + 1) * channels, :] += cot_ref[i].astype(F32)


def finish_kernel(
    factor, core_axis, mine_ref, other_ref, acc_ref, taps_ref,
    back_ref, kg_ref, dwb_ref, gain_ref, lnb_ref, ge_ref, eb_ref, gr_ref, rb_ref, sc_ref, ends_ref, side_ref,
):
    channels = kg_ref.shape[2]
    panel = gr_ref.shape[0]
    core = lax.axis_index(core_axis)
    rows, width = back_ref.shape[1:]
    high = edge_height(rows)
    low = mine_ref.shape[0] - 4 * high
    own, near, beyond = mine_ref[low : low + 2 * high, :], other_ref[low : low + 2 * high, :], other_ref[low + 2 * high :, :]
    above, below = jnp.where(core == 0, beyond, near), jnp.where(core == 0, near, beyond)
    for side in range(2):
        for k in range(HALO):
            at = side * high + k * rows
            ends_ref[side * HALO + k, 0:HALO, :] = above[at + rows - HALO : at + rows]
            ends_ref[side * HALO + k, HALO : HALO + rows, :] = own[at : at + rows]
            ends_ref[side * HALO + k, HALO + rows : 2 * HALO + rows, :] = below[at : at + HALO]
    side_ref[...] = jnp.zeros_like(side_ref)
    for side in range(2):
        for j in range(HALO):
            total = None
            for k in range(HALO):
                b = k + side * (SIDE - 1) - j
                if not 0 <= b < SIDE:
                    continue
                for a in range(SIDE):
                    tap = taps_ref[SIDE - 1 - a, SIDE - 1 - b : SIDE - b, :]
                    part = tap * ends_ref[side * HALO + k, a : a + rows, 0:channels]
                    total = part if total is None else total + part
            at = (side * HALO + j) * rows
            side_ref[at : at + rows, 0:channels] = total
    side = side_ref[...]
    upper = side.astype(BF16)
    lower = (side - upper.astype(F32)).astype(BF16)
    side_t = jnp.concatenate([upper, lower], axis=0).T
    count = side_ref.shape[0]
    q, l = iota((2 * count, LANES), 0), iota((2 * count, LANES), 1)
    q = jnp.where(q >= count, q - count, q)
    for i in range(rows):
        first = (q == l * rows + i) & (l < HALO)
        last = (q == (HALO + l - (LANES - HALO)) * rows + i) & (l >= LANES - HALO)
        extra = [dot(side_t, jnp.where(at, 1.0, 0.0).astype(BF16))[0:channels] for at in (first, last)]
        value = acc_ref[i * channels : (i + 1) * channels, :]
        tiles = [value[:, k : k + LANES] for k in range(0, width, LANES)]
        tiles[0] = tiles[0] + extra[0]
        tiles[-1] = tiles[-1] + extra[1]
        back_ref[:, i, :] = jnp.concatenate(tiles, axis=1).astype(BF16)
    mine, other = mine_ref[0:low, :] * factor, other_ref[0:low, :] * factor
    low, high = jnp.where(core == 0, mine, other), jnp.where(core == 0, other, mine)
    small = mine[panel:] + other[panel:]
    for b in range(SIDE):
        kg_ref[:, b, :] = small[b * 8 : b * 8 + SIDE, 0:channels]
    for b, ref in enumerate((dwb_ref, gain_ref, lnb_ref, rb_ref, sc_ref)):
        ref[...] = small[b * 8 + SIDE : b * 8 + 8, 0:channels]
    gr_ref[...] = low[0:panel, 0:channels]
    ge_ref[...] = high[0:panel, 0:channels]
    eye = iota((panel, panel), 0) == iota((panel, panel), 1)
    eb_ref[...] = jnp.sum(jnp.where(eye, high[0:panel, channels : channels + 1], 0.0), axis=0, keepdims=True)


def call(kernel, outs, *args, scratch=(), after=(), flops=0):
    size = sum(math.prod(a.shape) * a.dtype.itemsize for a in args)
    size += sum(math.prod(s) * jnp.dtype(d).itemsize for s, d in outs)
    count = len(args)

    def body(*refs):
        kernel(*refs[:count], *refs[count + len(after) :])

    in_vmem = pl.BlockSpec(memory_space=pltpu.VMEM)
    anywhere = pl.BlockSpec(memory_space=pl.ANY)
    return pl.pallas_call(
        body,
        out_shape=[jax.ShapeDtypeStruct(s, d) for s, d in outs],
        in_specs=[in_vmem] * count + [anywhere] * len(after),
        out_specs=[in_vmem] * len(outs),
        scratch_shapes=[pltpu.VMEM(s, d) for s, d in scratch],
        compiler_params=pltpu.CompilerParams(vmem_limit_bytes=40 * 2**20),
        cost_estimate=pl.CostEstimate(flops=flops, bytes_accessed=size, transcendentals=0),
    )(*args, *after)


def swap(x, axis, parity):
    size = lax.axis_size(axis)
    pairs = [(i, i + 1) for i in range(parity, size - 1, 2)]
    return lax.ppermute(x, axis, pairs + [(j, i) for i, j in pairs])


def crossed(x, axis, bits):
    return lax.ppermute(x, axis, [(i, i ^ bits) for i in range(lax.axis_size(axis))])


def edges_by_permutes(axes, edges):
    chip, core, filt = axes
    count = lax.axis_size(filt)
    right = [(i, i + 1) for i in range(count - 1)]
    left = [(j, i) for i, j in right]
    high = edges.shape[0] // 2
    own = jnp.concatenate([lax.ppermute(edges[:high], filt, right), lax.ppermute(edges[high:], filt, left)], axis=0)
    return jnp.concatenate([own, swap(own, (chip, core), 1)], axis=0)


def shards(
    axes, image, cotangent, kernel, dw_bias, layer_norm_gain, layer_norm_bias,
    w_expand, b_expand, w_reduce, b_reduce, layer_scale,
):
    chip, core, filt = axes
    chip_n, core_n, filt_n = (lax.axis_size(a) for a in axes)
    channels, rows, width = image.shape
    hidden_n = w_expand.shape[0]
    groups = channels // GROUP
    panel = hidden_n // filt_n
    tall = rows + 2 * HALO
    deep = SIDE * channels
    extent = width + LANES
    tokens = rows * width
    lift = channels + 16
    direct = chip_n == 4 and filt_n == 4
    strip = ((HALO, channels, width), BF16)
    block = ((rows, channels, width), BF16)
    high = edge_height(rows)
    edge = ((2 * high, LANES), BF16)
    row = lambda v: v.reshape(1, -1)

    space = (chip, core)
    lead = HALO * channels * (width // LANES)
    mid = jnp.transpose(image, (1, 0, 2))
    pair, far = call(functools.partial(enter_kernel, core), [strip, strip], mid)
    far = swap(far, space, 1)
    pair = swap(pair, core, 0)
    we_t, wr_t = w_expand.T, w_reduce.T
    taps = jnp.transpose(kernel, (1, 2, 0))
    cot_t, forward, backward, we2, wr2, columns = call(
        prepare_kernel,
        [
            block,
            ((groups, DEEP, DEEP), BF16),
            ((groups, DEEP, DEEP), BF16),
            ((hidden_n, lift), BF16),
            ((hidden_n, channels), BF16),
            ((channels, LANES), F32),
        ],
        cotangent, taps, row(dw_bias), row(layer_norm_gain), row(layer_norm_bias),
        we_t, row(b_expand), wr_t, row(b_reduce), row(layer_scale),
        scratch=[((lift, hidden_n), BF16), ((8, DEEP), F32)],
    )
    ends = ((edge_height(tall), channels), BF16)
    image_t, first, second = call(
        functools.partial(gather_kernel, axes), [((tall, channels, width), BF16), ends, ends], mid, pair, far,
        after=[columns],
    )
    first, second = swap(first, filt, 0), swap(second, filt, 1)
    small_n = 64
    flat = ((hidden_n, LANES), F32)
    out_t, dconv, far_out, x, vectors, share, keep = call(
        functools.partial(main_kernel, axes),
        [
            block, block, strip, ((tall, channels, extent), BF16), ((8, LANES), F32),
            ((HALO * channels * (width // LANES) + hidden_n, LANES), BF16), flat,
        ],
        image_t, first, second, cot_t, forward, we_t, wr_t, we2, wr2, columns, row(layer_scale),
        scratch=[
            ((tall * deep, width), BF16),
            ((rows * channels, width), F32),
            ((channels, width), F32),
            ((lift, tokens), BF16),
            ((channels, tokens), BF16),
            ((hidden_n, tokens), BF16),
            ((hidden_n, tokens), BF16),
        ],
    )
    output = jnp.transpose(out_t, (1, 0, 2))
    edges, small = call(
        depthwise_gradient_kernel,
        [edge, ((small_n, LANES), F32)],
        x, dconv, vectors,
        scratch=[((deep, rows * extent), BF16), ((deep, rows * extent), BF16), ((8, DEEP), F32)],
    )
    share = swap(share, core, 0)
    far = swap(far_out, space, 1) if direct else None
    low = panel + small_n
    if direct:
        sums = ((low, LANES), BF16)
        *sends, kept = call(
            functools.partial(columns_kernel, filt, panel),
            [((low + high, LANES), BF16)] * 3 + [((low, LANES), F32)],
            share, keep, small, edges,
            scratch=[flat],
        )
        third, second, first = (crossed(sends[k - 1], filt, k) for k in (3, 2, 1))
        send, plain = call(
            functools.partial(chips_kernel, filt), [((low + 2 * high, LANES), BF16), sums], kept, first, second, third,
            flops=4 * 10**9,
        )
        third, second, first = (crossed(plain if k == 2 else send, chip, k) for k in (3, 2, 1))
        (mine,) = call(
            functools.partial(total_kernel, axes),
            [((low + 4 * high, LANES), F32)],
            send, first, second, third,
            after=[output, far],
        )
    else:
        far = swap(far_out, space, 1)
        edges = edges_by_permutes(axes, edges).astype(F32)
        total, small = lax.psum((keep + share[-hidden_n:].astype(F32), small), (chip, filt))
        total = lax.dynamic_slice_in_dim(total, lax.axis_index(filt) * panel, panel, 0)
        mine = jnp.concatenate([total, small, edges], axis=0)
    other = swap(mine, core, 0)
    (back,) = call(
        functools.partial(back_kernel, core),
        [((rows * channels, width), F32)],
        dconv, share, far, cot_t, backward,
        scratch=[((tall * deep, width), BF16)],
        after=[mine],
    )
    factor = 1.0 / math.sqrt(tokens * chip_n * core_n * filt_n)
    line = ((1, channels), F32)
    matrix = ((panel, channels), F32)
    image_grad, kg, dwb, gain, lnb, ge, eb, gr, rb, sc = call(
        functools.partial(finish_kernel, factor, core),
        [
            ((channels, rows, width), BF16),
            ((SIDE, SIDE, channels), F32),
            line, line, line, matrix, ((1, panel), F32), matrix, line, line,
        ],
        mine, other, back, taps,
        scratch=[((2 * HALO, 16, LANES), F32), ((2 * HALO * rows, LANES), F32)],
    )
    flat = lambda v: v.reshape(-1)
    return (
        output, image_grad, jnp.transpose(kg, (2, 0, 1)),
        flat(dwb), flat(gain), flat(lnb), ge, flat(eb), gr, flat(rb), flat(sc),
    )


def solution(mesh):
    space, filt = mesh.devices.shape
    axes = ("chip", "core", "filt")
    pairs = Mesh(mesh.devices.reshape(space // 2, 2, filt), axes)
    pixels = P(None, ("chip", "core"), "filt")
    whole, shard = P(), P("filt")
    return jax.shard_map(
        functools.partial(shards, axes),
        mesh=pairs,
        in_specs=(pixels, pixels) + (whole,) * 9,
        out_specs=(pixels, pixels, whole, whole, whole, whole, shard, shard, shard, whole, whole),
        check_vma=False,
    )
```

```python
import functools
import math

import jax
import jax.numpy as jnp
from jax import lax
from jax.experimental import pallas as pl
from jax.experimental.pallas import tpu as pltpu
from jax.sharding import Mesh, PartitionSpec as P

F32 = jnp.float32
BF16 = jnp.bfloat16
SIDE = 7
HALO = 3
LANES = 128
GROUP = 32
DEEP = SIDE * GROUP
NT = (((1,), (1,)), ((), ()))
VECTORS = ("dwb", "gain", "lnb", "rb", "scale")


def iota(shape, dim):
    return lax.broadcasted_iota(jnp.int32, shape, dim)


def dot(a, b, dims=(((1,), (0,)), ((), ()))):
    return lax.dot_general(a, b, dims, preferred_element_type=F32)


def column(row):
    n = row.shape[1]
    eye = iota((n, n), 0) == iota((n, n), 1)
    return jnp.sum(jnp.where(eye, row, 0.0), axis=1, keepdims=True)


def widened(value):
    fill = jnp.zeros((value.shape[0], LANES - value.shape[1]), value.dtype)
    return jnp.concatenate([value, fill], axis=1)


def edge_height(rows):
    return -(-HALO * rows // 16) * 16


def pack_edges(rows):
    count = len(rows)
    width, high = rows[0].shape[1], edge_height(count)
    q, j = iota((2 * high, width), 0), iota((2 * high, width), 1)
    total = None
    for i, row in enumerate(rows):
        last = (q == count * (j - (width - HALO)) + i) & (j >= width - HALO)
        first = (q == high + count * j + i) & (j < HALO)
        pick = jnp.where(last | first, 1.0, 0.0).astype(BF16)
        part = dot(pick, row, NT)
        total = part if total is None else total + part
    return total.astype(BF16)


def halo_tile(edges_t, i, count):
    high = edges_t.shape[1] // 2
    q, l = iota((2 * high, LANES), 0), iota((2 * high, LANES), 1)
    left = (q == count * (l - (LANES - HALO)) + i) & (l >= LANES - HALO)
    right = (q == high + count * l + i) & (l < HALO)
    pick = jnp.where(left | right, 1.0, 0.0).astype(BF16)
    return dot(edges_t, pick).astype(BF16)


def group_diagonal():
    lane = iota((1, DEEP), 1)
    inner = lane
    for b in range(1, SIDE):
        inner = jnp.where(lane >= b * GROUP, lane - b * GROUP, inner)
    return inner == iota((GROUP, DEEP), 0)


def tap_matrices(taps_ref, line_ref, w_ref, flip):
    diagonal = group_diagonal()
    for g in range(w_ref.shape[0]):
        for b in range(SIDE):
            piece = taps_ref[:, SIDE - 1 - b if flip else b, g * GROUP : (g + 1) * GROUP]
            line_ref[0:SIDE, b * GROUP : (b + 1) * GROUP] = piece
        for m in range(SIDE):
            a = m if flip else SIDE - 1 - m
            w_ref[g, m * GROUP : (m + 1) * GROUP, :] = jnp.where(diagonal, line_ref[a : a + 1, :], 0.0).astype(BF16)


def shifted(x, amount):
    return x if amount % x.shape[1] == 0 else pltpu.roll(x, amount % x.shape[1], 1)


def spread(xs_ref, r, x):
    channels = x.shape[0]
    width = xs_ref.shape[1]
    for b in range(SIDE):
        moved = shifted(x, HALO - b)[:, :width]
        for g in range(channels // GROUP):
            at = r * SIDE * channels + g * DEEP + b * GROUP
            xs_ref[at : at + GROUP, :] = moved[g * GROUP : (g + 1) * GROUP]


def depthwise(w_ref, xs_ref, acc_ref, rows, taken, before_ref=None):
    groups = w_ref.shape[0]
    channels = groups * GROUP
    for g in range(groups):
        at = [slice(i * channels + g * GROUP, i * channels + (g + 1) * GROUP) for i in range(rows)]
        sums = [None if before_ref is None else before_ref[at[i], :] for i in range(rows)]
        for k, r in enumerate(taken):
            i0, i1 = max(0, r - (SIDE - 1)), min(rows - 1, r)
            m0 = SIDE - 1 - r + i0
            low = k * SIDE * channels + g * DEEP
            part = dot(w_ref[g, m0 * GROUP : (m0 + i1 - i0 + 1) * GROUP, :], xs_ref[low : low + DEEP, :])
            for i in range(i0, i1 + 1):
                piece = part[(i - i0) * GROUP : (i - i0 + 1) * GROUP]
                sums[i] = piece if sums[i] is None else sums[i] + piece
        for i in range(rows):
            acc_ref[at[i], :] = sums[i]


def own_rows_kernel(mid_ref, own_ref, w_ref, acc_ref, x_ref, xs_ref):
    rows, channels, _ = mid_ref.shape
    edges_t = own_ref[:, 0:channels].T
    for i in range(rows):
        x = jnp.concatenate([mid_ref[i], halo_tile(edges_t, i, rows)], axis=1)
        x_ref[i] = x
        spread(xs_ref, i, x)
    depthwise(w_ref, xs_ref, acc_ref, rows, range(HALO, HALO + rows))


def edges_kernel(axis, mid_ref, first_ref, second_ref):
    edges = pack_edges([mid_ref[i] for i in range(mid_ref.shape[0])])
    high = edges.shape[0] // 2
    even = lax.rem(lax.axis_index(axis), 2) == 0
    first_ref[...] = jnp.where(even, edges[:high], edges[high:])
    second_ref[...] = jnp.where(even, edges[high:], edges[:high])


def far_kernel(axes, mid_ref, first_ref, second_ref, own_ref, far_ref):
    even = lax.rem(lax.axis_index(axes[2]), 2) == 0
    first, second = first_ref[...], second_ref[...]
    edges = jnp.concatenate([jnp.where(even, second, first), jnp.where(even, first, second)], axis=0)
    own_ref[...] = widened(edges)
    put_strips(mid_ref, own_ref, far_ref, lax.axis_index(axes[1]))


def pair_kernel(core_axis, mid_ref, own_ref, pair_ref):
    put_strips(mid_ref, own_ref, pair_ref, 1 - lax.axis_index(core_axis))


def put_strips(mid_ref, edges_ref, to_ref, last):
    for k in range(HALO):
        put_strip(to_ref, k, mid_ref[k + (mid_ref.shape[0] - HALO) * last])
    to_ref[to_ref.shape[0] - edges_ref.shape[0] :, :] = edges_ref[...]


def put_strip(ref, k, row):
    channels, width = row.shape
    parts = width // LANES
    for p in range(parts):
        ref[(k * parts + p) * channels : (k * parts + p + 1) * channels, :] = row[:, p * LANES : (p + 1) * LANES]


def get_strip(ref, k, channels, width):
    parts = width // LANES
    pieces = [ref[(k * parts + p) * channels : (k * parts + p + 1) * channels, :] for p in range(parts)]
    return jnp.concatenate(pieces, axis=1)


def prepare_kernel(
    cot_ref, taps_ref, dwb_ref, gain_ref, lnb_ref, we_ref, be_ref, wr_ref, br_ref, scale_ref,
    cot_t_ref, forward_ref, backward_ref, we2_ref, wr2_ref, columns_ref, lift_ref, line_ref,
):
    for i in range(cot_t_ref.shape[0]):
        cot_t_ref[i] = cot_ref[:, i, :]
    tap_matrices(taps_ref, line_ref, forward_ref, False)
    tap_matrices(taps_ref, line_ref, backward_ref, True)
    channels, hidden_n = we_ref.shape
    extra = lift_ref.shape[0] - channels
    lift_ref[0:channels, :] = we_ref[...]
    lift_ref[channels:, :] = jnp.where(iota((extra, hidden_n), 0) == 0, be_ref[...].astype(F32), 0.0).astype(BF16)
    we2_ref[...] = lift_ref[...].T
    wr2_ref[...] = wr_ref[...].T
    lane = iota(columns_ref.shape, 1)
    total = jnp.zeros(columns_ref.shape, F32)
    for k, ref in enumerate((dwb_ref, gain_ref, lnb_ref, br_ref, scale_ref)):
        total = jnp.where(lane == k, column(ref[...]), total)
    columns_ref[...] = total


def gelu_parts(v):
    z = jnp.abs(v)
    t = 1.0 / (1.0 + (0.3275911 / math.sqrt(2.0)) * z)
    e = jnp.exp2((-0.5 * math.log2(math.e)) * (v * v))
    half = 0.5
    poly = t * (
        half * 0.254829592
        + t * (half * -0.284496736 + t * (half * 1.421413741 + t * (half * -1.453152027 + t * (half * 1.061405429))))
    )
    tail = poly * e
    return jnp.where(v >= 0.0, 1.0 - tail, tail), (v * (1.0 / math.sqrt(2.0 * math.pi))) * e


def main_kernel(
    axes,
    mid_ref, pair_ref, beyond_ref, own_ref, before_ref, cot_ref, w_ref, we_ref, wr_ref, we2_ref, wr2_ref, columns_ref, scale_ref,
    out_ref, dconv_ref, far_ref, x_ref, vectors_ref, share_ref, keep_ref,
    xs_ref, acc_ref, xhat_ref, nm_ref, db_ref, act_ref, dh_ref,
):
    rows, channels, width = cot_ref.shape
    hidden_n = we_ref.shape[1]
    core = lax.axis_index(axes[1])
    dwb, gain, lnb, br, scale = (columns_ref[:, k : k + 1] for k in range(5))
    lead = HALO * channels * (width // LANES)
    upper = core == 0
    high = own_ref.shape[0]
    near, beyond = (ref[ref.shape[0] - high :, 0:channels].T for ref in (pair_ref, beyond_ref))
    above, below = jnp.where(upper, beyond, near), jnp.where(upper, near, beyond)
    for k in range(HALO):
        pair, far = (get_strip(ref, k, channels, width) for ref in (pair_ref, beyond_ref))
        up, down = jnp.where(upper, far, pair), jnp.where(upper, pair, far)
        up = jnp.concatenate([up, halo_tile(above, rows - HALO + k, rows)], axis=1)
        down = jnp.concatenate([down, halo_tile(below, k, rows)], axis=1)
        x_ref[k] = up
        x_ref[HALO + k] = down
        spread(xs_ref, k, up)
        spread(xs_ref, HALO + k, down)
    taken = [*range(HALO), *range(HALO + rows, rows + 2 * HALO)]
    depthwise(w_ref, xs_ref, acc_ref, rows, taken, before_ref)
    extra = nm_ref.shape[0] - channels
    nm_ref[channels:, :] = jnp.where(iota((extra, rows * width), 0) == 0, 1.0, 0.0).astype(BF16)
    zero = jnp.zeros((channels, LANES), F32)
    sums = {k: zero for k in VECTORS}

    def add(name, value):
        for k in range(0, width, LANES):
            sums[name] = sums[name] + value[:, k : k + LANES]

    chunk = 128
    for i in range(rows):
        cols = slice(i * width, (i + 1) * width)
        conv = acc_ref[i * channels : (i + 1) * channels, :] + dwb
        conv = conv - jnp.mean(conv, axis=0, keepdims=True)
        inv = lax.rsqrt(jnp.mean(conv * conv, axis=0, keepdims=True) + 1e-6)
        xhat = conv * inv
        xhat_ref[...] = xhat
        nm_ref[0:channels, cols] = (xhat * gain + lnb).astype(BF16)
        cot = cot_ref[i].astype(F32)
        add("rb", cot)
        db_ref[:, cols] = (cot * scale).astype(BF16)
        for h0 in range(0, hidden_n, chunk):
            hs = slice(h0, h0 + chunk)
            hidden = dot(we2_ref[hs, :], nm_ref[:, cols])
            back = dot(wr2_ref[hs, :], db_ref[:, cols])
            phi, bump = gelu_parts(hidden)
            act_ref[hs, cols] = (hidden * phi).astype(BF16)
            dh_ref[hs, cols] = (back * (phi + bump)).astype(BF16)
        branch = dot(wr_ref[...], act_ref[:, cols]) + br
        out_ref[i] = (mid_ref[i].astype(F32) + scale * branch).astype(BF16)
        add("scale", cot * branch)
        d_normed = dot(we_ref[...], dh_ref[:, cols])
        xhat = xhat_ref[...]
        add("lnb", d_normed)
        add("gain", d_normed * xhat)
        d_xhat = d_normed * gain
        m1 = jnp.mean(d_xhat, axis=0, keepdims=True)
        m2 = jnp.mean(d_xhat * xhat, axis=0, keepdims=True)
        dconv = (inv * (d_xhat - m1 - xhat * m2)).astype(BF16)
        add("dwb", dconv.astype(F32))
        dconv_ref[i] = dconv
    for k in range(HALO):
        put_strip(share_ref, k, dconv_ref[k + (rows - HALO) * (1 - core)])
        far_ref[k] = dconv_ref[k + (rows - HALO) * core]
    g_reduce = widened(dot(act_ref[...], db_ref[...], NT))
    g_expand = widened(dot(dh_ref[...], nm_ref[...], NT))
    keep_ref[...] = jnp.where(core == 0, g_reduce, g_expand)
    share_ref[lead:, :] = jnp.where(core == 0, g_expand, g_reduce).astype(BF16)
    vectors_ref[...] = jnp.zeros_like(vectors_ref)
    for b, name in enumerate(VECTORS):
        total = jnp.sum(sums[name].T, axis=0, keepdims=True)
        vectors_ref[b : b + 1, 0:channels] = total * scale_ref[...] if name == "rb" else total


def depthwise_gradient_kernel(x_ref, own_x_ref, dconv_ref, vectors_ref, edges_ref, small_ref, wide_ref, dcs_ref, line_ref):
    rows, channels, width = dconv_ref.shape
    groups = channels // GROUP
    extent = width + LANES
    edges_ref[...] = widened(pack_edges([dconv_ref[i] for i in range(rows)]))
    for i in range(rows):
        padded = jnp.concatenate([dconv_ref[i], jnp.zeros((channels, LANES), BF16)], axis=1)
        columns = slice(i * extent, (i + 1) * extent)
        for b in range(SIDE):
            moved = shifted(padded, b - HALO)
            for g in range(groups):
                at = g * DEEP + b * GROUP
                dcs_ref[at : at + GROUP, columns] = moved[g * GROUP : (g + 1) * GROUP]
        for a in range(SIDE):
            r = i + a
            if HALO <= r < HALO + rows:
                x = own_x_ref[r - HALO]
            else:
                x = x_ref[r if r < HALO else r - rows]
            for g in range(groups):
                at = g * DEEP + a * GROUP
                wide_ref[at : at + GROUP, columns] = x[g * GROUP : (g + 1) * GROUP, :]
    small_ref[...] = jnp.zeros_like(small_ref)
    diagonal = group_diagonal()
    for g in range(groups):
        taps = dot(wide_ref[g * DEEP : (g + 1) * DEEP, :], dcs_ref[g * DEEP : (g + 1) * DEEP, :], NT)
        for a in range(SIDE):
            part = jnp.where(diagonal, taps[a * GROUP : (a + 1) * GROUP, :], 0.0)
            line_ref[a : a + 1, :] = jnp.sum(part, axis=0, keepdims=True)
        for b in range(SIDE):
            small_ref[b * 8 : b * 8 + SIDE, g * GROUP : (g + 1) * GROUP] = line_ref[0:SIDE, b * GROUP : (b + 1) * GROUP]
    for b in range(len(VECTORS)):
        small_ref[b * 8 + SIDE : b * 8 + 8, :] = vectors_ref[b : b + 1, :]


def columns_kernel(axis, panel, share_ref, keep_ref, small_ref, edges_ref, *refs):
    *send_refs, kept_ref, total_ref = refs
    f = lax.axis_index(axis)
    count = total_ref.shape[0]
    total_ref[...] = keep_ref[...] + share_ref[share_ref.shape[0] - count :, :].astype(F32)
    part = lambda k: total_ref[pl.ds(pl.multiple_of(k * panel, 8), panel), :]
    tail = small_ref[...].astype(BF16)
    small = tail.shape[0]
    high = edges_ref.shape[0] // 2
    for mate, send_ref in zip(mates(f), send_refs):
        send_ref[0:panel, :] = part(mate).astype(BF16)
        send_ref[panel : panel + small, :] = tail
        if send_ref.shape[0] > panel + small:
            send_ref[panel + small :, :] = jnp.where(mate > f, edges_ref[:high, :], edges_ref[high:, :])
    kept_ref[0:panel, :] = part(f)
    kept_ref[panel:, :] = tail.astype(F32)


def mates(index):
    low = 1 - 2 * lax.rem(index, 2)
    high = jnp.where(index < 2, 2, -2)
    return index + low, index + high, index + low + high


def four_sums(mine, parts):
    first, second, third = (part.astype(F32) for part in parts)
    return (mine + first) + (second + third)


def chips_kernel(axis, kept_ref, first_ref, second_ref, third_ref, send_ref, plain_ref):
    f = lax.axis_index(axis)
    even = lax.rem(f, 2) == 0
    count = kept_ref.shape[0]
    total = four_sums(kept_ref[...], [ref[0:count, :] for ref in (first_ref, second_ref, third_ref)]).astype(BF16)
    near, far = first_ref[count:, :], third_ref[count:, :]
    far = jnp.where((f == 0) | (f == lax.axis_size(axis) - 1), jnp.zeros_like(far), far)
    edges = [jnp.where(even, far, near), jnp.where(even, near, far)]
    plain_ref[...] = total
    send_ref[...] = jnp.concatenate([total, *edges], axis=0)


def total_kernel(axes, mine_ref, first_ref, second_ref, third_ref, total_ref):
    q, core = lax.axis_index(axes[0]), lax.axis_index(axes[1])
    count = second_ref.shape[0]
    wide = mine_ref.shape[0] - count
    mine = mine_ref[0:count, :].astype(F32)
    total_ref[0:count, :] = four_sums(mine, [ref[0:count, :] for ref in (first_ref, second_ref, third_ref)])
    total_ref[count : count + wide, :] = mine_ref[count:, :].astype(F32)
    other = q + 1 - 2 * core
    beside = lax.rem(q + core, 2) == 0
    value = jnp.where(beside, first_ref[count:, :], third_ref[count:, :]).astype(F32)
    total_ref[count + wide :, :] = jnp.where((other >= 0) & (other < lax.axis_size(axes[0])), value, 0.0)


def back_kernel(core_axis, mid_ref, share_ref, far_ref, cot_ref, w_ref, acc_ref, xs_ref):
    rows, channels, width = cot_ref.shape
    upper = lax.axis_index(core_axis) == 0
    nothing = jnp.zeros((channels, LANES), BF16)
    put = lambda r, x: spread(xs_ref, r, jnp.concatenate([x, nothing], axis=1))
    for k in range(HALO):
        pair, far = get_strip(share_ref, k, channels, width), far_ref[k]
        put(k, jnp.where(upper, far, pair))
        put(HALO + rows + k, jnp.where(upper, pair, far))
    for i in range(rows):
        put(HALO + i, mid_ref[i])
    depthwise(w_ref, xs_ref, acc_ref, rows, range(rows + 2 * HALO))
    for i in range(rows):
        acc_ref[i * channels : (i + 1) * channels, :] += cot_ref[i].astype(F32)


def finish_kernel(
    factor, core_axis, mine_ref, other_ref, acc_ref, taps_ref,
    back_ref, kg_ref, dwb_ref, gain_ref, lnb_ref, ge_ref, eb_ref, gr_ref, rb_ref, sc_ref, ends_ref, side_ref,
):
    channels = kg_ref.shape[2]
    panel = gr_ref.shape[0]
    core = lax.axis_index(core_axis)
    rows, width = back_ref.shape[1:]
    high = edge_height(rows)
    low = mine_ref.shape[0] - 4 * high
    own, near, beyond = mine_ref[low : low + 2 * high, :], other_ref[low : low + 2 * high, :], other_ref[low + 2 * high :, :]
    above, below = jnp.where(core == 0, beyond, near), jnp.where(core == 0, near, beyond)
    for side in range(2):
        for k in range(HALO):
            at = side * high + k * rows
            ends_ref[side * HALO + k, 0:HALO, :] = above[at + rows - HALO : at + rows]
            ends_ref[side * HALO + k, HALO : HALO + rows, :] = own[at : at + rows]
            ends_ref[side * HALO + k, HALO + rows : 2 * HALO + rows, :] = below[at : at + HALO]
    side_ref[...] = jnp.zeros_like(side_ref)
    for side in range(2):
        for j in range(HALO):
            total = None
            for k in range(HALO):
                b = k + side * (SIDE - 1) - j
                if not 0 <= b < SIDE:
                    continue
                for a in range(SIDE):
                    tap = taps_ref[SIDE - 1 - a, SIDE - 1 - b : SIDE - b, :]
                    part = tap * ends_ref[side * HALO + k, a : a + rows, 0:channels]
                    total = part if total is None else total + part
            at = (side * HALO + j) * rows
            side_ref[at : at + rows, 0:channels] = total
    side = side_ref[...]
    upper = side.astype(BF16)
    lower = (side - upper.astype(F32)).astype(BF16)
    side_t = jnp.concatenate([upper, lower], axis=0).T
    count = side_ref.shape[0]
    q, l = iota((2 * count, LANES), 0), iota((2 * count, LANES), 1)
    q = jnp.where(q >= count, q - count, q)
    for i in range(rows):
        first = (q == l * rows + i) & (l < HALO)
        last = (q == (HALO + l - (LANES - HALO)) * rows + i) & (l >= LANES - HALO)
        extra = [dot(side_t, jnp.where(at, 1.0, 0.0).astype(BF16))[0:channels] for at in (first, last)]
        value = acc_ref[i * channels : (i + 1) * channels, :]
        tiles = [value[:, k : k + LANES] for k in range(0, width, LANES)]
        tiles[0] = tiles[0] + extra[0]
        tiles[-1] = tiles[-1] + extra[1]
        back_ref[:, i, :] = jnp.concatenate(tiles, axis=1).astype(BF16)
    mine, other = mine_ref[0:low, :] * factor, other_ref[0:low, :] * factor
    low, high = jnp.where(core == 0, mine, other), jnp.where(core == 0, other, mine)
    small = mine[panel:] + other[panel:]
    for b in range(SIDE):
        kg_ref[:, b, :] = small[b * 8 : b * 8 + SIDE, 0:channels]
    for b, ref in enumerate((dwb_ref, gain_ref, lnb_ref, rb_ref, sc_ref)):
        ref[...] = small[b * 8 + SIDE : b * 8 + 8, 0:channels]
    gr_ref[...] = low[0:panel, 0:channels]
    ge_ref[...] = high[0:panel, 0:channels]
    eye = iota((panel, panel), 0) == iota((panel, panel), 1)
    eb_ref[...] = jnp.sum(jnp.where(eye, high[0:panel, channels : channels + 1], 0.0), axis=0, keepdims=True)


def call(kernel, outs, *args, scratch=(), after=(), flops=0):
    size = sum(math.prod(a.shape) * a.dtype.itemsize for a in args)
    size += sum(math.prod(s) * jnp.dtype(d).itemsize for s, d in outs)
    count = len(args)

    def body(*refs):
        kernel(*refs[:count], *refs[count + len(after) :])

    in_vmem = pl.BlockSpec(memory_space=pltpu.VMEM)
    anywhere = pl.BlockSpec(memory_space=pl.ANY)
    return pl.pallas_call(
        body,
        out_shape=[jax.ShapeDtypeStruct(s, d) for s, d in outs],
        in_specs=[in_vmem] * count + [anywhere] * len(after),
        out_specs=[in_vmem] * len(outs),
        scratch_shapes=[pltpu.VMEM(s, d) for s, d in scratch],
        compiler_params=pltpu.CompilerParams(vmem_limit_bytes=40 * 2**20),
        cost_estimate=pl.CostEstimate(flops=flops, bytes_accessed=size, transcendentals=0),
    )(*args, *after)


def swap(x, axis, parity):
    size = lax.axis_size(axis)
    pairs = [(i, i + 1) for i in range(parity, size - 1, 2)]
    return lax.ppermute(x, axis, pairs + [(j, i) for i, j in pairs])


def crossed(x, axis, bits):
    return lax.ppermute(x, axis, [(i, i ^ bits) for i in range(lax.axis_size(axis))])


def edges_by_permutes(axes, edges):
    chip, core, filt = axes
    count = lax.axis_size(filt)
    right = [(i, i + 1) for i in range(count - 1)]
    left = [(j, i) for i, j in right]
    high = edges.shape[0] // 2
    own = jnp.concatenate([lax.ppermute(edges[:high], filt, right), lax.ppermute(edges[high:], filt, left)], axis=0)
    return jnp.concatenate([own, swap(own, (chip, core), 1)], axis=0)


def shards(
    axes, image, cotangent, kernel, dw_bias, layer_norm_gain, layer_norm_bias,
    w_expand, b_expand, w_reduce, b_reduce, layer_scale,
):
    chip, core, filt = axes
    chip_n, core_n, filt_n = (lax.axis_size(a) for a in axes)
    channels, rows, width = image.shape
    hidden_n = w_expand.shape[0]
    groups = channels // GROUP
    panel = hidden_n // filt_n
    tall = rows + 2 * HALO
    deep = SIDE * channels
    extent = width + LANES
    tokens = rows * width
    lift = channels + 16
    direct = chip_n == 4 and filt_n == 4
    strip = ((HALO, channels, width), BF16)
    block = ((rows, channels, width), BF16)
    high = edge_height(rows)
    edge = ((2 * high, LANES), BF16)
    row = lambda v: v.reshape(1, -1)

    space = (chip, core)
    lead = HALO * channels * (width // LANES)
    mid = jnp.transpose(image, (1, 0, 2))
    ends = ((high, channels), BF16)
    lead = HALO * channels * (width // LANES)
    flat_strip = ((lead + 2 * high, LANES), BF16)
    first, second = call(functools.partial(edges_kernel, filt), [ends, ends], mid)
    first, second = swap(first, filt, 0), swap(second, filt, 1)
    own, far = call(functools.partial(far_kernel, axes), [edge, flat_strip], mid, first, second)
    far = swap(far, space, 1)
    we_t, wr_t = w_expand.T, w_reduce.T
    taps = jnp.transpose(kernel, (1, 2, 0))
    cot_t, forward, backward, we2, wr2, columns = call(
        prepare_kernel,
        [
            block,
            ((groups, DEEP, DEEP), BF16),
            ((groups, DEEP, DEEP), BF16),
            ((hidden_n, lift), BF16),
            ((hidden_n, channels), BF16),
            ((channels, LANES), F32),
        ],
        cotangent, taps, row(dw_bias), row(layer_norm_gain), row(layer_norm_bias),
        we_t, row(b_expand), wr_t, row(b_reduce), row(layer_scale),
        scratch=[((lift, hidden_n), BF16), ((8, DEEP), F32)],
        after=[own],
    )
    (pair,) = call(functools.partial(pair_kernel, core), [flat_strip], mid, own, after=[columns])
    pair = swap(pair, core, 0)
    before, own_x = call(
        own_rows_kernel,
        [((rows * channels, width), F32), ((rows, channels, extent), BF16)],
        mid, own, forward,
        scratch=[((rows * deep, width), BF16)],
    )
    small_n = 64
    flat = ((hidden_n, LANES), F32)
    out_t, dconv, far_out, x, vectors, share, keep = call(
        functools.partial(main_kernel, axes),
        [
            block, block, strip, ((2 * HALO, channels, extent), BF16), ((8, LANES), F32),
            ((HALO * channels * (width // LANES) + hidden_n, LANES), BF16), flat,
        ],
        mid, pair, far, own, before, cot_t, forward, we_t, wr_t, we2, wr2, columns, row(layer_scale),
        scratch=[
            ((2 * HALO * deep, width), BF16),
            ((rows * channels, width), F32),
            ((channels, width), F32),
            ((lift, tokens), BF16),
            ((channels, tokens), BF16),
            ((hidden_n, tokens), BF16),
            ((hidden_n, tokens), BF16),
        ],
    )
    output = jnp.transpose(out_t, (1, 0, 2))
    edges, small = call(
        depthwise_gradient_kernel,
        [edge, ((small_n, LANES), F32)],
        x, own_x, dconv, vectors,
        scratch=[((deep, rows * extent), BF16), ((deep, rows * extent), BF16), ((8, DEEP), F32)],
    )
    share = swap(share, core, 0)
    far = swap(far_out, space, 1) if direct else None
    low = panel + small_n
    if direct:
        sums = ((low, LANES), BF16)
        *sends, kept = call(
            functools.partial(columns_kernel, filt, panel),
            [((low + high, LANES), BF16), sums, ((low + high, LANES), BF16), ((low, LANES), F32)],
            share, keep, small, edges,
            scratch=[flat],
        )
        third, second, first = (crossed(sends[k - 1], filt, k) for k in (3, 2, 1))
        send, plain = call(
            functools.partial(chips_kernel, filt), [((low + 2 * high, LANES), BF16), sums], kept, first, second, third,
            flops=4 * 10**9,
        )
        third, second, first = (crossed(plain if k == 2 else send, chip, k) for k in (3, 2, 1))
        (mine,) = call(
            functools.partial(total_kernel, axes),
            [((low + 4 * high, LANES), F32)],
            send, first, second, third,
            after=[output, far],
        )
    else:
        far = swap(far_out, space, 1)
        edges = edges_by_permutes(axes, edges).astype(F32)
        total, small = lax.psum((keep + share[-hidden_n:].astype(F32), small), (chip, filt))
        total = lax.dynamic_slice_in_dim(total, lax.axis_index(filt) * panel, panel, 0)
        mine = jnp.concatenate([total, small, edges], axis=0)
    other = swap(mine, core, 0)
    (back,) = call(
        functools.partial(back_kernel, core),
        [((rows * channels, width), F32)],
        dconv, share, far, cot_t, backward,
        scratch=[((tall * deep, width), BF16)],
        after=[mine],
    )
    factor = 1.0 / math.sqrt(tokens * chip_n * core_n * filt_n)
    line = ((1, channels), F32)
    matrix = ((panel, channels), F32)
    image_grad, kg, dwb, gain, lnb, ge, eb, gr, rb, sc = call(
        functools.partial(finish_kernel, factor, core),
        [
            ((channels, rows, width), BF16),
            ((SIDE, SIDE, channels), F32),
            line, line, line, matrix, ((1, panel), F32), matrix, line, line,
        ],
        mine, other, back, taps,
        scratch=[((2 * HALO, 16, LANES), F32), ((2 * HALO * rows, LANES), F32)],
    )
    flat = lambda v: v.reshape(-1)
    return (
        output, image_grad, jnp.transpose(kg, (2, 0, 1)),
        flat(dwb), flat(gain), flat(lnb), ge, flat(eb), gr, flat(rb), flat(sc),
    )


def solution(mesh):
    space, filt = mesh.devices.shape
    axes = ("chip", "core", "filt")
    pairs = Mesh(mesh.devices.reshape(space // 2, 2, filt), axes)
    pixels = P(None, ("chip", "core"), "filt")
    whole, shard = P(), P("filt")
    return jax.shard_map(
        functools.partial(shards, axes),
        mesh=pairs,
        in_specs=(pixels, pixels) + (whole,) * 9,
        out_specs=(pixels, pixels, whole, whole, whole, whole, shard, shard, shard, whole, whole),
        check_vma=False,
    )
```

```python
import functools
import math

import jax
import jax.numpy as jnp
from jax import lax
from jax.experimental import pallas as pl
from jax.experimental.pallas import tpu as pltpu
from jax.sharding import Mesh, PartitionSpec as P

F32 = jnp.float32
BF16 = jnp.bfloat16
SIDE = 7
HALO = 3
LANES = 128
GROUP = 32
DEEP = SIDE * GROUP
NT = (((1,), (1,)), ((), ()))
VECTORS = ("dwb", "gain", "lnb", "rb", "scale")


def iota(shape, dim):
    return lax.broadcasted_iota(jnp.int32, shape, dim)


def dot(a, b, dims=(((1,), (0,)), ((), ()))):
    return lax.dot_general(a, b, dims, preferred_element_type=F32)


def column(row):
    n = row.shape[1]
    eye = iota((n, n), 0) == iota((n, n), 1)
    return jnp.sum(jnp.where(eye, row, 0.0), axis=1, keepdims=True)


def widened(value):
    fill = jnp.zeros((value.shape[0], LANES - value.shape[1]), value.dtype)
    return jnp.concatenate([value, fill], axis=1)


def edge_height(rows):
    return -(-HALO * rows // 16) * 16


def pack_edges(rows):
    count = len(rows)
    width, high = rows[0].shape[1], edge_height(count)
    q, j = iota((2 * high, width), 0), iota((2 * high, width), 1)
    total = None
    for i, row in enumerate(rows):
        last = (q == count * (j - (width - HALO)) + i) & (j >= width - HALO)
        first = (q == high + count * j + i) & (j < HALO)
        pick = jnp.where(last | first, 1.0, 0.0).astype(BF16)
        part = dot(pick, row, NT)
        total = part if total is None else total + part
    return total.astype(BF16)


def halo_tile(edges_t, i, count):
    high = edges_t.shape[1] // 2
    q, l = iota((2 * high, LANES), 0), iota((2 * high, LANES), 1)
    left = (q == count * (l - (LANES - HALO)) + i) & (l >= LANES - HALO)
    right = (q == high + count * l + i) & (l < HALO)
    pick = jnp.where(left | right, 1.0, 0.0).astype(BF16)
    return dot(edges_t, pick).astype(BF16)


def group_diagonal():
    lane = iota((1, DEEP), 1)
    inner = lane
    for b in range(1, SIDE):
        inner = jnp.where(lane >= b * GROUP, lane - b * GROUP, inner)
    return inner == iota((GROUP, DEEP), 0)


def tap_matrices(taps_ref, line_ref, w_ref, flip):
    diagonal = group_diagonal()
    for g in range(w_ref.shape[0]):
        for b in range(SIDE):
            piece = taps_ref[:, SIDE - 1 - b if flip else b, g * GROUP : (g + 1) * GROUP]
            line_ref[0:SIDE, b * GROUP : (b + 1) * GROUP] = piece
        for m in range(SIDE):
            a = m if flip else SIDE - 1 - m
            w_ref[g, m * GROUP : (m + 1) * GROUP, :] = jnp.where(diagonal, line_ref[a : a + 1, :], 0.0).astype(BF16)


def shifted(x, amount):
    return x if amount % x.shape[1] == 0 else pltpu.roll(x, amount % x.shape[1], 1)


def spread(xs_ref, r, x):
    channels = x.shape[0]
    width = xs_ref.shape[1]
    for b in range(SIDE):
        moved = shifted(x, HALO - b)[:, :width]
        for g in range(channels // GROUP):
            at = r * SIDE * channels + g * DEEP + b * GROUP
            xs_ref[at : at + GROUP, :] = moved[g * GROUP : (g + 1) * GROUP]


def depthwise(w_ref, xs_ref, acc_ref, rows, taken, before_ref=None):
    groups = w_ref.shape[0]
    channels = groups * GROUP
    for g in range(groups):
        at = [slice(i * channels + g * GROUP, i * channels + (g + 1) * GROUP) for i in range(rows)]
        sums = [None if before_ref is None else before_ref[at[i], :] for i in range(rows)]
        for k, r in enumerate(taken):
            i0, i1 = max(0, r - (SIDE - 1)), min(rows - 1, r)
            m0 = SIDE - 1 - r + i0
            low = k * SIDE * channels + g * DEEP
            part = dot(w_ref[g, m0 * GROUP : (m0 + i1 - i0 + 1) * GROUP, :], xs_ref[low : low + DEEP, :])
            for i in range(i0, i1 + 1):
                piece = part[(i - i0) * GROUP : (i - i0 + 1) * GROUP]
                sums[i] = piece if sums[i] is None else sums[i] + piece
        for i in range(rows):
            acc_ref[at[i], :] = sums[i]


def own_rows_kernel(mid_ref, own_ref, w_ref, acc_ref, x_ref, xs_ref):
    rows, channels, _ = mid_ref.shape
    edges_t = own_ref[:, 0:channels].T
    for i in range(rows):
        x = jnp.concatenate([mid_ref[i], halo_tile(edges_t, i, rows)], axis=1)
        x_ref[i] = x
        spread(xs_ref, i, x)
    depthwise(w_ref, xs_ref, acc_ref, rows, range(HALO, HALO + rows))


def edges_kernel(axis, mid_ref, second_ref, first_ref):
    edges = pack_edges([mid_ref[i] for i in range(mid_ref.shape[0])])
    high = edges.shape[0] // 2
    even = lax.rem(lax.axis_index(axis), 2) == 0
    first_ref[...] = jnp.where(even, edges[:high], edges[high:])
    second_ref[...] = jnp.where(even, edges[high:], edges[:high])


def far_kernel(axes, mid_ref, second_ref, first_ref, own_ref, far_ref):
    even = lax.rem(lax.axis_index(axes[2]), 2) == 0
    first, second = first_ref[...], second_ref[...]
    edges = jnp.concatenate([jnp.where(even, second, first), jnp.where(even, first, second)], axis=0)
    own_ref[...] = widened(edges)
    put_strips(mid_ref, own_ref, far_ref, lax.axis_index(axes[1]))


def pair_kernel(core_axis, mid_ref, own_ref, pair_ref):
    put_strips(mid_ref, own_ref, pair_ref, 1 - lax.axis_index(core_axis))


def put_strips(mid_ref, edges_ref, to_ref, last):
    for k in range(HALO):
        put_strip(to_ref, k, mid_ref[k + (mid_ref.shape[0] - HALO) * last])
    to_ref[to_ref.shape[0] - edges_ref.shape[0] :, :] = edges_ref[...]


def put_strip(ref, k, row):
    channels, width = row.shape
    parts = width // LANES
    for p in range(parts):
        ref[(k * parts + p) * channels : (k * parts + p + 1) * channels, :] = row[:, p * LANES : (p + 1) * LANES]


def get_strip(ref, k, channels, width):
    parts = width // LANES
    pieces = [ref[(k * parts + p) * channels : (k * parts + p + 1) * channels, :] for p in range(parts)]
    return jnp.concatenate(pieces, axis=1)


def prepare_kernel(
    cot_ref, taps_ref, dwb_ref, gain_ref, lnb_ref, we_ref, be_ref, wr_ref, br_ref, scale_ref,
    cot_t_ref, forward_ref, backward_ref, we2_ref, wr2_ref, columns_ref, lift_ref, line_ref,
):
    for i in range(cot_t_ref.shape[0]):
        cot_t_ref[i] = cot_ref[:, i, :]
    tap_matrices(taps_ref, line_ref, forward_ref, False)
    tap_matrices(taps_ref, line_ref, backward_ref, True)
    channels, hidden_n = we_ref.shape
    extra = lift_ref.shape[0] - channels
    lift_ref[0:channels, :] = we_ref[...]
    lift_ref[channels:, :] = jnp.where(iota((extra, hidden_n), 0) == 0, be_ref[...].astype(F32), 0.0).astype(BF16)
    we2_ref[...] = lift_ref[...].T
    wr2_ref[...] = wr_ref[...].T
    lane = iota(columns_ref.shape, 1)
    total = jnp.zeros(columns_ref.shape, F32)
    for k, ref in enumerate((dwb_ref, gain_ref, lnb_ref, br_ref, scale_ref)):
        total = jnp.where(lane == k, column(ref[...]), total)
    columns_ref[...] = total


def gelu_parts(v):
    z = jnp.abs(v)
    t = 1.0 / (1.0 + (0.3275911 / math.sqrt(2.0)) * z)
    e = jnp.exp2((-0.5 * math.log2(math.e)) * (v * v))
    half = 0.5
    poly = t * (
        half * 0.254829592
        + t * (half * -0.284496736 + t * (half * 1.421413741 + t * (half * -1.453152027 + t * (half * 1.061405429))))
    )
    tail = poly * e
    return jnp.where(v >= 0.0, 1.0 - tail, tail), (v * (1.0 / math.sqrt(2.0 * math.pi))) * e


def main_kernel(
    axes,
    mid_ref, pair_ref, beyond_ref, own_ref, before_ref, cot_ref, w_ref, we_ref, wr_ref, we2_ref, wr2_ref, columns_ref, scale_ref,
    out_ref, dconv_ref, far_ref, x_ref, vectors_ref, share_ref, keep_ref,
    xs_ref, acc_ref, xhat_ref, nm_ref, db_ref, act_ref, dh_ref,
):
    rows, channels, width = cot_ref.shape
    hidden_n = we_ref.shape[1]
    core = lax.axis_index(axes[1])
    dwb, gain, lnb, br, scale = (columns_ref[:, k : k + 1] for k in range(5))
    lead = HALO * channels * (width // LANES)
    upper = core == 0
    high = own_ref.shape[0]
    near, beyond = (ref[ref.shape[0] - high :, 0:channels].T for ref in (pair_ref, beyond_ref))
    above, below = jnp.where(upper, beyond, near), jnp.where(upper, near, beyond)
    for k in range(HALO):
        pair, far = (get_strip(ref, k, channels, width) for ref in (pair_ref, beyond_ref))
        up, down = jnp.where(upper, far, pair), jnp.where(upper, pair, far)
        up = jnp.concatenate([up, halo_tile(above, rows - HALO + k, rows)], axis=1)
        down = jnp.concatenate([down, halo_tile(below, k, rows)], axis=1)
        x_ref[k] = up
        x_ref[HALO + k] = down
        spread(xs_ref, k, up)
        spread(xs_ref, HALO + k, down)
    taken = [*range(HALO), *range(HALO + rows, rows + 2 * HALO)]
    depthwise(w_ref, xs_ref, acc_ref, rows, taken, before_ref)
    extra = nm_ref.shape[0] - channels
    nm_ref[channels:, :] = jnp.where(iota((extra, rows * width), 0) == 0, 1.0, 0.0).astype(BF16)
    zero = jnp.zeros((channels, LANES), F32)
    sums = {k: zero for k in VECTORS}

    def add(name, value):
        for k in range(0, width, LANES):
            sums[name] = sums[name] + value[:, k : k + LANES]

    chunk = 128
    for i in range(rows):
        cols = slice(i * width, (i + 1) * width)
        conv = acc_ref[i * channels : (i + 1) * channels, :] + dwb
        conv = conv - jnp.mean(conv, axis=0, keepdims=True)
        inv = lax.rsqrt(jnp.mean(conv * conv, axis=0, keepdims=True) + 1e-6)
        xhat = conv * inv
        xhat_ref[...] = xhat
        nm_ref[0:channels, cols] = (xhat * gain + lnb).astype(BF16)
        cot = cot_ref[i].astype(F32)
        add("rb", cot)
        db_ref[:, cols] = (cot * scale).astype(BF16)
        for h0 in range(0, hidden_n, chunk):
            hs = slice(h0, h0 + chunk)
            hidden = dot(we2_ref[hs, :], nm_ref[:, cols])
            back = dot(wr2_ref[hs, :], db_ref[:, cols])
            phi, bump = gelu_parts(hidden)
            act_ref[hs, cols] = (hidden * phi).astype(BF16)
            dh_ref[hs, cols] = (back * (phi + bump)).astype(BF16)
        branch = dot(wr_ref[...], act_ref[:, cols]) + br
        out_ref[i] = (mid_ref[i].astype(F32) + scale * branch).astype(BF16)
        add("scale", cot * branch)
        d_normed = dot(we_ref[...], dh_ref[:, cols])
        xhat = xhat_ref[...]
        add("lnb", d_normed)
        add("gain", d_normed * xhat)
        d_xhat = d_normed * gain
        m1 = jnp.mean(d_xhat, axis=0, keepdims=True)
        m2 = jnp.mean(d_xhat * xhat, axis=0, keepdims=True)
        dconv = (inv * (d_xhat - m1 - xhat * m2)).astype(BF16)
        add("dwb", dconv.astype(F32))
        dconv_ref[i] = dconv
    for k in range(HALO):
        put_strip(share_ref, k, dconv_ref[k + (rows - HALO) * (1 - core)])
        far_ref[k] = dconv_ref[k + (rows - HALO) * core]
    g_reduce = widened(dot(act_ref[...], db_ref[...], NT))
    g_expand = widened(dot(dh_ref[...], nm_ref[...], NT))
    keep_ref[...] = jnp.where(core == 0, g_reduce, g_expand)
    share_ref[lead:, :] = jnp.where(core == 0, g_expand, g_reduce).astype(BF16)
    vectors_ref[...] = jnp.zeros_like(vectors_ref)
    for b, name in enumerate(VECTORS):
        total = jnp.sum(sums[name].T, axis=0, keepdims=True)
        vectors_ref[b : b + 1, 0:channels] = total * scale_ref[...] if name == "rb" else total


def depthwise_gradient_kernel(x_ref, own_x_ref, dconv_ref, vectors_ref, edges_ref, small_ref, wide_ref, dcs_ref, line_ref):
    rows, channels, width = dconv_ref.shape
    groups = channels // GROUP
    extent = width + LANES
    edges_ref[...] = widened(pack_edges([dconv_ref[i] for i in range(rows)]))
    for i in range(rows):
        padded = jnp.concatenate([dconv_ref[i], jnp.zeros((channels, LANES), BF16)], axis=1)
        columns = slice(i * extent, (i + 1) * extent)
        for b in range(SIDE):
            moved = shifted(padded, b - HALO)
            for g in range(groups):
                at = g * DEEP + b * GROUP
                dcs_ref[at : at + GROUP, columns] = moved[g * GROUP : (g + 1) * GROUP]
        for a in range(SIDE):
            r = i + a
            if HALO <= r < HALO + rows:
                x = own_x_ref[r - HALO]
            else:
                x = x_ref[r if r < HALO else r - rows]
            for g in range(groups):
                at = g * DEEP + a * GROUP
                wide_ref[at : at + GROUP, columns] = x[g * GROUP : (g + 1) * GROUP, :]
    small_ref[...] = jnp.zeros_like(small_ref)
    diagonal = group_diagonal()
    for g in range(groups):
        taps = dot(wide_ref[g * DEEP : (g + 1) * DEEP, :], dcs_ref[g * DEEP : (g + 1) * DEEP, :], NT)
        for a in range(SIDE):
            part = jnp.where(diagonal, taps[a * GROUP : (a + 1) * GROUP, :], 0.0)
            line_ref[a : a + 1, :] = jnp.sum(part, axis=0, keepdims=True)
        for b in range(SIDE):
            small_ref[b * 8 : b * 8 + SIDE, g * GROUP : (g + 1) * GROUP] = line_ref[0:SIDE, b * GROUP : (b + 1) * GROUP]
    for b in range(len(VECTORS)):
        small_ref[b * 8 + SIDE : b * 8 + 8, :] = vectors_ref[b : b + 1, :]


def columns_kernel(axis, panel, share_ref, keep_ref, small_ref, edges_ref, *refs):
    *send_refs, kept_ref, total_ref = refs
    f = lax.axis_index(axis)
    count = total_ref.shape[0]
    total_ref[...] = keep_ref[...] + share_ref[share_ref.shape[0] - count :, :].astype(F32)
    part = lambda k: total_ref[pl.ds(pl.multiple_of(k * panel, 8), panel), :]
    tail = small_ref[...].astype(BF16)
    small = tail.shape[0]
    high = edges_ref.shape[0] // 2
    for mate, send_ref in zip(mates(f), send_refs):
        send_ref[0:panel, :] = part(mate).astype(BF16)
        send_ref[panel : panel + small, :] = tail
        if send_ref.shape[0] > panel + small:
            send_ref[panel + small :, :] = jnp.where(mate > f, edges_ref[:high, :], edges_ref[high:, :])
    kept_ref[0:panel, :] = part(f)
    kept_ref[panel:, :] = tail.astype(F32)


def mates(index):
    low = 1 - 2 * lax.rem(index, 2)
    high = jnp.where(index < 2, 2, -2)
    return index + low, index + high, index + low + high


def four_sums(mine, parts):
    first, second, third = (part.astype(F32) for part in parts)
    return (mine + first) + (second + third)


def chips_kernel(axis, kept_ref, first_ref, second_ref, third_ref, send_ref, plain_ref):
    f = lax.axis_index(axis)
    even = lax.rem(f, 2) == 0
    count = kept_ref.shape[0]
    total = four_sums(kept_ref[...], [ref[0:count, :] for ref in (first_ref, second_ref, third_ref)]).astype(BF16)
    near, far = first_ref[count:, :], third_ref[count:, :]
    far = jnp.where((f == 0) | (f == lax.axis_size(axis) - 1), jnp.zeros_like(far), far)
    edges = [jnp.where(even, far, near), jnp.where(even, near, far)]
    plain_ref[...] = total
    send_ref[...] = jnp.concatenate([total, *edges], axis=0)


def total_kernel(axes, mine_ref, first_ref, second_ref, third_ref, total_ref):
    q, core = lax.axis_index(axes[0]), lax.axis_index(axes[1])
    count = second_ref.shape[0]
    wide = mine_ref.shape[0] - count
    mine = mine_ref[0:count, :].astype(F32)
    total_ref[0:count, :] = four_sums(mine, [ref[0:count, :] for ref in (first_ref, second_ref, third_ref)])
    total_ref[count : count + wide, :] = mine_ref[count:, :].astype(F32)
    other = q + 1 - 2 * core
    beside = lax.rem(q + core, 2) == 0
    value = jnp.where(beside, first_ref[count:, :], third_ref[count:, :]).astype(F32)
    total_ref[count + wide :, :] = jnp.where((other >= 0) & (other < lax.axis_size(axes[0])), value, 0.0)


def back_kernel(core_axis, mid_ref, share_ref, far_ref, cot_ref, w_ref, acc_ref, xs_ref):
    rows, channels, width = cot_ref.shape
    upper = lax.axis_index(core_axis) == 0
    nothing = jnp.zeros((channels, LANES), BF16)
    put = lambda r, x: spread(xs_ref, r, jnp.concatenate([x, nothing], axis=1))
    for k in range(HALO):
        pair, far = get_strip(share_ref, k, channels, width), far_ref[k]
        put(k, jnp.where(upper, far, pair))
        put(HALO + rows + k, jnp.where(upper, pair, far))
    for i in range(rows):
        put(HALO + i, mid_ref[i])
    depthwise(w_ref, xs_ref, acc_ref, rows, range(rows + 2 * HALO))
    for i in range(rows):
        acc_ref[i * channels : (i + 1) * channels, :] += cot_ref[i].astype(F32)


def finish_kernel(
    factor, core_axis, mine_ref, other_ref, acc_ref, taps_ref,
    back_ref, kg_ref, dwb_ref, gain_ref, lnb_ref, ge_ref, eb_ref, gr_ref, rb_ref, sc_ref, ends_ref, side_ref,
):
    channels = kg_ref.shape[2]
    panel = gr_ref.shape[0]
    core = lax.axis_index(core_axis)
    rows, width = back_ref.shape[1:]
    high = edge_height(rows)
    low = mine_ref.shape[0] - 4 * high
    own, near, beyond = mine_ref[low : low + 2 * high, :], other_ref[low : low + 2 * high, :], other_ref[low + 2 * high :, :]
    above, below = jnp.where(core == 0, beyond, near), jnp.where(core == 0, near, beyond)
    for side in range(2):
        for k in range(HALO):
            at = side * high + k * rows
            ends_ref[side * HALO + k, 0:HALO, :] = above[at + rows - HALO : at + rows]
            ends_ref[side * HALO + k, HALO : HALO + rows, :] = own[at : at + rows]
            ends_ref[side * HALO + k, HALO + rows : 2 * HALO + rows, :] = below[at : at + HALO]
    side_ref[...] = jnp.zeros_like(side_ref)
    taps = [taps_ref[a] for a in range(SIDE)]
    for side in range(2):
        for j in range(HALO):
            total = None
            for k in range(HALO):
                b = k + side * (SIDE - 1) - j
                if not 0 <= b < SIDE:
                    continue
                for a in range(SIDE):
                    tap = taps[SIDE - 1 - a][SIDE - 1 - b : SIDE - b]
                    part = tap * ends_ref[side * HALO + k, a : a + rows, 0:channels]
                    total = part if total is None else total + part
            at = (side * HALO + j) * rows
            side_ref[at : at + rows, 0:channels] = total
    side = side_ref[...]
    upper = side.astype(BF16)
    lower = (side - upper.astype(F32)).astype(BF16)
    side_t = jnp.concatenate([upper, lower], axis=0).T
    count = side_ref.shape[0]
    q, l = iota((2 * count, LANES), 0), iota((2 * count, LANES), 1)
    q = jnp.where(q >= count, q - count, q)
    for i in range(rows):
        first = (q == l * rows + i) & (l < HALO)
        last = (q == (HALO + l - (LANES - HALO)) * rows + i) & (l >= LANES - HALO)
        extra = [dot(side_t, jnp.where(at, 1.0, 0.0).astype(BF16))[0:channels] for at in (first, last)]
        value = acc_ref[i * channels : (i + 1) * channels, :]
        tiles = [value[:, k : k + LANES] for k in range(0, width, LANES)]
        tiles[0] = tiles[0] + extra[0]
        tiles[-1] = tiles[-1] + extra[1]
        back_ref[:, i, :] = jnp.concatenate(tiles, axis=1).astype(BF16)
    mine, other = mine_ref[0:low, :] * factor, other_ref[0:low, :] * factor
    low, high = jnp.where(core == 0, mine, other), jnp.where(core == 0, other, mine)
    small = mine[panel:] + other[panel:]
    for b in range(SIDE):
        kg_ref[:, b, :] = small[b * 8 : b * 8 + SIDE, 0:channels]
    for b, ref in enumerate((dwb_ref, gain_ref, lnb_ref, rb_ref, sc_ref)):
        ref[...] = small[b * 8 + SIDE : b * 8 + 8, 0:channels]
    gr_ref[...] = low[0:panel, 0:channels]
    ge_ref[...] = high[0:panel, 0:channels]
    eye = iota((panel, panel), 0) == iota((panel, panel), 1)
    eb_ref[...] = jnp.sum(jnp.where(eye, high[0:panel, channels : channels + 1], 0.0), axis=0, keepdims=True)


def call(kernel, outs, *args, scratch=(), after=(), flops=0):
    size = sum(math.prod(a.shape) * a.dtype.itemsize for a in args)
    size += sum(math.prod(s) * jnp.dtype(d).itemsize for s, d in outs)
    count = len(args)

    def body(*refs):
        kernel(*refs[:count], *refs[count + len(after) :])

    in_vmem = pl.BlockSpec(memory_space=pltpu.VMEM)
    anywhere = pl.BlockSpec(memory_space=pl.ANY)
    return pl.pallas_call(
        body,
        out_shape=[jax.ShapeDtypeStruct(s, d) for s, d in outs],
        in_specs=[in_vmem] * count + [anywhere] * len(after),
        out_specs=[in_vmem] * len(outs),
        scratch_shapes=[pltpu.VMEM(s, d) for s, d in scratch],
        compiler_params=pltpu.CompilerParams(vmem_limit_bytes=40 * 2**20),
        cost_estimate=pl.CostEstimate(flops=flops, bytes_accessed=size, transcendentals=0),
    )(*args, *after)


def swap(x, axis, parity):
    size = lax.axis_size(axis)
    pairs = [(i, i + 1) for i in range(parity, size - 1, 2)]
    return lax.ppermute(x, axis, pairs + [(j, i) for i, j in pairs])


def crossed(x, axis, bits):
    return lax.ppermute(x, axis, [(i, i ^ bits) for i in range(lax.axis_size(axis))])


def edges_by_permutes(axes, edges):
    chip, core, filt = axes
    count = lax.axis_size(filt)
    right = [(i, i + 1) for i in range(count - 1)]
    left = [(j, i) for i, j in right]
    high = edges.shape[0] // 2
    own = jnp.concatenate([lax.ppermute(edges[:high], filt, right), lax.ppermute(edges[high:], filt, left)], axis=0)
    return jnp.concatenate([own, swap(own, (chip, core), 1)], axis=0)


def shards(
    axes, image, cotangent, kernel, dw_bias, layer_norm_gain, layer_norm_bias,
    w_expand, b_expand, w_reduce, b_reduce, layer_scale,
):
    chip, core, filt = axes
    chip_n, core_n, filt_n = (lax.axis_size(a) for a in axes)
    channels, rows, width = image.shape
    hidden_n = w_expand.shape[0]
    groups = channels // GROUP
    panel = hidden_n // filt_n
    tall = rows + 2 * HALO
    deep = SIDE * channels
    extent = width + LANES
    tokens = rows * width
    lift = channels + 16
    direct = chip_n == 4 and filt_n == 4
    strip = ((HALO, channels, width), BF16)
    block = ((rows, channels, width), BF16)
    high = edge_height(rows)
    edge = ((2 * high, LANES), BF16)
    row = lambda v: v.reshape(1, -1)

    space = (chip, core)
    lead = HALO * channels * (width // LANES)
    mid = jnp.transpose(image, (1, 0, 2))
    ends = ((high, channels), BF16)
    lead = HALO * channels * (width // LANES)
    flat_strip = ((lead + 2 * high, LANES), BF16)
    second, first = call(functools.partial(edges_kernel, filt), [ends, ends], mid)
    second, first = swap(second, filt, 1), swap(first, filt, 0)
    own, far = call(functools.partial(far_kernel, axes), [edge, flat_strip], mid, second, first)
    far = swap(far, space, 1)
    we_t, wr_t = w_expand.T, w_reduce.T
    taps = jnp.transpose(kernel, (1, 2, 0))
    cot_t, forward, backward, we2, wr2, columns = call(
        prepare_kernel,
        [
            block,
            ((groups, DEEP, DEEP), BF16),
            ((groups, DEEP, DEEP), BF16),
            ((hidden_n, lift), BF16),
            ((hidden_n, channels), BF16),
            ((channels, LANES), F32),
        ],
        cotangent, taps, row(dw_bias), row(layer_norm_gain), row(layer_norm_bias),
        we_t, row(b_expand), wr_t, row(b_reduce), row(layer_scale),
        scratch=[((lift, hidden_n), BF16), ((16, DEEP), F32)],
        after=[own],
    )
    (pair,) = call(functools.partial(pair_kernel, core), [flat_strip], mid, own, after=[columns])
    pair = swap(pair, core, 0)
    before, own_x = call(
        own_rows_kernel,
        [((rows * channels, width), F32), ((rows, channels, extent), BF16)],
        mid, own, forward,
        scratch=[((rows * deep, width), BF16)],
    )
    small_n = 64
    flat = ((hidden_n, LANES), F32)
    out_t, dconv, far_out, x, vectors, share, keep = call(
        functools.partial(main_kernel, axes),
        [
            block, block, strip, ((2 * HALO, channels, extent), BF16), ((16, LANES), F32),
            ((HALO * channels * (width // LANES) + hidden_n, LANES), BF16), flat,
        ],
        mid, pair, far, own, before, cot_t, forward, we_t, wr_t, we2, wr2, columns, row(layer_scale),
        scratch=[
            ((2 * HALO * deep, width), BF16),
            ((rows * channels, width), F32),
            ((channels, width), F32),
            ((lift, tokens), BF16),
            ((channels, tokens), BF16),
            ((hidden_n, tokens), BF16),
            ((hidden_n, tokens), BF16),
        ],
    )
    output = jnp.transpose(out_t, (1, 0, 2))
    edges, small = call(
        depthwise_gradient_kernel,
        [edge, ((small_n, LANES), F32)],
        x, own_x, dconv, vectors,
        scratch=[((deep, rows * extent), BF16), ((deep, rows * extent), BF16), ((16, DEEP), F32)],
    )
    share = swap(share, core, 0)
    far = swap(far_out, space, 1) if direct else None
    low = panel + small_n
    if direct:
        sums = ((low, LANES), BF16)
        *sends, kept = call(
            functools.partial(columns_kernel, filt, panel),
            [((low + high, LANES), BF16), sums, ((low + high, LANES), BF16), ((low, LANES), F32)],
            share, keep, small, edges,
            scratch=[flat],
        )
        third, second, first = (crossed(sends[k - 1], filt, k) for k in (3, 2, 1))
        send, plain = call(
            functools.partial(chips_kernel, filt), [((low + 2 * high, LANES), BF16), sums], kept, first, second, third,
            flops=4 * 10**9,
        )
        third, second, first = (crossed(plain if k == 2 else send, chip, k) for k in (3, 2, 1))
        (mine,) = call(
            functools.partial(total_kernel, axes),
            [((low + 4 * high, LANES), F32)],
            send, first, second, third,
            after=[output, far],
        )
    else:
        far = swap(far_out, space, 1)
        edges = edges_by_permutes(axes, edges).astype(F32)
        total, small = lax.psum((keep + share[-hidden_n:].astype(F32), small), (chip, filt))
        total = lax.dynamic_slice_in_dim(total, lax.axis_index(filt) * panel, panel, 0)
        mine = jnp.concatenate([total, small, edges], axis=0)
    other = swap(mine, core, 0)
    (back,) = call(
        functools.partial(back_kernel, core),
        [((rows * channels, width), F32)],
        dconv, share, far, cot_t, backward,
        scratch=[((tall * deep, width), BF16)],
        after=[mine],
    )
    factor = 1.0 / math.sqrt(tokens * chip_n * core_n * filt_n)
    line = ((1, channels), F32)
    matrix = ((panel, channels), F32)
    image_grad, kg, dwb, gain, lnb, ge, eb, gr, rb, sc = call(
        functools.partial(finish_kernel, factor, core),
        [
            ((channels, rows, width), BF16),
            ((SIDE, SIDE, channels), F32),
            line, line, line, matrix, ((1, panel), F32), matrix, line, line,
        ],
        mine, other, back, taps,
        scratch=[((2 * HALO, 16, LANES), F32), ((edge_height(2 * rows), LANES), F32)],
    )
    flat = lambda v: v.reshape(-1)
    return (
        output, image_grad, jnp.transpose(kg, (2, 0, 1)),
        flat(dwb), flat(gain), flat(lnb), ge, flat(eb), gr, flat(rb), flat(sc),
    )


def solution(mesh):
    space, filt = mesh.devices.shape
    axes = ("chip", "core", "filt")
    pairs = Mesh(mesh.devices.reshape(space // 2, 2, filt), axes)
    pixels = P(None, ("chip", "core"), "filt")
    whole, shard = P(), P("filt")
    return jax.shard_map(
        functools.partial(shards, axes),
        mesh=pairs,
        in_specs=(pixels, pixels) + (whole,) * 9,
        out_specs=(pixels, pixels, whole, whole, whole, whole, shard, shard, shard, whole, whole),
        check_vma=False,
    )
```

```python
import functools
import math

import jax
import jax.numpy as jnp
from jax import lax
from jax.experimental import pallas as pl
from jax.experimental.pallas import tpu as pltpu
from jax.sharding import Mesh, PartitionSpec as P

F32 = jnp.float32
BF16 = jnp.bfloat16
SIDE = 7
HALO = 3
LANES = 128
GROUP = 32
DEEP = SIDE * GROUP
NT = (((1,), (1,)), ((), ()))
VECTORS = ("dwb", "gain", "lnb", "rb", "scale")


def iota(shape, dim):
    return lax.broadcasted_iota(jnp.int32, shape, dim)


def dot(a, b, dims=(((1,), (0,)), ((), ()))):
    return lax.dot_general(a, b, dims, preferred_element_type=F32)


def column(row):
    n = row.shape[1]
    eye = iota((n, n), 0) == iota((n, n), 1)
    return jnp.sum(jnp.where(eye, row, 0.0), axis=1, keepdims=True)


def widened(value):
    fill = jnp.zeros((value.shape[0], LANES - value.shape[1]), value.dtype)
    return jnp.concatenate([value, fill], axis=1)


def edge_height(rows):
    return -(-HALO * rows // 16) * 16


def pack_edges(rows):
    count = len(rows)
    width, high = rows[0].shape[1], edge_height(count)
    q, j = iota((2 * high, width), 0), iota((2 * high, width), 1)
    total = None
    for i, row in enumerate(rows):
        last = (q == count * (j - (width - HALO)) + i) & (j >= width - HALO)
        first = (q == high + count * j + i) & (j < HALO)
        pick = jnp.where(last | first, 1.0, 0.0).astype(BF16)
        part = dot(pick, row, NT)
        total = part if total is None else total + part
    return total.astype(BF16)


def halo_tile(edges_t, i, count):
    high = edges_t.shape[1] // 2
    q, l = iota((2 * high, LANES), 0), iota((2 * high, LANES), 1)
    left = (q == count * (l - (LANES - HALO)) + i) & (l >= LANES - HALO)
    right = (q == high + count * l + i) & (l < HALO)
    pick = jnp.where(left | right, 1.0, 0.0).astype(BF16)
    return dot(edges_t, pick).astype(BF16)


def group_diagonal():
    lane = iota((1, DEEP), 1)
    inner = lane
    for b in range(1, SIDE):
        inner = jnp.where(lane >= b * GROUP, lane - b * GROUP, inner)
    return inner == iota((GROUP, DEEP), 0)


def tap_matrices(taps_ref, line_ref, w_ref, flip):
    diagonal = group_diagonal()
    for g in range(w_ref.shape[0]):
        for b in range(SIDE):
            piece = taps_ref[:, SIDE - 1 - b if flip else b, g * GROUP : (g + 1) * GROUP]
            line_ref[0:SIDE, b * GROUP : (b + 1) * GROUP] = piece
        for m in range(SIDE):
            a = m if flip else SIDE - 1 - m
            w_ref[g, m * GROUP : (m + 1) * GROUP, :] = jnp.where(diagonal, line_ref[a : a + 1, :], 0.0).astype(BF16)


def shifted(x, amount):
    return x if amount % x.shape[1] == 0 else pltpu.roll(x, amount % x.shape[1], 1)


def spread(xs_ref, r, x):
    channels = x.shape[0]
    width = xs_ref.shape[1]
    for b in range(SIDE):
        moved = shifted(x, HALO - b)[:, :width]
        for g in range(channels // GROUP):
            at = r * SIDE * channels + g * DEEP + b * GROUP
            xs_ref[at : at + GROUP, :] = moved[g * GROUP : (g + 1) * GROUP]


def depthwise(w_ref, xs_ref, acc_ref, rows, taken, before_ref=None):
    groups = w_ref.shape[0]
    channels = groups * GROUP
    for g in range(groups):
        at = [slice(i * channels + g * GROUP, i * channels + (g + 1) * GROUP) for i in range(rows)]
        sums = [None if before_ref is None else before_ref[at[i], :] for i in range(rows)]
        for k, r in enumerate(taken):
            i0, i1 = max(0, r - (SIDE - 1)), min(rows - 1, r)
            m0 = SIDE - 1 - r + i0
            low = k * SIDE * channels + g * DEEP
            part = dot(w_ref[g, m0 * GROUP : (m0 + i1 - i0 + 1) * GROUP, :], xs_ref[low : low + DEEP, :])
            for i in range(i0, i1 + 1):
                piece = part[(i - i0) * GROUP : (i - i0 + 1) * GROUP]
                sums[i] = piece if sums[i] is None else sums[i] + piece
        for i in range(rows):
            acc_ref[at[i], :] = sums[i]


def own_rows_kernel(mid_ref, own_ref, w_ref, acc_ref, x_ref, xs_ref):
    rows, channels, _ = mid_ref.shape
    edges_t = own_ref[:, 0:channels].T
    for i in range(rows):
        x = jnp.concatenate([mid_ref[i], halo_tile(edges_t, i, rows)], axis=1)
        x_ref[i] = x
        spread(xs_ref, i, x)
    depthwise(w_ref, xs_ref, acc_ref, rows, range(HALO, HALO + rows))


def edges_kernel(axis, mid_ref, second_ref, first_ref):
    edges = pack_edges([mid_ref[i] for i in range(mid_ref.shape[0])])
    high = edges.shape[0] // 2
    even = lax.rem(lax.axis_index(axis), 2) == 0
    first_ref[...] = jnp.where(even, edges[:high], edges[high:])
    second_ref[...] = jnp.where(even, edges[high:], edges[:high])


def far_kernel(axes, mid_ref, second_ref, first_ref, own_ref, far_ref):
    even = lax.rem(lax.axis_index(axes[2]), 2) == 0
    first, second = first_ref[...], second_ref[...]
    edges = jnp.concatenate([jnp.where(even, second, first), jnp.where(even, first, second)], axis=0)
    own_ref[...] = widened(edges)
    put_strips(mid_ref, own_ref, far_ref, lax.axis_index(axes[1]))


def pair_kernel(core_axis, mid_ref, own_ref, pair_ref):
    put_strips(mid_ref, own_ref, pair_ref, 1 - lax.axis_index(core_axis))


def put_strips(mid_ref, edges_ref, to_ref, last):
    for k in range(HALO):
        put_strip(to_ref, k, mid_ref[k + (mid_ref.shape[0] - HALO) * last])
    to_ref[to_ref.shape[0] - edges_ref.shape[0] :, :] = edges_ref[...]


def put_strip(ref, k, row):
    channels, width = row.shape
    parts = width // LANES
    for p in range(parts):
        ref[(k * parts + p) * channels : (k * parts + p + 1) * channels, :] = row[:, p * LANES : (p + 1) * LANES]


def get_strip(ref, k, channels, width):
    parts = width // LANES
    pieces = [ref[(k * parts + p) * channels : (k * parts + p + 1) * channels, :] for p in range(parts)]
    return jnp.concatenate(pieces, axis=1)


def prepare_kernel(
    cot_ref, taps_ref, dwb_ref, gain_ref, lnb_ref, we_ref, be_ref, wr_ref, br_ref, scale_ref,
    cot_t_ref, forward_ref, backward_ref, we2_ref, wr2_ref, columns_ref, lift_ref, line_ref,
):
    for i in range(cot_t_ref.shape[0]):
        cot_t_ref[i] = cot_ref[:, i, :]
    tap_matrices(taps_ref, line_ref, forward_ref, False)
    tap_matrices(taps_ref, line_ref, backward_ref, True)
    channels, hidden_n = we_ref.shape
    extra = lift_ref.shape[0] - channels
    lift_ref[0:channels, :] = we_ref[...]
    lift_ref[channels:, :] = jnp.where(iota((extra, hidden_n), 0) == 0, be_ref[...].astype(F32), 0.0).astype(BF16)
    we2_ref[...] = lift_ref[...].T
    wr2_ref[...] = wr_ref[...].T
    lane = iota(columns_ref.shape, 1)
    total = jnp.zeros(columns_ref.shape, F32)
    for k, ref in enumerate((dwb_ref, gain_ref, lnb_ref, br_ref, scale_ref)):
        total = jnp.where(lane == k, column(ref[...]), total)
    columns_ref[...] = total


def gelu_parts(v):
    z = jnp.abs(v)
    t = 1.0 / (1.0 + (0.3275911 / math.sqrt(2.0)) * z)
    e = jnp.exp2((-0.5 * math.log2(math.e)) * (v * v))
    half = 0.5
    poly = t * (
        half * 0.254829592
        + t * (half * -0.284496736 + t * (half * 1.421413741 + t * (half * -1.453152027 + t * (half * 1.061405429))))
    )
    tail = poly * e
    return jnp.where(v >= 0.0, 1.0 - tail, tail), (v * (1.0 / math.sqrt(2.0 * math.pi))) * e


def main_kernel(
    axes,
    mid_ref, pair_ref, beyond_ref, own_ref, before_ref, cot_ref, w_ref, we_ref, wr_ref, we2_ref, wr2_ref, columns_ref, scale_ref,
    out_ref, dconv_ref, far_ref, x_ref, vectors_ref, share_ref, keep_ref,
    xs_ref, acc_ref, xhat_ref, nm_ref, db_ref, act_ref, dh_ref,
):
    rows, channels, width = cot_ref.shape
    hidden_n = we_ref.shape[1]
    core = lax.axis_index(axes[1])
    dwb, gain, lnb, br, scale = (columns_ref[:, k : k + 1] for k in range(5))
    lead = HALO * channels * (width // LANES)
    upper = core == 0
    high = own_ref.shape[0]
    near, beyond = (ref[ref.shape[0] - high :, 0:channels].T for ref in (pair_ref, beyond_ref))
    above, below = jnp.where(upper, beyond, near), jnp.where(upper, near, beyond)
    for k in range(HALO):
        pair, far = (get_strip(ref, k, channels, width) for ref in (pair_ref, beyond_ref))
        up, down = jnp.where(upper, far, pair), jnp.where(upper, pair, far)
        up = jnp.concatenate([up, halo_tile(above, rows - HALO + k, rows)], axis=1)
        down = jnp.concatenate([down, halo_tile(below, k, rows)], axis=1)
        x_ref[k] = up
        x_ref[HALO + k] = down
        spread(xs_ref, k, up)
        spread(xs_ref, HALO + k, down)
    taken = [*range(HALO), *range(HALO + rows, rows + 2 * HALO)]
    depthwise(w_ref, xs_ref, acc_ref, rows, taken, before_ref)
    extra = nm_ref.shape[0] - channels
    nm_ref[channels:, :] = jnp.where(iota((extra, rows * width), 0) == 0, 1.0, 0.0).astype(BF16)
    zero = jnp.zeros((channels, LANES), F32)
    sums = {k: zero for k in VECTORS}

    def add(name, value):
        for k in range(0, width, LANES):
            sums[name] = sums[name] + value[:, k : k + LANES]

    chunk = 128
    for i in range(rows):
        cols = slice(i * width, (i + 1) * width)
        conv = acc_ref[i * channels : (i + 1) * channels, :] + dwb
        conv = conv - jnp.mean(conv, axis=0, keepdims=True)
        inv = lax.rsqrt(jnp.mean(conv * conv, axis=0, keepdims=True) + 1e-6)
        xhat = conv * inv
        xhat_ref[...] = xhat
        nm_ref[0:channels, cols] = (xhat * gain + lnb).astype(BF16)
        cot = cot_ref[i].astype(F32)
        add("rb", cot)
        db_ref[:, cols] = (cot * scale).astype(BF16)
        for h0 in range(0, hidden_n, chunk):
            hs = slice(h0, h0 + chunk)
            hidden = dot(we2_ref[hs, :], nm_ref[:, cols])
            back = dot(wr2_ref[hs, :], db_ref[:, cols])
            phi, bump = gelu_parts(hidden)
            act_ref[hs, cols] = (hidden * phi).astype(BF16)
            dh_ref[hs, cols] = (back * (phi + bump)).astype(BF16)
        branch = dot(wr_ref[...], act_ref[:, cols]) + br
        out_ref[i] = (mid_ref[i].astype(F32) + scale * branch).astype(BF16)
        add("scale", cot * branch)
        d_normed = dot(we_ref[...], dh_ref[:, cols])
        xhat = xhat_ref[...]
        add("lnb", d_normed)
        add("gain", d_normed * xhat)
        d_xhat = d_normed * gain
        m1 = jnp.mean(d_xhat, axis=0, keepdims=True)
        m2 = jnp.mean(d_xhat * xhat, axis=0, keepdims=True)
        dconv = (inv * (d_xhat - m1 - xhat * m2)).astype(BF16)
        add("dwb", dconv.astype(F32))
        dconv_ref[i] = dconv
    for k in range(HALO):
        put_strip(share_ref, k, dconv_ref[k + (rows - HALO) * (1 - core)])
        far_ref[k] = dconv_ref[k + (rows - HALO) * core]
    g_reduce = widened(dot(act_ref[...], db_ref[...], NT))
    g_expand = widened(dot(dh_ref[...], nm_ref[...], NT))
    keep_ref[...] = jnp.where(core == 0, g_reduce, g_expand)
    share_ref[lead:, :] = jnp.where(core == 0, g_expand, g_reduce).astype(BF16)
    vectors_ref[...] = jnp.zeros_like(vectors_ref)
    for b, name in enumerate(VECTORS):
        total = jnp.sum(sums[name].T, axis=0, keepdims=True)
        vectors_ref[b : b + 1, 0:channels] = total * scale_ref[...] if name == "rb" else total


def depthwise_gradient_kernel(x_ref, own_x_ref, dconv_ref, vectors_ref, edges_ref, small_ref, wide_ref, dcs_ref, line_ref):
    rows, channels, width = dconv_ref.shape
    groups = channels // GROUP
    extent = width + LANES
    edges_ref[...] = widened(pack_edges([dconv_ref[i] for i in range(rows)]))
    for i in range(rows):
        padded = jnp.concatenate([dconv_ref[i], jnp.zeros((channels, LANES), BF16)], axis=1)
        columns = slice(i * extent, (i + 1) * extent)
        for b in range(SIDE):
            moved = shifted(padded, b - HALO)
            for g in range(groups):
                at = g * DEEP + b * GROUP
                dcs_ref[at : at + GROUP, columns] = moved[g * GROUP : (g + 1) * GROUP]
        for a in range(SIDE):
            r = i + a
            if HALO <= r < HALO + rows:
                x = own_x_ref[r - HALO]
            else:
                x = x_ref[r if r < HALO else r - rows]
            for g in range(groups):
                at = g * DEEP + a * GROUP
                wide_ref[at : at + GROUP, columns] = x[g * GROUP : (g + 1) * GROUP, :]
    small_ref[...] = jnp.zeros_like(small_ref)
    diagonal = group_diagonal()
    for g in range(groups):
        taps = dot(wide_ref[g * DEEP : (g + 1) * DEEP, :], dcs_ref[g * DEEP : (g + 1) * DEEP, :], NT)
        for a in range(SIDE):
            part = jnp.where(diagonal, taps[a * GROUP : (a + 1) * GROUP, :], 0.0)
            line_ref[a : a + 1, :] = jnp.sum(part, axis=0, keepdims=True)
        for b in range(SIDE):
            small_ref[b * 8 : b * 8 + SIDE, g * GROUP : (g + 1) * GROUP] = line_ref[0:SIDE, b * GROUP : (b + 1) * GROUP]
    for b in range(len(VECTORS)):
        small_ref[b * 8 + SIDE : b * 8 + 8, :] = vectors_ref[b : b + 1, :]


def columns_kernel(axis, panel, share_ref, keep_ref, small_ref, edges_ref, *refs):
    *send_refs, kept_ref, total_ref = refs
    f = lax.axis_index(axis)
    count = total_ref.shape[0]
    total_ref[...] = keep_ref[...] + share_ref[share_ref.shape[0] - count :, :].astype(F32)
    part = lambda k: total_ref[pl.ds(pl.multiple_of(k * panel, 8), panel), :]
    tail = small_ref[...].astype(BF16)
    small = tail.shape[0]
    high = edges_ref.shape[0] // 2
    for mate, send_ref in zip(mates(f), send_refs):
        send_ref[0:panel, :] = part(mate).astype(BF16)
        send_ref[panel : panel + small, :] = tail
        if send_ref.shape[0] > panel + small:
            send_ref[panel + small :, :] = jnp.where(mate > f, edges_ref[:high, :], edges_ref[high:, :])
    kept_ref[0:panel, :] = part(f)
    kept_ref[panel:, :] = tail.astype(F32)


def mates(index):
    low = 1 - 2 * lax.rem(index, 2)
    high = jnp.where(index < 2, 2, -2)
    return index + low, index + high, index + low + high


def four_sums(mine, parts):
    first, second, third = (part.astype(F32) for part in parts)
    return (mine + first) + (second + third)


def chips_kernel(axis, third_ref, second_ref, first_ref, kept_ref, send_ref, plain_ref):
    f = lax.axis_index(axis)
    even = lax.rem(f, 2) == 0
    count = kept_ref.shape[0]
    total = four_sums(kept_ref[...], [ref[0:count, :] for ref in (first_ref, second_ref, third_ref)]).astype(BF16)
    near, far = first_ref[count:, :], third_ref[count:, :]
    far = jnp.where((f == 0) | (f == lax.axis_size(axis) - 1), jnp.zeros_like(far), far)
    edges = [jnp.where(even, far, near), jnp.where(even, near, far)]
    plain_ref[...] = total
    send_ref[...] = jnp.concatenate([total, *edges], axis=0)


def total_kernel(axes, third_ref, second_ref, first_ref, mine_ref, total_ref):
    q, core = lax.axis_index(axes[0]), lax.axis_index(axes[1])
    count = second_ref.shape[0]
    wide = mine_ref.shape[0] - count
    mine = mine_ref[0:count, :].astype(F32)
    total_ref[0:count, :] = four_sums(mine, [ref[0:count, :] for ref in (first_ref, second_ref, third_ref)])
    total_ref[count : count + wide, :] = mine_ref[count:, :].astype(F32)
    other = q + 1 - 2 * core
    beside = lax.rem(q + core, 2) == 0
    value = jnp.where(beside, first_ref[count:, :], third_ref[count:, :]).astype(F32)
    total_ref[count + wide :, :] = jnp.where((other >= 0) & (other < lax.axis_size(axes[0])), value, 0.0)


def back_kernel(core_axis, mid_ref, share_ref, far_ref, cot_ref, w_ref, acc_ref, xs_ref):
    rows, channels, width = cot_ref.shape
    upper = lax.axis_index(core_axis) == 0
    nothing = jnp.zeros((channels, LANES), BF16)
    put = lambda r, x: spread(xs_ref, r, jnp.concatenate([x, nothing], axis=1))
    for k in range(HALO):
        pair, far = get_strip(share_ref, k, channels, width), far_ref[k]
        put(k, jnp.where(upper, far, pair))
        put(HALO + rows + k, jnp.where(upper, pair, far))
    for i in range(rows):
        put(HALO + i, mid_ref[i])
    depthwise(w_ref, xs_ref, acc_ref, rows, range(rows + 2 * HALO))
    for i in range(rows):
        acc_ref[i * channels : (i + 1) * channels, :] += cot_ref[i].astype(F32)


def finish_kernel(
    factor, core_axis, mine_ref, other_ref, acc_ref, taps_ref,
    back_ref, kg_ref, dwb_ref, gain_ref, lnb_ref, ge_ref, eb_ref, gr_ref, rb_ref, sc_ref, ends_ref, side_ref,
):
    channels = kg_ref.shape[2]
    panel = gr_ref.shape[0]
    core = lax.axis_index(core_axis)
    rows, width = back_ref.shape[1:]
    high = edge_height(rows)
    low = mine_ref.shape[0] - 4 * high
    own, near, beyond = mine_ref[low : low + 2 * high, :], other_ref[low : low + 2 * high, :], other_ref[low + 2 * high :, :]
    above, below = jnp.where(core == 0, beyond, near), jnp.where(core == 0, near, beyond)
    for side in range(2):
        for k in range(HALO):
            at = side * high + k * rows
            ends_ref[side * HALO + k, 0:HALO, :] = above[at + rows - HALO : at + rows]
            ends_ref[side * HALO + k, HALO : HALO + rows, :] = own[at : at + rows]
            ends_ref[side * HALO + k, HALO + rows : 2 * HALO + rows, :] = below[at : at + HALO]
    side_ref[...] = jnp.zeros_like(side_ref)
    taps = [taps_ref[a] for a in range(SIDE)]
    for side in range(2):
        for j in range(HALO):
            total = None
            for k in range(HALO):
                b = k + side * (SIDE - 1) - j
                if not 0 <= b < SIDE:
                    continue
                for a in range(SIDE):
                    tap = taps[SIDE - 1 - a][SIDE - 1 - b : SIDE - b]
                    part = tap * ends_ref[side * HALO + k, a : a + rows, 0:channels]
                    total = part if total is None else total + part
            at = (side * HALO + j) * rows
            side_ref[at : at + rows, 0:channels] = total
    side = side_ref[...]
    upper = side.astype(BF16)
    lower = (side - upper.astype(F32)).astype(BF16)
    side_t = jnp.concatenate([upper, lower], axis=0).T
    count = side_ref.shape[0]
    q, l = iota((2 * count, LANES), 0), iota((2 * count, LANES), 1)
    q = jnp.where(q >= count, q - count, q)
    for i in range(rows):
        first = (q == l * rows + i) & (l < HALO)
        last = (q == (HALO + l - (LANES - HALO)) * rows + i) & (l >= LANES - HALO)
        extra = [dot(side_t, jnp.where(at, 1.0, 0.0).astype(BF16))[0:channels] for at in (first, last)]
        value = acc_ref[i * channels : (i + 1) * channels, :]
        tiles = [value[:, k : k + LANES] for k in range(0, width, LANES)]
        tiles[0] = tiles[0] + extra[0]
        tiles[-1] = tiles[-1] + extra[1]
        back_ref[:, i, :] = jnp.concatenate(tiles, axis=1).astype(BF16)
    mine, other = mine_ref[0:low, :] * factor, other_ref[0:low, :] * factor
    low, high = jnp.where(core == 0, mine, other), jnp.where(core == 0, other, mine)
    small = mine[panel:] + other[panel:]
    for b in range(SIDE):
        kg_ref[:, b, :] = small[b * 8 : b * 8 + SIDE, 0:channels]
    for b, ref in enumerate((dwb_ref, gain_ref, lnb_ref, rb_ref, sc_ref)):
        ref[...] = small[b * 8 + SIDE : b * 8 + 8, 0:channels]
    gr_ref[...] = low[0:panel, 0:channels]
    ge_ref[...] = high[0:panel, 0:channels]
    eye = iota((panel, panel), 0) == iota((panel, panel), 1)
    eb_ref[...] = jnp.sum(jnp.where(eye, high[0:panel, channels : channels + 1], 0.0), axis=0, keepdims=True)


def call(kernel, outs, *args, scratch=(), after=(), flops=0):
    size = sum(math.prod(a.shape) * a.dtype.itemsize for a in args)
    size += sum(math.prod(s) * jnp.dtype(d).itemsize for s, d in outs)
    count = len(args)

    def body(*refs):
        kernel(*refs[:count], *refs[count + len(after) :])

    in_vmem = pl.BlockSpec(memory_space=pltpu.VMEM)
    anywhere = pl.BlockSpec(memory_space=pl.ANY)
    return pl.pallas_call(
        body,
        out_shape=[jax.ShapeDtypeStruct(s, d) for s, d in outs],
        in_specs=[in_vmem] * count + [anywhere] * len(after),
        out_specs=[in_vmem] * len(outs),
        scratch_shapes=[pltpu.VMEM(s, d) for s, d in scratch],
        compiler_params=pltpu.CompilerParams(vmem_limit_bytes=40 * 2**20),
        cost_estimate=pl.CostEstimate(flops=flops, bytes_accessed=size, transcendentals=0),
    )(*args, *after)


def swap(x, axis, parity):
    size = lax.axis_size(axis)
    pairs = [(i, i + 1) for i in range(parity, size - 1, 2)]
    return lax.ppermute(x, axis, pairs + [(j, i) for i, j in pairs])


def crossed(x, axis, bits):
    return lax.ppermute(x, axis, [(i, i ^ bits) for i in range(lax.axis_size(axis))])


def edges_by_permutes(axes, edges):
    chip, core, filt = axes
    count = lax.axis_size(filt)
    right = [(i, i + 1) for i in range(count - 1)]
    left = [(j, i) for i, j in right]
    high = edges.shape[0] // 2
    own = jnp.concatenate([lax.ppermute(edges[:high], filt, right), lax.ppermute(edges[high:], filt, left)], axis=0)
    return jnp.concatenate([own, swap(swap(own, (chip, core), 1), core, 0)], axis=0)


def shards(
    axes, image, cotangent, kernel, dw_bias, layer_norm_gain, layer_norm_bias,
    w_expand, b_expand, w_reduce, b_reduce, layer_scale,
):
    chip, core, filt = axes
    chip_n, core_n, filt_n = (lax.axis_size(a) for a in axes)
    channels, rows, width = image.shape
    hidden_n = w_expand.shape[0]
    groups = channels // GROUP
    panel = hidden_n // filt_n
    tall = rows + 2 * HALO
    deep = SIDE * channels
    extent = width + LANES
    tokens = rows * width
    lift = channels + 16
    direct = chip_n == 4 and filt_n == 4
    strip = ((HALO, channels, width), BF16)
    block = ((rows, channels, width), BF16)
    high = edge_height(rows)
    edge = ((2 * high, LANES), BF16)
    row = lambda v: v.reshape(1, -1)

    space = (chip, core)
    lead = HALO * channels * (width // LANES)
    mid = jnp.transpose(image, (1, 0, 2))
    ends = ((high, channels), BF16)
    lead = HALO * channels * (width // LANES)
    flat_strip = ((lead + 2 * high, LANES), BF16)
    second, first = call(functools.partial(edges_kernel, filt), [ends, ends], mid)
    second, first = swap(second, filt, 1), swap(first, filt, 0)
    own, far = call(functools.partial(far_kernel, axes), [edge, flat_strip], mid, second, first)
    far = swap(far, space, 1)
    we_t, wr_t = w_expand.T, w_reduce.T
    taps = jnp.transpose(kernel, (1, 2, 0))
    cot_t, forward, backward, we2, wr2, columns = call(
        prepare_kernel,
        [
            block,
            ((groups, DEEP, DEEP), BF16),
            ((groups, DEEP, DEEP), BF16),
            ((hidden_n, lift), BF16),
            ((hidden_n, channels), BF16),
            ((channels, LANES), F32),
        ],
        cotangent, taps, row(dw_bias), row(layer_norm_gain), row(layer_norm_bias),
        we_t, row(b_expand), wr_t, row(b_reduce), row(layer_scale),
        scratch=[((lift, hidden_n), BF16), ((16, DEEP), F32)],
        after=[own],
    )
    (pair,) = call(functools.partial(pair_kernel, core), [flat_strip], mid, own, after=[columns])
    pair = swap(pair, core, 0)
    before, own_x = call(
        own_rows_kernel,
        [((rows * channels, width), F32), ((rows, channels, extent), BF16)],
        mid, own, forward,
        scratch=[((rows * deep, width), BF16)],
    )
    small_n = 64
    flat = ((hidden_n, LANES), F32)
    out_t, dconv, far_out, x, vectors, share, keep = call(
        functools.partial(main_kernel, axes),
        [
            block, block, strip, ((2 * HALO, channels, extent), BF16), ((16, LANES), F32),
            ((HALO * channels * (width // LANES) + hidden_n, LANES), BF16), flat,
        ],
        mid, pair, far, own, before, cot_t, forward, we_t, wr_t, we2, wr2, columns, row(layer_scale),
        scratch=[
            ((2 * HALO * deep, width), BF16),
            ((rows * channels, width), F32),
            ((channels, width), F32),
            ((lift, tokens), BF16),
            ((channels, tokens), BF16),
            ((hidden_n, tokens), BF16),
            ((hidden_n, tokens), BF16),
        ],
    )
    output = jnp.transpose(out_t, (1, 0, 2))
    edges, small = call(
        depthwise_gradient_kernel,
        [edge, ((small_n, LANES), F32)],
        x, own_x, dconv, vectors,
        scratch=[((deep, rows * extent), BF16), ((deep, rows * extent), BF16), ((16, DEEP), F32)],
    )
    share = swap(share, core, 0)
    far = swap(far_out, space, 1) if direct else None
    low = panel + small_n
    if direct:
        sums = ((low, LANES), BF16)
        *sends, kept = call(
            functools.partial(columns_kernel, filt, panel),
            [((low + high, LANES), BF16), sums, ((low + high, LANES), BF16), ((low, LANES), F32)],
            share, keep, small, edges,
            scratch=[flat],
        )
        third, second, first = (crossed(sends[k - 1], filt, k) for k in (3, 2, 1))
        send, plain = call(
            functools.partial(chips_kernel, filt), [((low + 2 * high, LANES), BF16), sums], third, second, first, kept,
            flops=4 * 10**9,
        )
        third, second, first = (crossed(plain if k == 2 else send, chip, k) for k in (3, 2, 1))
        (mine,) = call(
            functools.partial(total_kernel, axes),
            [((low + 4 * high, LANES), F32)],
            third, second, first, send,
            after=[output, far],
        )
    else:
        far = swap(far_out, space, 1)
        edges = edges_by_permutes(axes, edges).astype(F32)
        total, small = lax.psum((keep + share[-hidden_n:].astype(F32), small), (chip, filt))
        total = lax.dynamic_slice_in_dim(total, lax.axis_index(filt) * panel, panel, 0)
        mine = jnp.concatenate([total, small, edges], axis=0)
    other = swap(mine, core, 0)
    (back,) = call(
        functools.partial(back_kernel, core),
        [((rows * channels, width), F32)],
        dconv, share, far, cot_t, backward,
        scratch=[((tall * deep, width), BF16)],
        after=[mine],
    )
    factor = 1.0 / math.sqrt(tokens * chip_n * core_n * filt_n)
    line = ((1, channels), F32)
    matrix = ((panel, channels), F32)
    image_grad, kg, dwb, gain, lnb, ge, eb, gr, rb, sc = call(
        functools.partial(finish_kernel, factor, core),
        [
            ((channels, rows, width), BF16),
            ((SIDE, SIDE, channels), F32),
            line, line, line, matrix, ((1, panel), F32), matrix, line, line,
        ],
        mine, other, back, taps,
        scratch=[((2 * HALO, 16, LANES), F32), ((edge_height(2 * rows), LANES), F32)],
    )
    flat = lambda v: v.reshape(-1)
    return (
        output, image_grad, jnp.transpose(kg, (2, 0, 1)),
        flat(dwb), flat(gain), flat(lnb), ge, flat(eb), gr, flat(rb), flat(sc),
    )


def solution(mesh):
    space, filt = mesh.devices.shape
    axes = ("chip", "core", "filt")
    pairs = Mesh(mesh.devices.reshape(space // 2, 2, filt), axes)
    pixels = P(None, ("chip", "core"), "filt")
    whole, shard = P(), P("filt")
    return jax.shard_map(
        functools.partial(shards, axes),
        mesh=pairs,
        in_specs=(pixels, pixels) + (whole,) * 9,
        out_specs=(pixels, pixels, whole, whole, whole, whole, shard, shard, shard, whole, whole),
        check_vma=False,
    )
```

```python
import functools
import math

import jax
import jax.numpy as jnp
from jax import lax
from jax.experimental import pallas as pl
from jax.experimental.pallas import tpu as pltpu
from jax.sharding import Mesh, PartitionSpec as P

F32 = jnp.float32
BF16 = jnp.bfloat16
SIDE = 7
HALO = 3
LANES = 128
GROUP = 32
DEEP = SIDE * GROUP
NT = (((1,), (1,)), ((), ()))
VECTORS = ("dwb", "gain", "lnb", "rb", "scale")


def iota(shape, dim):
    return lax.broadcasted_iota(jnp.int32, shape, dim)


def dot(a, b, dims=(((1,), (0,)), ((), ()))):
    return lax.dot_general(a, b, dims, preferred_element_type=F32)


def column(row):
    n = row.shape[1]
    eye = iota((n, n), 0) == iota((n, n), 1)
    return jnp.sum(jnp.where(eye, row, 0.0), axis=1, keepdims=True)


def widened(value):
    fill = jnp.zeros((value.shape[0], LANES - value.shape[1]), value.dtype)
    return jnp.concatenate([value, fill], axis=1)


def edge_height(rows):
    return -(-HALO * rows // 16) * 16


def pack_edges(rows):
    count = len(rows)
    width, high = rows[0].shape[1], edge_height(count)
    q, j = iota((2 * high, width), 0), iota((2 * high, width), 1)
    total = None
    for i, row in enumerate(rows):
        last = (q == count * (j - (width - HALO)) + i) & (j >= width - HALO)
        first = (q == high + count * j + i) & (j < HALO)
        pick = jnp.where(last | first, 1.0, 0.0).astype(BF16)
        part = dot(pick, row, NT)
        total = part if total is None else total + part
    return total.astype(BF16)


def halo_tile(edges_t, i, count):
    high = edges_t.shape[1] // 2
    q, l = iota((2 * high, LANES), 0), iota((2 * high, LANES), 1)
    left = (q == count * (l - (LANES - HALO)) + i) & (l >= LANES - HALO)
    right = (q == high + count * l + i) & (l < HALO)
    pick = jnp.where(left | right, 1.0, 0.0).astype(BF16)
    return dot(edges_t, pick).astype(BF16)


def group_diagonal():
    lane = iota((1, DEEP), 1)
    inner = lane
    for b in range(1, SIDE):
        inner = jnp.where(lane >= b * GROUP, lane - b * GROUP, inner)
    return inner == iota((GROUP, DEEP), 0)


def tap_matrices(taps_ref, line_ref, w_ref, flip):
    diagonal = group_diagonal()
    for g in range(w_ref.shape[0]):
        for b in range(SIDE):
            piece = taps_ref[:, SIDE - 1 - b if flip else b, g * GROUP : (g + 1) * GROUP]
            line_ref[0:SIDE, b * GROUP : (b + 1) * GROUP] = piece
        for m in range(SIDE):
            a = m if flip else SIDE - 1 - m
            w_ref[g, m * GROUP : (m + 1) * GROUP, :] = jnp.where(diagonal, line_ref[a : a + 1, :], 0.0).astype(BF16)


def shifted(x, amount):
    return x if amount % x.shape[1] == 0 else pltpu.roll(x, amount % x.shape[1], 1)


def spread(xs_ref, r, x):
    channels = x.shape[0]
    width = xs_ref.shape[1]
    for b in range(SIDE):
        moved = shifted(x, HALO - b)[:, :width]
        for g in range(channels // GROUP):
            at = r * SIDE * channels + g * DEEP + b * GROUP
            xs_ref[at : at + GROUP, :] = moved[g * GROUP : (g + 1) * GROUP]


def depthwise(w_ref, xs_ref, acc_ref, rows, taken, before_ref=None):
    groups = w_ref.shape[0]
    channels = groups * GROUP
    for g in range(groups):
        at = [slice(i * channels + g * GROUP, i * channels + (g + 1) * GROUP) for i in range(rows)]
        sums = [None if before_ref is None else before_ref[at[i], :] for i in range(rows)]
        for k, r in enumerate(taken):
            i0, i1 = max(0, r - (SIDE - 1)), min(rows - 1, r)
            m0 = SIDE - 1 - r + i0
            low = k * SIDE * channels + g * DEEP
            part = dot(w_ref[g, m0 * GROUP : (m0 + i1 - i0 + 1) * GROUP, :], xs_ref[low : low + DEEP, :])
            for i in range(i0, i1 + 1):
                piece = part[(i - i0) * GROUP : (i - i0 + 1) * GROUP]
                sums[i] = piece if sums[i] is None else sums[i] + piece
        for i in range(rows):
            acc_ref[at[i], :] = sums[i]


def own_rows_kernel(mid_ref, own_ref, w_ref, acc_ref, x_ref, xs_ref):
    rows, channels, _ = mid_ref.shape
    edges_t = own_ref[:, 0:channels].T
    for i in range(rows):
        x = jnp.concatenate([mid_ref[i], halo_tile(edges_t, i, rows)], axis=1)
        x_ref[i] = x
        spread(xs_ref, i, x)
    depthwise(w_ref, xs_ref, acc_ref, rows, range(HALO, HALO + rows))


def edges_kernel(axis, mid_ref, second_ref, first_ref):
    edges = pack_edges([mid_ref[i] for i in range(mid_ref.shape[0])])
    high = edges.shape[0] // 2
    even = lax.rem(lax.axis_index(axis), 2) == 0
    first_ref[...] = jnp.where(even, edges[:high], edges[high:])
    second_ref[...] = jnp.where(even, edges[high:], edges[:high])


def far_kernel(axes, mid_ref, second_ref, first_ref, own_ref, far_ref):
    even = lax.rem(lax.axis_index(axes[2]), 2) == 0
    first, second = first_ref[...], second_ref[...]
    edges = jnp.concatenate([jnp.where(even, second, first), jnp.where(even, first, second)], axis=0)
    own_ref[...] = widened(edges)
    put_strips(mid_ref, own_ref, far_ref, lax.axis_index(axes[1]))


def pair_kernel(core_axis, mid_ref, own_ref, pair_ref):
    put_strips(mid_ref, own_ref, pair_ref, 1 - lax.axis_index(core_axis))


def put_strips(mid_ref, edges_ref, to_ref, last):
    for k in range(HALO):
        put_strip(to_ref, k, mid_ref[k + (mid_ref.shape[0] - HALO) * last])
    to_ref[to_ref.shape[0] - edges_ref.shape[0] :, :] = edges_ref[...]


def put_strip(ref, k, row):
    channels, width = row.shape
    parts = width // LANES
    for p in range(parts):
        ref[(k * parts + p) * channels : (k * parts + p + 1) * channels, :] = row[:, p * LANES : (p + 1) * LANES]


def get_strip(ref, k, channels, width):
    parts = width // LANES
    pieces = [ref[(k * parts + p) * channels : (k * parts + p + 1) * channels, :] for p in range(parts)]
    return jnp.concatenate(pieces, axis=1)


def prepare_kernel(
    cot_ref, taps_ref, dwb_ref, gain_ref, lnb_ref, we_ref, be_ref, wr_ref, br_ref, scale_ref,
    cot_t_ref, forward_ref, backward_ref, we2_ref, wr2_ref, columns_ref, lift_ref, line_ref,
):
    for i in range(cot_t_ref.shape[0]):
        cot_t_ref[i] = cot_ref[:, i, :]
    tap_matrices(taps_ref, line_ref, forward_ref, False)
    tap_matrices(taps_ref, line_ref, backward_ref, True)
    channels, hidden_n = we_ref.shape
    extra = lift_ref.shape[0] - channels
    lift_ref[0:channels, :] = we_ref[...]
    lift_ref[channels:, :] = jnp.where(iota((extra, hidden_n), 0) == 0, be_ref[...].astype(F32), 0.0).astype(BF16)
    we2_ref[...] = lift_ref[...].T
    wr2_ref[...] = wr_ref[...].T
    lane = iota(columns_ref.shape, 1)
    total = jnp.zeros(columns_ref.shape, F32)
    for k, ref in enumerate((dwb_ref, gain_ref, lnb_ref, br_ref, scale_ref)):
        total = jnp.where(lane == k, column(ref[...]), total)
    columns_ref[...] = total


def gelu_parts(v):
    z = jnp.abs(v)
    t = 1.0 / (1.0 + (0.3275911 / math.sqrt(2.0)) * z)
    e = jnp.exp2((-0.5 * math.log2(math.e)) * (v * v))
    half = 0.5
    poly = t * (
        half * 0.254829592
        + t * (half * -0.284496736 + t * (half * 1.421413741 + t * (half * -1.453152027 + t * (half * 1.061405429))))
    )
    tail = poly * e
    return jnp.where(v >= 0.0, 1.0 - tail, tail), (v * (1.0 / math.sqrt(2.0 * math.pi))) * e


def main_kernel(
    axes,
    mid_ref, pair_ref, beyond_ref, own_ref, before_ref, cot_ref, w_ref, we_ref, wr_ref, we2_ref, wr2_ref, columns_ref, scale_ref,
    out_ref, dconv_ref, far_ref, x_ref, vectors_ref, share_ref, keep_ref,
    xs_ref, acc_ref, xhat_ref, nm_ref, db_ref, act_ref, dh_ref,
):
    rows, channels, width = cot_ref.shape
    hidden_n = we_ref.shape[1]
    core = lax.axis_index(axes[1])
    dwb, gain, lnb, br, scale = (columns_ref[:, k : k + 1] for k in range(5))
    lead = HALO * channels * (width // LANES)
    upper = core == 0
    high = own_ref.shape[0]
    near, beyond = (ref[ref.shape[0] - high :, 0:channels].T for ref in (pair_ref, beyond_ref))
    above, below = jnp.where(upper, beyond, near), jnp.where(upper, near, beyond)
    for k in range(HALO):
        pair, far = (get_strip(ref, k, channels, width) for ref in (pair_ref, beyond_ref))
        up, down = jnp.where(upper, far, pair), jnp.where(upper, pair, far)
        up = jnp.concatenate([up, halo_tile(above, rows - HALO + k, rows)], axis=1)
        down = jnp.concatenate([down, halo_tile(below, k, rows)], axis=1)
        x_ref[k] = up
        x_ref[HALO + k] = down
        spread(xs_ref, k, up)
        spread(xs_ref, HALO + k, down)
    taken = [*range(HALO), *range(HALO + rows, rows + 2 * HALO)]
    depthwise(w_ref, xs_ref, acc_ref, rows, taken, before_ref)
    extra = nm_ref.shape[0] - channels
    nm_ref[channels:, :] = jnp.where(iota((extra, rows * width), 0) == 0, 1.0, 0.0).astype(BF16)
    zero = jnp.zeros((channels, LANES), F32)
    sums = {k: zero for k in VECTORS}

    def add(name, value):
        for k in range(0, width, LANES):
            sums[name] = sums[name] + value[:, k : k + LANES]

    chunk = 128
    for i in range(rows):
        cols = slice(i * width, (i + 1) * width)
        conv = acc_ref[i * channels : (i + 1) * channels, :] + dwb
        conv = conv - jnp.mean(conv, axis=0, keepdims=True)
        inv = lax.rsqrt(jnp.mean(conv * conv, axis=0, keepdims=True) + 1e-6)
        xhat = conv * inv
        xhat_ref[...] = xhat
        nm_ref[0:channels, cols] = (xhat * gain + lnb).astype(BF16)
        cot = cot_ref[i].astype(F32)
        add("rb", cot)
        db_ref[:, cols] = (cot * scale).astype(BF16)
        for h0 in range(0, hidden_n, chunk):
            hs = slice(h0, h0 + chunk)
            hidden = dot(we2_ref[hs, :], nm_ref[:, cols])
            back = dot(wr2_ref[hs, :], db_ref[:, cols])
            phi, bump = gelu_parts(hidden)
            act_ref[hs, cols] = (hidden * phi).astype(BF16)
            dh_ref[hs, cols] = (back * (phi + bump)).astype(BF16)
        branch = dot(wr_ref[...], act_ref[:, cols]) + br
        out_ref[i] = (mid_ref[i].astype(F32) + scale * branch).astype(BF16)
        add("scale", cot * branch)
        d_normed = dot(we_ref[...], dh_ref[:, cols])
        xhat = xhat_ref[...]
        add("lnb", d_normed)
        add("gain", d_normed * xhat)
        d_xhat = d_normed * gain
        m1 = jnp.mean(d_xhat, axis=0, keepdims=True)
        m2 = jnp.mean(d_xhat * xhat, axis=0, keepdims=True)
        dconv = (inv * (d_xhat - m1 - xhat * m2)).astype(BF16)
        add("dwb", dconv.astype(F32))
        dconv_ref[i] = dconv
    for k in range(HALO):
        put_strip(share_ref, k, dconv_ref[k + (rows - HALO) * (1 - core)])
        far_ref[k] = dconv_ref[k + (rows - HALO) * core]
    g_reduce = widened(dot(act_ref[...], db_ref[...], NT))
    g_expand = widened(dot(dh_ref[...], nm_ref[...], NT))
    keep_ref[...] = jnp.where(core == 0, g_reduce, g_expand)
    share_ref[lead:, :] = jnp.where(core == 0, g_expand, g_reduce).astype(BF16)
    vectors_ref[...] = jnp.zeros_like(vectors_ref)
    for b, name in enumerate(VECTORS):
        total = jnp.sum(sums[name].T, axis=0, keepdims=True)
        vectors_ref[b : b + 1, 0:channels] = total * scale_ref[...] if name == "rb" else total


def depthwise_gradient_kernel(x_ref, own_x_ref, dconv_ref, vectors_ref, edges_ref, small_ref, wide_ref, dcs_ref, line_ref):
    rows, channels, width = dconv_ref.shape
    groups = channels // GROUP
    extent = width + LANES
    edges_ref[...] = widened(pack_edges([dconv_ref[i] for i in range(rows)]))
    for i in range(rows):
        padded = jnp.concatenate([dconv_ref[i], jnp.zeros((channels, LANES), BF16)], axis=1)
        columns = slice(i * extent, (i + 1) * extent)
        for b in range(SIDE):
            moved = shifted(padded, b - HALO)
            for g in range(groups):
                at = g * DEEP + b * GROUP
                dcs_ref[at : at + GROUP, columns] = moved[g * GROUP : (g + 1) * GROUP]
        for a in range(SIDE):
            r = i + a
            if HALO <= r < HALO + rows:
                x = own_x_ref[r - HALO]
            else:
                x = x_ref[r if r < HALO else r - rows]
            for g in range(groups):
                at = g * DEEP + a * GROUP
                wide_ref[at : at + GROUP, columns] = x[g * GROUP : (g + 1) * GROUP, :]
    small_ref[...] = jnp.zeros_like(small_ref)
    diagonal = group_diagonal()
    for g in range(groups):
        taps = dot(wide_ref[g * DEEP : (g + 1) * DEEP, :], dcs_ref[g * DEEP : (g + 1) * DEEP, :], NT)
        for a in range(SIDE):
            part = jnp.where(diagonal, taps[a * GROUP : (a + 1) * GROUP, :], 0.0)
            line_ref[a : a + 1, :] = jnp.sum(part, axis=0, keepdims=True)
        for b in range(SIDE):
            small_ref[b * 8 : b * 8 + SIDE, g * GROUP : (g + 1) * GROUP] = line_ref[0:SIDE, b * GROUP : (b + 1) * GROUP]
    for b in range(len(VECTORS)):
        small_ref[b * 8 + SIDE : b * 8 + 8, :] = vectors_ref[b : b + 1, :]


def columns_kernel(axis, panel, share_ref, keep_ref, small_ref, edges_ref, *refs):
    *send_refs, kept_ref, total_ref = refs
    f = lax.axis_index(axis)
    count = total_ref.shape[0]
    total_ref[...] = keep_ref[...] + share_ref[share_ref.shape[0] - count :, :].astype(F32)
    part = lambda k: total_ref[pl.ds(pl.multiple_of(k * panel, 8), panel), :]
    tail = small_ref[...].astype(BF16)
    small = tail.shape[0]
    high = edges_ref.shape[0] // 2
    for mate, send_ref in zip(mates(f), send_refs):
        send_ref[0:panel, :] = part(mate).astype(BF16)
        send_ref[panel : panel + small, :] = tail
        if send_ref.shape[0] > panel + small:
            send_ref[panel + small :, :] = jnp.where(mate > f, edges_ref[:high, :], edges_ref[high:, :])
    kept_ref[0:panel, :] = part(f)
    kept_ref[panel:, :] = tail.astype(F32)


def mates(index):
    low = 1 - 2 * lax.rem(index, 2)
    high = jnp.where(index < 2, 2, -2)
    return index + low, index + high, index + low + high


def four_sums(mine, parts):
    first, second, third = (part.astype(F32) for part in parts)
    return (mine + first) + (second + third)


def chips_kernel(axis, third_ref, second_ref, first_ref, kept_ref, send_ref, plain_ref):
    f = lax.axis_index(axis)
    even = lax.rem(f, 2) == 0
    count = kept_ref.shape[0]
    total = four_sums(kept_ref[...], [ref[0:count, :] for ref in (first_ref, second_ref, third_ref)]).astype(BF16)
    near, far = first_ref[count:, :], third_ref[count:, :]
    far = jnp.where((f == 0) | (f == lax.axis_size(axis) - 1), jnp.zeros_like(far), far)
    edges = [jnp.where(even, far, near), jnp.where(even, near, far)]
    plain_ref[...] = total
    send_ref[...] = jnp.concatenate([total, *edges], axis=0)


def total_kernel(axes, second_ref, third_ref, first_ref, mine_ref, total_ref):
    q, core = lax.axis_index(axes[0]), lax.axis_index(axes[1])
    count = second_ref.shape[0]
    wide = mine_ref.shape[0] - count
    mine = mine_ref[0:count, :].astype(F32)
    total_ref[0:count, :] = four_sums(mine, [ref[0:count, :] for ref in (first_ref, second_ref, third_ref)])
    total_ref[count : count + wide, :] = mine_ref[count:, :].astype(F32)
    other = q + 1 - 2 * core
    beside = lax.rem(q + core, 2) == 0
    value = jnp.where(beside, first_ref[count:, :], third_ref[count:, :]).astype(F32)
    total_ref[count + wide :, :] = jnp.where((other >= 0) & (other < lax.axis_size(axes[0])), value, 0.0)


def back_kernel(core_axis, mid_ref, share_ref, far_ref, cot_ref, w_ref, acc_ref, xs_ref):
    rows, channels, width = cot_ref.shape
    upper = lax.axis_index(core_axis) == 0
    nothing = jnp.zeros((channels, LANES), BF16)
    put = lambda r, x: spread(xs_ref, r, jnp.concatenate([x, nothing], axis=1))
    for k in range(HALO):
        pair, far = get_strip(share_ref, k, channels, width), far_ref[k]
        put(k, jnp.where(upper, far, pair))
        put(HALO + rows + k, jnp.where(upper, pair, far))
    for i in range(rows):
        put(HALO + i, mid_ref[i])
    depthwise(w_ref, xs_ref, acc_ref, rows, range(rows + 2 * HALO))
    for i in range(rows):
        acc_ref[i * channels : (i + 1) * channels, :] += cot_ref[i].astype(F32)


def finish_kernel(
    factor, core_axis, mine_ref, other_ref, acc_ref, taps_ref,
    back_ref, kg_ref, dwb_ref, gain_ref, lnb_ref, ge_ref, eb_ref, gr_ref, rb_ref, sc_ref, ends_ref, side_ref,
):
    channels = kg_ref.shape[2]
    panel = gr_ref.shape[0]
    core = lax.axis_index(core_axis)
    rows, width = back_ref.shape[1:]
    high = edge_height(rows)
    low = mine_ref.shape[0] - 4 * high
    own, near, beyond = mine_ref[low : low + 2 * high, :], other_ref[low : low + 2 * high, :], other_ref[low + 2 * high :, :]
    above, below = jnp.where(core == 0, beyond, near), jnp.where(core == 0, near, beyond)
    for side in range(2):
        for k in range(HALO):
            at = side * high + k * rows
            ends_ref[side * HALO + k, 0:HALO, :] = above[at + rows - HALO : at + rows]
            ends_ref[side * HALO + k, HALO : HALO + rows, :] = own[at : at + rows]
            ends_ref[side * HALO + k, HALO + rows : 2 * HALO + rows, :] = below[at : at + HALO]
    side_ref[...] = jnp.zeros_like(side_ref)
    taps = [taps_ref[a] for a in range(SIDE)]
    for side in range(2):
        for j in range(HALO):
            total = None
            for k in range(HALO):
                b = k + side * (SIDE - 1) - j
                if not 0 <= b < SIDE:
                    continue
                for a in range(SIDE):
                    tap = taps[SIDE - 1 - a][SIDE - 1 - b : SIDE - b]
                    part = tap * ends_ref[side * HALO + k, a : a + rows, 0:channels]
                    total = part if total is None else total + part
            at = (side * HALO + j) * rows
            side_ref[at : at + rows, 0:channels] = total
    side = side_ref[...]
    upper = side.astype(BF16)
    lower = (side - upper.astype(F32)).astype(BF16)
    side_t = jnp.concatenate([upper, lower], axis=0).T
    count = side_ref.shape[0]
    q, l = iota((2 * count, LANES), 0), iota((2 * count, LANES), 1)
    q = jnp.where(q >= count, q - count, q)
    for i in range(rows):
        first = (q == l * rows + i) & (l < HALO)
        last = (q == (HALO + l - (LANES - HALO)) * rows + i) & (l >= LANES - HALO)
        extra = [dot(side_t, jnp.where(at, 1.0, 0.0).astype(BF16))[0:channels] for at in (first, last)]
        value = acc_ref[i * channels : (i + 1) * channels, :]
        tiles = [value[:, k : k + LANES] for k in range(0, width, LANES)]
        tiles[0] = tiles[0] + extra[0]
        tiles[-1] = tiles[-1] + extra[1]
        back_ref[:, i, :] = jnp.concatenate(tiles, axis=1).astype(BF16)
    mine, other = mine_ref[0:low, :] * factor, other_ref[0:low, :] * factor
    low, high = jnp.where(core == 0, mine, other), jnp.where(core == 0, other, mine)
    small = mine[panel:] + other[panel:]
    for b in range(SIDE):
        kg_ref[:, b, :] = small[b * 8 : b * 8 + SIDE, 0:channels]
    for b, ref in enumerate((dwb_ref, gain_ref, lnb_ref, rb_ref, sc_ref)):
        ref[...] = small[b * 8 + SIDE : b * 8 + 8, 0:channels]
    gr_ref[...] = low[0:panel, 0:channels]
    ge_ref[...] = high[0:panel, 0:channels]
    eye = iota((panel, panel), 0) == iota((panel, panel), 1)
    eb_ref[...] = jnp.sum(jnp.where(eye, high[0:panel, channels : channels + 1], 0.0), axis=0, keepdims=True)


def call(kernel, outs, *args, scratch=(), after=(), flops=0):
    size = sum(math.prod(a.shape) * a.dtype.itemsize for a in args)
    size += sum(math.prod(s) * jnp.dtype(d).itemsize for s, d in outs)
    count = len(args)

    def body(*refs):
        kernel(*refs[:count], *refs[count + len(after) :])

    in_vmem = pl.BlockSpec(memory_space=pltpu.VMEM)
    anywhere = pl.BlockSpec(memory_space=pl.ANY)
    return pl.pallas_call(
        body,
        out_shape=[jax.ShapeDtypeStruct(s, d) for s, d in outs],
        in_specs=[in_vmem] * count + [anywhere] * len(after),
        out_specs=[in_vmem] * len(outs),
        scratch_shapes=[pltpu.VMEM(s, d) for s, d in scratch],
        compiler_params=pltpu.CompilerParams(vmem_limit_bytes=40 * 2**20),
        cost_estimate=pl.CostEstimate(flops=flops, bytes_accessed=size, transcendentals=0),
    )(*args, *after)


def swap(x, axis, parity):
    size = lax.axis_size(axis)
    pairs = [(i, i + 1) for i in range(parity, size - 1, 2)]
    return lax.ppermute(x, axis, pairs + [(j, i) for i, j in pairs])


def crossed(x, axis, bits):
    return lax.ppermute(x, axis, [(i, i ^ bits) for i in range(lax.axis_size(axis))])


def edges_by_permutes(axes, edges):
    chip, core, filt = axes
    count = lax.axis_size(filt)
    right = [(i, i + 1) for i in range(count - 1)]
    left = [(j, i) for i, j in right]
    high = edges.shape[0] // 2
    own = jnp.concatenate([lax.ppermute(edges[:high], filt, right), lax.ppermute(edges[high:], filt, left)], axis=0)
    return jnp.concatenate([own, swap(swap(own, (chip, core), 1), core, 0)], axis=0)


def shards(
    axes, image, cotangent, kernel, dw_bias, layer_norm_gain, layer_norm_bias,
    w_expand, b_expand, w_reduce, b_reduce, layer_scale,
):
    chip, core, filt = axes
    chip_n, core_n, filt_n = (lax.axis_size(a) for a in axes)
    channels, rows, width = image.shape
    hidden_n = w_expand.shape[0]
    groups = channels // GROUP
    panel = hidden_n // filt_n
    tall = rows + 2 * HALO
    deep = SIDE * channels
    extent = width + LANES
    tokens = rows * width
    lift = channels + 16
    direct = chip_n == 4 and filt_n == 4
    strip = ((HALO, channels, width), BF16)
    block = ((rows, channels, width), BF16)
    high = edge_height(rows)
    edge = ((2 * high, LANES), BF16)
    row = lambda v: v.reshape(1, -1)

    space = (chip, core)
    lead = HALO * channels * (width // LANES)
    mid = jnp.transpose(image, (1, 0, 2))
    ends = ((high, channels), BF16)
    lead = HALO * channels * (width // LANES)
    flat_strip = ((lead + 2 * high, LANES), BF16)
    second, first = call(functools.partial(edges_kernel, filt), [ends, ends], mid)
    second, first = swap(second, filt, 1), swap(first, filt, 0)
    own, far = call(functools.partial(far_kernel, axes), [edge, flat_strip], mid, second, first)
    far = swap(far, space, 1)
    we_t, wr_t = w_expand.T, w_reduce.T
    taps = jnp.transpose(kernel, (1, 2, 0))
    cot_t, forward, backward, we2, wr2, columns = call(
        prepare_kernel,
        [
            block,
            ((groups, DEEP, DEEP), BF16),
            ((groups, DEEP, DEEP), BF16),
            ((hidden_n, lift), BF16),
            ((hidden_n, channels), BF16),
            ((channels, LANES), F32),
        ],
        cotangent, taps, row(dw_bias), row(layer_norm_gain), row(layer_norm_bias),
        we_t, row(b_expand), wr_t, row(b_reduce), row(layer_scale),
        scratch=[((lift, hidden_n), BF16), ((16, DEEP), F32)],
        after=[own],
    )
    (pair,) = call(functools.partial(pair_kernel, core), [flat_strip], mid, own, after=[columns])
    pair = swap(pair, core, 0)
    before, own_x = call(
        own_rows_kernel,
        [((rows * channels, width), F32), ((rows, channels, extent), BF16)],
        mid, own, forward,
        scratch=[((rows * deep, width), BF16)],
    )
    small_n = 64
    flat = ((hidden_n, LANES), F32)
    out_t, dconv, far_out, x, vectors, share, keep = call(
        functools.partial(main_kernel, axes),
        [
            block, block, strip, ((2 * HALO, channels, extent), BF16), ((16, LANES), F32),
            ((HALO * channels * (width // LANES) + hidden_n, LANES), BF16), flat,
        ],
        mid, pair, far, own, before, cot_t, forward, we_t, wr_t, we2, wr2, columns, row(layer_scale),
        scratch=[
            ((2 * HALO * deep, width), BF16),
            ((rows * channels, width), F32),
            ((channels, width), F32),
            ((lift, tokens), BF16),
            ((channels, tokens), BF16),
            ((hidden_n, tokens), BF16),
            ((hidden_n, tokens), BF16),
        ],
    )
    output = jnp.transpose(out_t, (1, 0, 2))
    edges, small = call(
        depthwise_gradient_kernel,
        [edge, ((small_n, LANES), F32)],
        x, own_x, dconv, vectors,
        scratch=[((deep, rows * extent), BF16), ((deep, rows * extent), BF16), ((16, DEEP), F32)],
    )
    share = swap(share, core, 0)
    far = swap(far_out, space, 1) if direct else None
    low = panel + small_n
    if direct:
        sums = ((low, LANES), BF16)
        *sends, kept = call(
            functools.partial(columns_kernel, filt, panel),
            [((low + high, LANES), BF16), sums, ((low + high, LANES), BF16), ((low, LANES), F32)],
            share, keep, small, edges,
            scratch=[flat],
        )
        third, second, first = (crossed(sends[k - 1], filt, k) for k in (3, 2, 1))
        send, plain = call(
            functools.partial(chips_kernel, filt), [((low + 2 * high, LANES), BF16), sums], third, second, first, kept,
            flops=4 * 10**9,
        )
        third, second, first = (crossed(plain if k == 2 else send, chip, k) for k in (3, 2, 1))
        (mine,) = call(
            functools.partial(total_kernel, axes),
            [((low + 4 * high, LANES), F32)],
            second, third, first, send,
            after=[output, far],
        )
    else:
        far = swap(far_out, space, 1)
        edges = edges_by_permutes(axes, edges).astype(F32)
        total, small = lax.psum((keep + share[-hidden_n:].astype(F32), small), (chip, filt))
        total = lax.dynamic_slice_in_dim(total, lax.axis_index(filt) * panel, panel, 0)
        mine = jnp.concatenate([total, small, edges], axis=0)
    other = swap(mine, core, 0)
    (back,) = call(
        functools.partial(back_kernel, core),
        [((rows * channels, width), F32)],
        dconv, share, far, cot_t, backward,
        scratch=[((tall * deep, width), BF16)],
        after=[mine],
    )
    factor = 1.0 / math.sqrt(tokens * chip_n * core_n * filt_n)
    line = ((1, channels), F32)
    matrix = ((panel, channels), F32)
    image_grad, kg, dwb, gain, lnb, ge, eb, gr, rb, sc = call(
        functools.partial(finish_kernel, factor, core),
        [
            ((channels, rows, width), BF16),
            ((SIDE, SIDE, channels), F32),
            line, line, line, matrix, ((1, panel), F32), matrix, line, line,
        ],
        mine, other, back, taps,
        scratch=[((2 * HALO, 16, LANES), F32), ((edge_height(2 * rows), LANES), F32)],
    )
    flat = lambda v: v.reshape(-1)
    return (
        output, image_grad, jnp.transpose(kg, (2, 0, 1)),
        flat(dwb), flat(gain), flat(lnb), ge, flat(eb), gr, flat(rb), flat(sc),
    )


def solution(mesh):
    space, filt = mesh.devices.shape
    axes = ("chip", "core", "filt")
    pairs = Mesh(mesh.devices.reshape(space // 2, 2, filt), axes)
    pixels = P(None, ("chip", "core"), "filt")
    whole, shard = P(), P("filt")
    return jax.shard_map(
        functools.partial(shards, axes),
        mesh=pairs,
        in_specs=(pixels, pixels) + (whole,) * 9,
        out_specs=(pixels, pixels, whole, whole, whole, whole, shard, shard, shard, whole, whole),
        check_vma=False,
    )
```
